256 devices in a mesh: pipe: 8 (over x_hi, y), dp: 32 (over z, x_lo, core).
Axes of the slice: x: 4 (x_hi: 2, x_lo: 2; x = x_hi * 2 + x_lo), y: 4, z: 8, core: 2. Of those that a mesh axis runs over, the one named last changes fastest.
Arguments:
- section_inputs: bfloat16 [8, 2, 2, 4096, 3584], P('pipe', None, None, 'dp'), may hold values from -6 to 6
- carry_in: bfloat16 [8, 2, 4096, 3584], P('pipe', None, 'dp'), may hold values from -6 to 6
- loss_mask: int32 [2, 2, 4096], P(None, None, 'dp'), may hold values 0 or 1
- weights: float32 [8, 2, 3584, 256], P('pipe', None, 'dp'), may hold values from -6 to 6
- moment1: float32 [8, 2, 3584, 256], P('pipe', None, 'dp'), may hold values from -4 to 4
- moment2: float32 [8, 2, 3584, 256], P('pipe', None, 'dp'), may hold values from 0.1 to 2
Outputs:
- carry_out: bfloat16 [8, 2, 4096, 3584], P('pipe', None, 'dp')
- new_weights: float32 [8, 2, 3584, 256], P('pipe', None, 'dp')
- new_moment1: float32 [8, 2, 3584, 256], P('pipe', None, 'dp')
- new_moment2: float32 [8, 2, 3584, 256], P('pipe', None, 'dp')
The draws below stay inside these ranges and needn't reach their ends.
All inputs are finite; a program needn't handle non-finite values. No bound on the sum of `loss_mask` on one device may be relied on, other than what follows from the above.
Results may differ from the reference program's by a relative error of at most 0.015.
Values may be sent and summed in bfloat16 or wider, within the bound.
No kernel may reach another device: no remote copies, remote signals or barrier semaphores. Data moves between devices by JAX's collectives and lax.ppermute only.
A program may use at most 128 MiB of HBM per device.

```python
import math
import jax
import jax.numpy as jnp
from jax import lax

D = 3584
LATENT = 256
TOK_DEV = 128
STEPS = 2
ADAM_STEP = 10
SECTIONS = 8
TOKENS_MB = 4096
N_DP = 32


def set_ends(drawn, stream_key, low, top_value):
    index_at = [jax.random.randint(jax.random.fold_in(stream_key, axis), (), 0, length) for axis, length in enumerate(drawn.shape)]
    longest = drawn.shape.index(max(drawn.shape))
    next_to = index_at[:longest] + [(index_at[longest] + 1) % drawn.shape[longest]] + index_at[longest + 1:]
    return drawn.at[tuple(index_at)].set(low).at[tuple(next_to)].set(top_value)


def raised(drawn, stream_key, source, target, shards_of, factor):
    owner, partner = [(jnp.arange(drawn.shape[dim]) // (drawn.shape[dim] // shards_of)).reshape([-1 if axis == dim else 1 for axis in range(drawn.ndim)]) for dim in (source, target)]
    chosen = jax.random.permutation(stream_key, shards_of)[partner]
    strong = (owner == chosen) | (owner == (partner + shards_of // 2) % shards_of)
    return jnp.where(strong, factor * drawn, drawn)


def block_levels(key, shape, pieces, smallest, largest):
    def one(axis_at, blocks):
        heights = jax.random.uniform(jax.random.fold_in(jax.random.fold_in(key, 6), axis_at), (blocks,), jnp.float32, smallest / len(pieces), largest / len(pieces))
        return jnp.repeat(jnp.exp(heights), shape[axis_at] // blocks).reshape((-1,) + (1,) * (len(shape) - axis_at - 1))

    level = one(*pieces[0])
    for cut in pieces[1:]:
        level = level * one(*cut)
    return level


def centred(stream_key, shape, spread, reach, shards=(), kind=jnp.bfloat16):
    values = spread * jax.random.normal(stream_key, shape, jnp.float32)
    if shards:
        values = values * block_levels(stream_key, shape, shards, -0.22, 0.18)
    return jnp.clip(values, -reach, reach).astype(kind)


def gaussian_with(key, shape, deviation, reach, cuts, heavy, held_as=jnp.bfloat16):
    values = deviation * jax.random.normal(key, shape, jnp.float32)
    if cuts:
        values = values * block_levels(key, shape, cuts, -0.22, 0.18)
    return jnp.clip(raised(values, jax.random.fold_in(key, 3), *heavy), -reach, reach).astype(held_as)


def setup_inputs(seed: int = 0) -> dict:
    seeds = jax.random.split(jax.random.key(seed), 7)
    return {
        "section_inputs": gaussian_with(seeds[0], (SECTIONS, STEPS, 2, TOKENS_MB, D), 1.0, 6.0, ((0, 8), (3, 32)), (3, 4, 32, 2.75)),
        "carry_in": gaussian_with(seeds[1], (SECTIONS, 2, TOKENS_MB, D), 1.0, 6.0, ((0, 8), (2, 32)), (2, 3, 32, 2.75)),
        "loss_mask": set_ends((jax.random.randint(seeds[2], (STEPS, 2, TOKENS_MB), 0, 4) < 3).astype(jnp.int32), jax.random.fold_in(seeds[2], 1), 0, 1),
        "weights": centred(seeds[3], (SECTIONS, 2, D, LATENT), 1.0, 6.0, ((0, 8), (2, 32)), jnp.float32),
        "moment1": centred(seeds[4], (SECTIONS, 2, D, LATENT), 0.5, 4.0, ((0, 8), (2, 32)), jnp.float32),
        "moment2": jnp.clip(jnp.exp(math.log(2.0) - 2.9957323 * jax.random.uniform(seeds[5], (SECTIONS, 2, D, LATENT), jnp.float32) ** block_levels(seeds[5], (SECTIONS, 2, D, LATENT), ((0, 8), (2, 32)), -0.2, 0.2)), 0.1, 2.0),
    }


NORM_EPS = 1e-06
BETA_ONE = 0.9
BETA_TWO = 0.95
ADAM_EPS = 1e-08
LEARN_RATE = 0.02
DECAY_RATE = 0.1
CLIP_EPS = 1e-06

def normalize(latent):
    factor = lax.rsqrt(lax.optimization_barrier(jnp.mean(latent * latent, axis=-1, keepdims=True)) + NORM_EPS)
    return (factor, (latent * factor).astype(jnp.bfloat16))

def section_pass(inputs, arrived, mask_row, w_down, w_up, at_end):
    latent = jnp.dot(inputs, w_down, preferred_element_type=jnp.float32)
    factor, normed = normalize(latent)
    output = inputs.astype(jnp.float32) + jnp.dot(normed, w_up.T, preferred_element_type=jnp.float32)
    from_loss = (mask_row.astype(jnp.float32)[:, None] * output).astype(jnp.bfloat16)
    cotangent = jnp.where(at_end, from_loss, arrived)
    d_norm = jnp.dot(cotangent, w_up, preferred_element_type=jnp.float32)
    inner = lax.optimization_barrier(jnp.mean(d_norm * latent, axis=-1, keepdims=True))
    d_latent = (factor * (d_norm - latent * (factor * factor * inner))).astype(jnp.bfloat16)
    outgoing = (cotangent.astype(jnp.float32) + jnp.dot(d_latent, w_down.T, preferred_element_type=jnp.float32)).astype(jnp.bfloat16)
    return (outgoing, cotangent, normed, d_latent)

def block_terms(left, right, multiplier):
    left_blocks = left.reshape(STEPS, N_DP, TOK_DEV, left.shape[-1]).astype(jnp.float32)
    right_blocks = right.reshape(STEPS, N_DP, TOK_DEV, right.shape[-1]).astype(jnp.float32)
    partial_sum = jnp.einsum('kjrx,kjrl->jxl', left_blocks, right_blocks) * multiplier
    rounded = lax.optimization_barrier(partial_sum.astype(jnp.bfloat16))
    return lax.optimization_barrier(jnp.sum(rounded.astype(jnp.float32), axis=0))

def select_rows(array, rank, way):
    return lax.dynamic_index_in_dim(array, rank, 0, keepdims=False)[:, way]

def reference(section_inputs, carry_in, loss_mask, weights, moment1, moment2):
    multipliers = jnp.array([D ** (-0.5), LATENT ** (-0.5)], jnp.float32).reshape(1, 2, 1, 1)
    working = (weights * multipliers).astype(jnp.bfloat16)
    mirrored = working[::-1]
    places = jnp.arange(SECTIONS, dtype=jnp.int32)
    a_end = places == SECTIONS - 1
    b_end = places == 0
    arrived = carry_in
    cot_list = []
    normed_list = []
    dlatent_list = []
    outgoing = carry_in
    for step_index in range(STEPS):

        def run(stacked):
            inputs, came, own_copy, partner, end_a, end_b = stacked
            direction_a = section_pass(inputs[0], came[0], loss_mask[step_index, 0], own_copy[0], own_copy[1], end_a)
            direction_b = section_pass(inputs[1], came[1], loss_mask[step_index, 1], partner[0], partner[1], end_b)
            return tuple((jnp.stack([direction_a[number], direction_b[number]]) for number in range(4)))
        outgoing, cotangent, normed, d_latent = lax.map(run, (section_inputs[:, step_index], arrived, working, mirrored, a_end, b_end))
        cot_list.append(cotangent)
        normed_list.append(normed)
        dlatent_list.append(d_latent)
        empty_rows = jnp.zeros_like(outgoing[:1, 0])
        next_a = jnp.concatenate([outgoing[1:, 0], empty_rows], axis=0)
        next_b = jnp.concatenate([empty_rows, outgoing[:-1, 1]], axis=0)
        arrived = jnp.stack([next_a, next_b], axis=1)
    carry_out = outgoing
    all_cots = jnp.stack(cot_list, axis=1)
    all_normed = jnp.stack(normed_list, axis=1)
    all_dlatent = jnp.stack(dlatent_list, axis=1)

    def section_gradient(section_index):
        mirror_rank = SECTIONS - 1 - section_index
        down_part = block_terms(select_rows(section_inputs, section_index, 0), select_rows(all_dlatent, section_index, 0), D ** (-0.5))
        down_part = down_part + block_terms(select_rows(section_inputs, mirror_rank, 1), select_rows(all_dlatent, mirror_rank, 1), D ** (-0.5))
        up_part = block_terms(select_rows(all_cots, section_index, 0), select_rows(all_normed, section_index, 0), LATENT ** (-0.5))
        up_part = up_part + block_terms(select_rows(all_cots, mirror_rank, 1), select_rows(all_normed, mirror_rank, 1), LATENT ** (-0.5))
        return jnp.stack([down_part, up_part])
    gradient = lax.map(section_gradient, jnp.arange(SECTIONS, dtype=jnp.int32))
    square_total = jnp.sum(gradient * gradient)
    clip_limit = math.sqrt(2.0 * SECTIONS * D * LATENT)
    clip_scale = jnp.minimum(1.0, clip_limit / jnp.sqrt(square_total + CLIP_EPS))
    clipped = gradient * clip_scale
    new_moment1 = BETA_ONE * moment1 + (1.0 - BETA_ONE) * clipped
    new_moment2 = BETA_TWO * moment2 + (1.0 - BETA_TWO) * clipped * clipped
    update = new_moment1 / (1.0 - BETA_ONE ** ADAM_STEP) / (jnp.sqrt(new_moment2 / (1.0 - BETA_TWO ** ADAM_STEP)) + ADAM_EPS)
    new_weights = weights - LEARN_RATE * (update + DECAY_RATE * weights)
    return (carry_out, new_weights, new_moment1, new_moment2)
```

```python
import functools
import math

import jax
import jax.numpy as jnp
from jax import lax
from jax.experimental import pallas as pl
from jax.experimental.pallas import tpu as pltpu
from jax.sharding import Mesh
from jax.sharding import PartitionSpec as P

D = 3584
LATENT = 256
STEPS = 2
ADAM_STEP = 10
TOK = 128
ROWS = 112
NZ = 8
NP = 8

NORM_EPS = 1e-06
BETA_ONE = 0.9
BETA_TWO = 0.95
ADAM_EPS = 1e-08
LEARN_RATE = 0.02
DECAY_RATE = 0.1
CLIP_EPS = 1e-06

SCALES = (D ** (-0.5), LATENT ** (-0.5))
PIPE = ("xh", "y")
DP = ("z", "xl", "core")
BF = jnp.bfloat16
F32 = jnp.float32
BLOCK = 896


def shift(value, axis, by, size):
    return lax.ppermute(value, axis, [(i, (i + by) % size) for i in range(size)])


def swap(value, axis):
    return lax.ppermute(value, axis, [(0, 1), (1, 0)])


def mirror(value):
    return lax.ppermute(value, PIPE, [(i, NP - 1 - i) for i in range(NP)])


def mirror_cross(value):
    pairs = [(i * 2 + a, (NP - 1 - i) * 2 + 1 - a) for i in range(NP) for a in range(2)]
    return lax.ppermute(value, ("xh", "y", "xl"), pairs)


def vspec():
    return pl.BlockSpec(memory_space=pltpu.VMEM)


def sspec():
    return pl.BlockSpec(memory_space=pltpu.SMEM)


def call(kernel, out_shape, ins, flops, limit_mb):
    nbytes = sum(math.prod(a.shape) * a.dtype.itemsize for a in list(ins) + list(out_shape))
    return pl.pallas_call(
        kernel,
        out_shape=out_shape,
        in_specs=[sspec()] + [vspec()] * (len(ins) - 1),
        out_specs=[vspec()] * len(out_shape),
        compiler_params=pltpu.CompilerParams(vmem_limit_bytes=limit_mb * 2**20),
        cost_estimate=pl.CostEstimate(flops=flops, bytes_accessed=nbytes, transcendentals=0),
    )(*ins)


def sds(shape, dtype):
    return jax.ShapeDtypeStruct(shape, dtype)


def place(where_ref, chunks, w_ref):
    z = where_ref[0]
    core = where_ref[1]
    for other in range(2):
        c = core if other == 0 else 1 - core
        for k in range(NZ):
            zz = lax.rem(z + k, NZ)
            for xl in range(2):
                row = pl.multiple_of(zz * 448 + xl * 224 + c * ROWS, 16)
                for sec in range(2):
                    ref = chunks[other][k]
                    if isinstance(ref, tuple):
                        val = ref[xl][sec]
                    else:
                        val = ref[xl, sec]
                    w_ref[sec, pl.ds(row, ROWS), :] = val


def dot_t(a, b):
    return lax.dot_general(a, b, (((1,), (1,)), ((), ())), preferred_element_type=F32)


def dot_tn(a, b):
    return lax.dot_general(a, b, (((0,), (0,)), ((), ())), preferred_element_type=F32)


def dot(a, b):
    return jnp.dot(a, b, preferred_element_type=F32)


def split_chunks(refs):
    out = []
    for core in range(2):
        r = refs[core * 9 : core * 9 + 9]
        out.append([r[0], r[1], r[2], r[3], (r[7], r[8]), r[4], r[5], r[6]])
    return out


def latent_kernel(where_ref, x_ref, *refs):
    chunks = split_chunks(refs[:18])
    w_ref, latent_ref, factor_ref, normed_ref = refs[18:]
    place(where_ref, chunks, w_ref)
    for u in range(2):
        rows = x_ref[0, :, u].reshape(STEPS * TOK, D)
        latent = dot(rows, w_ref[u])
        factor = lax.rsqrt(jnp.mean(latent * latent, axis=-1, keepdims=True) + NORM_EPS)
        normed = (latent * factor).astype(BF)
        latent_ref[u] = latent
        factor_ref[u] = jnp.broadcast_to(factor, (STEPS * TOK, 128))
        normed_ref[u] = normed


def backward(latent, factor, d_norm):
    inner = jnp.mean(d_norm * latent, axis=-1, keepdims=True)
    return (factor * (d_norm - latent * (factor * factor * inner))).astype(BF)


def step_cotangent(u, k, is_end, x_ref, w_up_ref, mask_ref, normed_ref, arrived_ref, cot_ref):
    @pl.when(is_end)
    def _():
        normed = normed_ref[u, k * TOK : (k + 1) * TOK]
        for b in range(D // BLOCK):
            cols = slice(b * BLOCK, (b + 1) * BLOCK)
            out = x_ref[0, k, u, :, cols].astype(F32) + dot_t(normed, w_up_ref[u, cols])
            cot_ref[u, :, cols] = (mask_ref[k, u] * out).astype(BF)

    @pl.when(jnp.logical_not(is_end))
    def _():
        cot_ref[u] = arrived_ref[u]


def step0_kernel(where_ref, x_ref, carry_ref, mask_ref, w_down_ref, latent_ref, factor_ref, normed_ref, *refs):
    chunks = split_chunks(refs[:18])
    w_up_ref, cot_ref, d_lat_ref, out_a_ref, out_b_ref = refs[18:]
    place(where_ref, chunks, w_up_ref)
    pipe = where_ref[2]
    for u in range(2):
        is_end = pipe == (NP - 1 if u == 0 else 0)
        step_cotangent(u, 0, is_end, x_ref, w_up_ref, mask_ref, normed_ref, carry_ref.at[0], cot_ref)
        d_norm = dot(cot_ref[u], w_up_ref[u])
        d_lat = backward(latent_ref[u, :TOK], factor_ref[u, :TOK, :1], d_norm)
        d_lat_ref[u] = d_lat
        out_ref = out_a_ref if u == 0 else out_b_ref
        for b in range(D // BLOCK):
            cols = slice(b * BLOCK, (b + 1) * BLOCK)
            out_ref[:, cols] = (cot_ref[u, :, cols].astype(F32) + dot_t(d_lat, w_down_ref[u, cols])).astype(BF)


def step1_kernel(
    where_ref, x_ref, mask_ref, w_down_ref, w_up_ref, latent_ref, factor_ref, normed_ref,
    cot0_ref, d_lat0_ref, arr_a_ref, arr_b_ref,
    carry_out_ref, mine_down_ref, other_down_ref, mine_up_ref, other_up_ref, cot_ref,
):
    z = where_ref[0]
    core = where_ref[1]
    pipe = where_ref[2]
    first = core == 0

    def emit(u, b, grad, mine_ref, other_ref):
        for i in range(2):
            zrel = lax.rem(2 * b + i - z + NZ, NZ)
            for xl in range(2):
                base = (i * 4 + xl * 2) * ROWS
                even = grad[base : base + ROWS]
                odd = grad[base + ROWS : base + 2 * ROWS]
                mine_ref[zrel, xl, u] = jnp.where(first, even, odd)
                other_ref[zrel, xl, u] = jnp.where(first, odd, even)

    for u in range(2):
        is_end = pipe == (NP - 1 if u == 0 else 0)
        arr_ref = arr_a_ref if u == 0 else arr_b_ref

        @pl.when(is_end)
        def _():
            normed = normed_ref[u, TOK:]
            for b in range(D // BLOCK):
                cols = slice(b * BLOCK, (b + 1) * BLOCK)
                out = x_ref[0, 1, u, :, cols].astype(F32) + dot_t(normed, w_up_ref[u, cols])
                cot_ref[u, :, cols] = (mask_ref[1, u] * out).astype(BF)

        @pl.when(jnp.logical_not(is_end))
        def _():
            cot_ref[u] = arr_ref[...]

    for u in range(2):
        for b in range(D // BLOCK):
            cols = slice(b * BLOCK, (b + 1) * BLOCK)
            cots = jnp.concatenate([cot0_ref[u, :, cols], cot_ref[u, :, cols]], axis=0)
            grad = (dot_tn(cots, normed_ref[u]) * SCALES[1]).astype(BF)
            emit(u, b, grad, mine_up_ref, other_up_ref)

    for u in range(2):
        d_norm = dot(cot_ref[u], w_up_ref[u])
        d_lat = backward(latent_ref[u, TOK:], factor_ref[u, TOK:, :1], d_norm)
        d_lats = jnp.concatenate([d_lat0_ref[u], d_lat], axis=0)
        for b in range(D // BLOCK):
            cols = slice(b * BLOCK, (b + 1) * BLOCK)
            xs = x_ref[0, :, u, :, cols].reshape(STEPS * TOK, BLOCK)
            grad = (dot_tn(xs, d_lats) * SCALES[0]).astype(BF)
            emit(u, b, grad, mine_down_ref, other_down_ref)
        for b in range(D // BLOCK):
            cols = slice(b * BLOCK, (b + 1) * BLOCK)
            carry_out_ref[0, u, :, cols] = (
                cot_ref[u, :, cols].astype(F32) + dot_t(d_lat, w_down_ref[u, cols])
            ).astype(BF)


def ring_gather(chunk):
    ahead = back = chunk
    from_behind, from_front = [], []
    for _ in range(3):
        ahead = shift(ahead, "z", 1, NZ)
        back = shift(back, "z", -1, NZ)
        from_behind.append(ahead)
        from_front.append(back)
    half0 = shift(ahead[0], "z", 1, NZ)
    half1 = shift(back[1], "z", -1, NZ)
    return [chunk] + from_front + from_behind[::-1] + [half0, half1]


def add(*parts):
    total = parts[0].astype(F32)
    for part in parts[1:]:
        total = total + part.astype(F32)
    return total


def ring_scatter(mine, theirs):
    ahead = shift(add(mine[4, 0], theirs[4, 0]).astype(BF), "z", 1, NZ)
    back = shift(add(mine[4, 1], theirs[4, 1]).astype(BF), "z", -1, NZ)
    ahead = jnp.stack([add(mine[3, 0], theirs[3, 0], ahead), add(mine[3, 1], theirs[3, 1])]).astype(BF)
    back = jnp.stack([add(mine[5, 0], theirs[5, 0]), add(mine[5, 1], theirs[5, 1], back)]).astype(BF)
    for k in (2, 1):
        ahead = shift(ahead, "z", 1, NZ)
        back = shift(back, "z", -1, NZ)
        ahead = add(mine[k], theirs[k], ahead).astype(BF)
        back = add(mine[NZ - k], theirs[NZ - k], back).astype(BF)
    ahead = shift(ahead, "z", 1, NZ)
    back = shift(back, "z", -1, NZ)
    return add(mine[0], theirs[0], ahead, back)


def local(section_inputs, carry_in, loss_mask, weights, moment1, moment2):
    z = lax.axis_index("z")
    xl = lax.axis_index("xl")
    core = lax.axis_index("core")
    pipe = lax.axis_index(PIPE)
    where = jnp.stack([z, core, pipe, xl]).astype(jnp.int32)
    multipliers = jnp.array(SCALES, F32).reshape(2, 1, 1)
    own = (weights[0] * multipliers).astype(BF)
    mask = jnp.broadcast_to(loss_mask.astype(F32)[..., None], (STEPS, 2, TOK, BLOCK))
    mask = loss_mask.astype(F32)[..., None]

    near = swap(own, "xl")
    mirrored = mirror(own)
    crossed = mirror_cross(own)
    here = jnp.stack([own, mirrored], axis=1)
    there = jnp.stack([near, crossed], axis=1)
    low = jnp.where(xl == 0, here, there)
    high = jnp.where(xl == 0, there, here)
    quad = jnp.stack([low, high], axis=1)

    chunks_down = ring_gather(quad[0])
    chunks_down = chunks_down + [swap(c, "core") for c in chunks_down]
    chunks_up = ring_gather(quad[1])
    chunks_up = chunks_up + [swap(c, "core") for c in chunks_up]

    unit = 2 * TOK * D * LATENT
    w_down, latent, factor, normed = call(
        latent_kernel,
        [sds((2, D, LATENT), BF), sds((2, STEPS * TOK, LATENT), F32), sds((2, STEPS * TOK, 128), F32),
         sds((2, STEPS * TOK, LATENT), BF)],
        [where, section_inputs] + chunks_down,
        4 * unit,
        24,
    )
    w_up, cot0, d_lat0, out_a, out_b = call(
        step0_kernel,
        [sds((2, D, LATENT), BF), sds((2, TOK, D), BF), sds((2, TOK, LATENT), BF), sds((TOK, D), BF), sds((TOK, D), BF)],
        [where, section_inputs, carry_in, mask, w_down, latent, factor, normed] + chunks_up,
        6 * unit,
        36,
    )
    arr_a = lax.ppermute(out_a, PIPE, [(i, i - 1) for i in range(1, NP)])
    arr_b = lax.ppermute(out_b, PIPE, [(i, i + 1) for i in range(NP - 1)])
    half = sds((NZ, 2, 2, ROWS, LATENT), BF)
    carry_out, mine_down, other_down, mine_up, other_up, _ = call(
        step1_kernel,
        [sds((1, 2, TOK, D), BF), half, half, half, half, sds((2, TOK, D), BF)],
        [where, section_inputs, mask, w_down, w_up, latent, factor, normed, cot0, d_lat0, arr_a, arr_b],
        14 * unit,
        44,
    )
    theirs_up = swap(other_up, "core")
    theirs_down = swap(other_down, "core")
    sum_up = ring_scatter(mine_up, theirs_up)
    sum_down = ring_scatter(mine_down, theirs_down)
    total = jnp.stack([sum_down, sum_up])
    keep = jnp.where(xl == 0, total[:, 0], total[:, 1])
    give = jnp.where(xl == 0, total[:, 1], total[:, 0]).astype(BF)
    near = swap(give[:, 0], "xl")
    mirrored = mirror(keep[:, 1].astype(BF))
    crossed = mirror_cross(give[:, 1])
    gradient = (keep[:, 0] + add(near, mirrored, crossed))[None]

    squares = jnp.sum((gradient * gradient).reshape(-1, 8, LATENT), axis=0)
    squares = squares[:, :128] + squares[:, 128:]
    for axis in ("core", "xl"):
        squares = squares + swap(squares, axis)
    for bit in (1, 2, 4):
        squares = squares + lax.ppermute(squares, "z", [(i, i ^ bit) for i in range(NZ)])
    for bit in (1, 2, 4):
        squares = squares + lax.ppermute(squares, PIPE, [(i, i ^ bit) for i in range(NP)])
    square_total = jnp.sum(squares)
    clip_limit = math.sqrt(2.0 * NP * D * LATENT)
    clip_scale = jnp.minimum(1.0, clip_limit / jnp.sqrt(square_total + CLIP_EPS))
    clipped = gradient * clip_scale
    new_moment1 = BETA_ONE * moment1 + (1.0 - BETA_ONE) * clipped
    new_moment2 = BETA_TWO * moment2 + (1.0 - BETA_TWO) * clipped * clipped
    update = (
        new_moment1
        / (1.0 - BETA_ONE**ADAM_STEP)
        / (jnp.sqrt(new_moment2 / (1.0 - BETA_TWO**ADAM_STEP)) + ADAM_EPS)
    )
    new_weights = weights - LEARN_RATE * (update + DECAY_RATE * weights)
    return (carry_out, new_weights, new_moment1, new_moment2)


def solution(mesh):
    fine = Mesh(mesh.devices.reshape(2, 4, 8, 2, 2), PIPE + DP)
    rows = P(PIPE, None, DP, None)
    return jax.shard_map(
        local,
        mesh=fine,
        in_specs=(P(PIPE, None, None, DP, None), rows, P(None, None, DP), rows, rows, rows),
        out_specs=(rows, rows, rows, rows),
        check_vma=False,
    )
```

```python
import math

import jax
import jax.numpy as jnp
from jax import lax
from jax.experimental import pallas as pl
from jax.experimental.pallas import tpu as pltpu
from jax.sharding import Mesh
from jax.sharding import PartitionSpec as P

D = 3584
LATENT = 256
STEPS = 2
ADAM_STEP = 10
TOK = 128
ROWS = 112
NZ = 8
NP = 8

NORM_EPS = 1e-06
BETA_ONE = 0.9
BETA_TWO = 0.95
ADAM_EPS = 1e-08
LEARN_RATE = 0.02
DECAY_RATE = 0.1
CLIP_EPS = 1e-06

SCALES = (D ** (-0.5), LATENT ** (-0.5))
PIPE = ("xh", "y")
DP = ("z", "xl", "core")
BF = jnp.bfloat16
F32 = jnp.float32
BLOCK = 896
KERNEL_MB = 12


def shift(value, axis, by, size):
    return lax.ppermute(value, axis, [(i, (i + by) % size) for i in range(size)])


def swap(value, axis):
    return lax.ppermute(value, axis, [(0, 1), (1, 0)])


def mirror(value):
    return lax.ppermute(value, PIPE, [(i, NP - 1 - i) for i in range(NP)])


def mirror_cross(value):
    pairs = [(i * 2 + a, (NP - 1 - i) * 2 + 1 - a) for i in range(NP) for a in range(2)]
    return lax.ppermute(value, ("xh", "y", "xl"), pairs)


def vspec():
    return pl.BlockSpec(memory_space=pltpu.VMEM)


def sspec():
    return pl.BlockSpec(memory_space=pltpu.SMEM)


def call(kernel, out_shape, ins, flops, limit_mb, scratch=()):
    nbytes = sum(math.prod(a.shape) * a.dtype.itemsize for a in list(ins) + list(out_shape))
    return pl.pallas_call(
        kernel,
        out_shape=out_shape,
        in_specs=[sspec()] + [vspec()] * (len(ins) - 1),
        out_specs=[vspec()] * len(out_shape),
        scratch_shapes=list(scratch),
        compiler_params=pltpu.CompilerParams(vmem_limit_bytes=limit_mb * 2**20),
        cost_estimate=pl.CostEstimate(flops=flops, bytes_accessed=nbytes, transcendentals=0),
    )(*ins)


def sds(shape, dtype):
    return jax.ShapeDtypeStruct(shape, dtype)


def place(where_ref, chunks, kind, w_ref):
    z = where_ref[0]
    core = where_ref[1]
    for other in range(2):
        c = core if other == 0 else 1 - core
        for k in range(NZ):
            zz = lax.rem(z + k, NZ)
            ref = chunks[other][k]
            for xl in range(2):
                row = pl.multiple_of(zz * 448 + xl * 224 + c * ROWS, 16)
                for sec in range(2):
                    val = ref[kind][xl, sec] if isinstance(ref, tuple) else ref[kind, xl, sec]
                    w_ref[sec, pl.ds(row, ROWS), :] = val


def dot_t(a, b):
    return lax.dot_general(a, b, (((1,), (1,)), ((), ())), preferred_element_type=F32)


def dot_tn(a, b):
    return lax.dot_general(a, b, (((0,), (0,)), ((), ())), preferred_element_type=F32)


def dot(a, b):
    return jnp.dot(a, b, preferred_element_type=F32)


def split_chunks(refs):
    out = []
    for core in range(2):
        r = refs[core * 9 : core * 9 + 9]
        out.append([r[0], r[1], r[2], r[3], (r[7], r[8]), r[4], r[5], r[6]])
    return out


def backward(latent, factor, d_norm):
    inner = jnp.mean(d_norm * latent, axis=-1, keepdims=True)
    return (factor * (d_norm - latent * (factor * factor * inner))).astype(BF)


def step_cotangent(u, k, is_end, x_ref, w_up_ref, mask_ref, normed_ref, arrived_ref, cot_ref):
    @pl.when(is_end)
    def _():
        normed = normed_ref[u, k * TOK : (k + 1) * TOK]
        for b in range(D // BLOCK):
            cols = slice(b * BLOCK, (b + 1) * BLOCK)
            out = x_ref[0, k, u, :, cols].astype(F32) + dot_t(normed, w_up_ref[u, cols])
            cot_ref[u, :, cols] = (mask_ref[k, u] * out).astype(BF)

    @pl.when(jnp.logical_not(is_end))
    def _():
        cot_ref[u] = arrived_ref[u]


def step0_kernel(where_ref, x_ref, carry_ref, mask_ref, *refs):
    chunks = split_chunks(refs[:18])
    w_down_ref, w_up_ref, latent_ref, factor_ref, normed_ref, cot_ref, d_lat_ref, out_a_ref, out_b_ref = refs[18:]
    place(where_ref, chunks, 0, w_down_ref)
    for u in range(2):
        rows = x_ref[0, :, u].reshape(STEPS * TOK, D)
        latent = dot(rows, w_down_ref[u])
        factor = lax.rsqrt(jnp.mean(latent * latent, axis=-1, keepdims=True) + NORM_EPS)
        latent_ref[u] = latent
        factor_ref[u] = jnp.broadcast_to(factor, (STEPS * TOK, 128))
        normed_ref[u] = (latent * factor).astype(BF)
    place(where_ref, chunks, 1, w_up_ref)
    pipe = where_ref[2]
    for u in range(2):
        is_end = pipe == (NP - 1 if u == 0 else 0)
        step_cotangent(u, 0, is_end, x_ref, w_up_ref, mask_ref, normed_ref, carry_ref.at[0], cot_ref)
        d_norm = dot(cot_ref[u], w_up_ref[u])
        d_lat = backward(latent_ref[u, :TOK], factor_ref[u, :TOK, :1], d_norm)
        d_lat_ref[u] = d_lat
        out_ref = out_a_ref if u == 0 else out_b_ref
        for b in range(D // BLOCK):
            cols = slice(b * BLOCK, (b + 1) * BLOCK)
            out_ref[:, cols] = (cot_ref[u, :, cols].astype(F32) + dot_t(d_lat, w_down_ref[u, cols])).astype(BF)


def step1_kernel(
    where_ref, x_ref, mask_ref, w_down_ref, w_up_ref, latent_ref, factor_ref, normed_ref,
    cot0_ref, d_lat0_ref, arr_a_ref, arr_b_ref,
    carry_out_ref, mine_down_ref, other_down_ref, mine_up_ref, other_up_ref, cot_ref,
):
    z = where_ref[0]
    core = where_ref[1]
    pipe = where_ref[2]
    first = core == 0

    def emit(u, b, grad, mine_ref, other_ref):
        for i in range(2):
            zrel = lax.rem(2 * b + i - z + NZ, NZ)
            for xl in range(2):
                base = (i * 4 + xl * 2) * ROWS
                even = grad[base : base + ROWS]
                odd = grad[base + ROWS : base + 2 * ROWS]
                mine_ref[zrel, xl, u] = jnp.where(first, even, odd)
                other_ref[zrel, xl, u] = jnp.where(first, odd, even)

    for u in range(2):
        is_end = pipe == (NP - 1 if u == 0 else 0)
        arr_ref = arr_a_ref if u == 0 else arr_b_ref

        @pl.when(is_end)
        def _():
            normed = normed_ref[u, TOK:]
            for b in range(D // BLOCK):
                cols = slice(b * BLOCK, (b + 1) * BLOCK)
                out = x_ref[0, 1, u, :, cols].astype(F32) + dot_t(normed, w_up_ref[u, cols])
                cot_ref[u, :, cols] = (mask_ref[1, u] * out).astype(BF)

        @pl.when(jnp.logical_not(is_end))
        def _():
            cot_ref[u] = arr_ref[...]

    for u in range(2):
        for b in range(D // BLOCK):
            cols = slice(b * BLOCK, (b + 1) * BLOCK)
            cots = jnp.concatenate([cot0_ref[u, :, cols], cot_ref[u, :, cols]], axis=0)
            grad = (dot_tn(cots, normed_ref[u]) * SCALES[1]).astype(BF)
            emit(u, b, grad, mine_up_ref, other_up_ref)

    for u in range(2):
        d_norm = dot(cot_ref[u], w_up_ref[u])
        d_lat = backward(latent_ref[u, TOK:], factor_ref[u, TOK:, :1], d_norm)
        d_lats = jnp.concatenate([d_lat0_ref[u], d_lat], axis=0)
        for b in range(D // BLOCK):
            cols = slice(b * BLOCK, (b + 1) * BLOCK)
            xs = x_ref[0, :, u, :, cols].reshape(STEPS * TOK, BLOCK)
            grad = (dot_tn(xs, d_lats) * SCALES[0]).astype(BF)
            emit(u, b, grad, mine_down_ref, other_down_ref)
        for b in range(D // BLOCK):
            cols = slice(b * BLOCK, (b + 1) * BLOCK)
            carry_out_ref[0, u, :, cols] = (
                cot_ref[u, :, cols].astype(F32) + dot_t(d_lat, w_down_ref[u, cols])
            ).astype(BF)


def ring_gather(chunk):
    ahead = back = chunk
    from_behind, from_front = [], []
    for _ in range(3):
        ahead = shift(ahead, "z", 1, NZ)
        back = shift(back, "z", -1, NZ)
        from_behind.append(ahead)
        from_front.append(back)
    half0 = shift(ahead[0], "z", 1, NZ)
    half1 = shift(back[1], "z", -1, NZ)
    return [chunk] + from_front + from_behind[::-1] + [half0, half1]


def add(*parts):
    total = parts[0].astype(F32)
    for part in parts[1:]:
        total = total + part.astype(F32)
    return total


def ring_scatter(mine, theirs):
    ahead = shift(add(mine[4, 0], theirs[4, 0]).astype(BF), "z", 1, NZ)
    back = shift(add(mine[4, 1], theirs[4, 1]).astype(BF), "z", -1, NZ)
    ahead = jnp.stack([add(mine[3, 0], theirs[3, 0], ahead), add(mine[3, 1], theirs[3, 1])]).astype(BF)
    back = jnp.stack([add(mine[5, 0], theirs[5, 0]), add(mine[5, 1], theirs[5, 1], back)]).astype(BF)
    for k in (2, 1):
        ahead = shift(ahead, "z", 1, NZ)
        back = shift(back, "z", -1, NZ)
        ahead = add(mine[k], theirs[k], ahead).astype(BF)
        back = add(mine[NZ - k], theirs[NZ - k], back).astype(BF)
    ahead = shift(ahead, "z", 1, NZ)
    back = shift(back, "z", -1, NZ)
    return add(mine[0], theirs[0], ahead, back)


def local(section_inputs, carry_in, loss_mask, weights, moment1, moment2):
    z = lax.axis_index("z")
    xl = lax.axis_index("xl")
    core = lax.axis_index("core")
    pipe = lax.axis_index(PIPE)
    where = jnp.stack([z, core, pipe, xl]).astype(jnp.int32)
    multipliers = jnp.array(SCALES, F32).reshape(2, 1, 1)
    own = (weights[0] * multipliers).astype(BF)
    mask = loss_mask.astype(F32)[..., None]

    near = swap(own, "xl")
    mirrored = mirror(own)
    crossed = mirror_cross(own)
    here = jnp.stack([own, mirrored], axis=1)
    there = jnp.stack([near, crossed], axis=1)
    low = jnp.where(xl == 0, here, there)
    high = jnp.where(xl == 0, there, here)
    quad = jnp.stack([low, high], axis=1)

    chunks = ring_gather(quad)
    chunks = chunks + [swap(c, "core") for c in chunks]

    unit = 2 * TOK * D * LATENT
    weight = sds((2, D, LATENT), BF)
    w_down, w_up, latent, factor, normed, cot0, d_lat0, out_a, out_b = call(
        step0_kernel,
        [weight, weight, sds((2, STEPS * TOK, LATENT), F32), sds((2, STEPS * TOK, 128), F32),
         sds((2, STEPS * TOK, LATENT), BF), sds((2, TOK, D), BF), sds((2, TOK, LATENT), BF),
         sds((TOK, D), BF), sds((TOK, D), BF)],
        [where, section_inputs, carry_in, mask] + chunks,
        10 * unit,
        KERNEL_MB,
    )
    arr_a = lax.ppermute(out_a, PIPE, [(i, i - 1) for i in range(1, NP)])
    arr_b = lax.ppermute(out_b, PIPE, [(i, i + 1) for i in range(NP - 1)])
    half = sds((NZ, 2, 2, ROWS, LATENT), BF)
    carry_out, mine_down, other_down, mine_up, other_up = call(
        step1_kernel,
        [sds((1, 2, TOK, D), BF), half, half, half, half],
        [where, section_inputs, mask, w_down, w_up, latent, factor, normed, cot0, d_lat0, arr_a, arr_b],
        14 * unit,
        KERNEL_MB,
        [pltpu.VMEM((2, TOK, D), BF)],
    )
    theirs_up = swap(other_up, "core")
    theirs_down = swap(other_down, "core")
    sum_up = ring_scatter(mine_up, theirs_up)
    sum_down = ring_scatter(mine_down, theirs_down)
    total = jnp.stack([sum_down, sum_up])
    keep = jnp.where(xl == 0, total[:, 0], total[:, 1])
    give = jnp.where(xl == 0, total[:, 1], total[:, 0]).astype(BF)
    near = swap(give[:, 0], "xl")
    mirrored = mirror(keep[:, 1].astype(BF))
    crossed = mirror_cross(give[:, 1])
    gradient = (keep[:, 0] + add(near, mirrored, crossed))[None]

    squares = jnp.sum((gradient * gradient).reshape(-1, 8, LATENT), axis=0)
    squares = squares[:, :128] + squares[:, 128:]
    for axes, size, bits in (
        (("xl", "core"), 4, (1, 2)), ("z", NZ, (1, 2)), (("y",), 4, (1, 2)), (("xh", "z"), 16, (4, 8)),
    ):
        parts = [squares]
        for flip in (bits[0], bits[1], bits[0] + bits[1]):
            parts.append(lax.ppermute(squares, axes, [(i, i ^ flip) for i in range(size)]))
        squares = (parts[0] + parts[1]) + (parts[2] + parts[3])
    square_total = jnp.sum(squares)
    clip_limit = math.sqrt(2.0 * NP * D * LATENT)
    clip_scale = jnp.minimum(1.0, clip_limit / jnp.sqrt(square_total + CLIP_EPS))
    clipped = gradient * clip_scale
    new_moment1 = BETA_ONE * moment1 + (1.0 - BETA_ONE) * clipped
    new_moment2 = BETA_TWO * moment2 + (1.0 - BETA_TWO) * clipped * clipped
    update = (
        new_moment1
        / (1.0 - BETA_ONE**ADAM_STEP)
        / (jnp.sqrt(new_moment2 / (1.0 - BETA_TWO**ADAM_STEP)) + ADAM_EPS)
    )
    new_weights = weights - LEARN_RATE * (update + DECAY_RATE * weights)
    return (carry_out, new_weights, new_moment1, new_moment2)


def solution(mesh):
    fine = Mesh(mesh.devices.reshape(2, 4, 8, 2, 2), PIPE + DP)
    rows = P(PIPE, None, DP, None)
    return jax.shard_map(
        local,
        mesh=fine,
        in_specs=(P(PIPE, None, None, DP, None), rows, P(None, None, DP), rows, rows, rows),
        out_specs=(rows, rows, rows, rows),
        check_vma=False,
    )
```

```python
import math

import jax
import jax.numpy as jnp
from jax import lax
from jax.experimental import pallas as pl
from jax.experimental.pallas import tpu as pltpu
from jax.sharding import Mesh
from jax.sharding import PartitionSpec as P

D = 3584
LATENT = 256
STEPS = 2
ADAM_STEP = 10
TOK = 128
ROWS = 112
NZ = 8
NP = 8
BLOCK = 896
KERNEL_MB = 12
EARLY = (0, 1, 7, 2, 6)

NORM_EPS = 1e-06
BETA_ONE = 0.9
BETA_TWO = 0.95
ADAM_EPS = 1e-08
LEARN_RATE = 0.02
DECAY_RATE = 0.1
CLIP_EPS = 1e-06

SCALES = (D ** (-0.5), LATENT ** (-0.5))
PIPE = ("xh", "y")
DP = ("z", "xl", "core")
BF = jnp.bfloat16
F32 = jnp.float32


def shift(value, axis, by, size):
    return lax.ppermute(value, axis, [(i, (i + by) % size) for i in range(size)])


def swap(value, axis):
    return lax.ppermute(value, axis, [(0, 1), (1, 0)])


def mirror(value):
    return lax.ppermute(value, PIPE, [(i, NP - 1 - i) for i in range(NP)])


def mirror_cross(value):
    pairs = [(i * 2 + a, (NP - 1 - i) * 2 + 1 - a) for i in range(NP) for a in range(2)]
    return lax.ppermute(value, ("xh", "y", "xl"), pairs)


def sds(shape, dtype):
    return jax.ShapeDtypeStruct(shape, dtype)


def call(kernel, out_shape, ins, flops, hbm=(), scratch=()):
    operands = list(ins) + list(hbm)
    nbytes = sum(math.prod(a.shape) * a.dtype.itemsize for a in operands + list(out_shape))
    vmem = pl.BlockSpec(memory_space=pltpu.VMEM)
    return pl.pallas_call(
        kernel,
        out_shape=out_shape,
        in_specs=[pl.BlockSpec(memory_space=pltpu.SMEM)]
        + [vmem] * (len(ins) - 1)
        + [pl.BlockSpec(memory_space=pl.ANY)] * len(hbm),
        out_specs=[vmem] * len(out_shape),
        scratch_shapes=list(scratch),
        compiler_params=pltpu.CompilerParams(vmem_limit_bytes=KERNEL_MB * 2**20),
        cost_estimate=pl.CostEstimate(flops=flops, bytes_accessed=nbytes, transcendentals=0),
    )(*operands)


def dot(a, b):
    return jnp.dot(a, b, preferred_element_type=F32)


def dot_t(a, b):
    return lax.dot_general(a, b, (((1,), (1,)), ((), ())), preferred_element_type=F32)


def dot_tn(a, b):
    return lax.dot_general(a, b, (((0,), (0,)), ((), ())), preferred_element_type=F32)


def backward(latent, factor, d_norm):
    inner = jnp.mean(d_norm * latent, axis=-1, keepdims=True)
    return (factor * (d_norm - latent * (factor * factor * inner))).astype(BF)


def is_end(where_ref, u):
    return where_ref[2] == (NP - 1 if u == 0 else 0)


def quad_kernel(where_ref, own_ref, mirrored_ref, near_ref, crossed_ref, out_ref):
    xl = where_ref[3]
    out_ref[xl, 0] = own_ref[...]
    out_ref[xl, 1] = mirrored_ref[...]
    out_ref[1 - xl, 0] = near_ref[...]
    out_ref[1 - xl, 1] = crossed_ref[...]


def pack_kernel(where_ref, *refs):
    out_ref = refs[-1]
    for i, ref in enumerate(refs[:-1]):
        out_ref[i] = ref[...]


def step0_kernel(u, where_ref, mask_ref, *refs):
    (x_hbm, carry_hbm, w_ref, latent_ref, factor_ref, normed_ref, cot_ref, d_lat_ref, out_ref,
     x_ref, x_sem, carry_sem) = refs[-12:]
    z = where_ref[0]
    core = where_ref[1]
    x_copy = pltpu.make_async_copy(x_hbm.at[0, :, u], x_ref, x_sem)
    x_copy.start()
    carry_copy = pltpu.make_async_copy(carry_hbm.at[0, u], cot_ref, carry_sem)
    carry_copy.start()

    for part, c in enumerate((core, 1 - core)):
        early_ref, front_ref, behind_ref, low_ref, high_ref = refs[part * 5 : part * 5 + 5]
        for k in range(NZ):
            zz = lax.rem(z + k, NZ)
            for xl in range(2):
                row = pl.multiple_of(zz * 448 + xl * 224 + c * ROWS, 16)
                for kind in range(2):
                    if k in EARLY:
                        block = early_ref[EARLY.index(k), xl, u, kind]
                    elif k == 4:
                        block = (low_ref, high_ref)[xl][u, kind]
                    else:
                        block = (front_ref if k == 3 else behind_ref)[xl, u, kind]
                    w_ref[kind, pl.ds(row, ROWS), :] = block
    x_copy.wait()
    latent = dot(x_ref[...].reshape(STEPS * TOK, D), w_ref[0])
    factor = lax.rsqrt(jnp.mean(latent * latent, axis=-1, keepdims=True) + NORM_EPS)
    latent_ref[...] = latent
    factor_ref[...] = jnp.broadcast_to(factor, (STEPS * TOK, 128))
    normed_ref[...] = (latent * factor).astype(BF)
    carry_copy.wait()

    @pl.when(is_end(where_ref, u))
    def _():
        for b in range(D // BLOCK):
            cols = slice(b * BLOCK, (b + 1) * BLOCK)
            out = x_ref[0, :, cols].astype(F32) + dot_t(normed_ref[:TOK], w_ref[1, cols])
            cot_ref[:, cols] = (mask_ref[0, u] * out).astype(BF)

    d_norm = dot(cot_ref[...], w_ref[1])
    d_lat_ref[...] = backward(latent_ref[:TOK], factor_ref[:TOK, :1], d_norm)
    for b in range(D // BLOCK):
        cols = slice(b * BLOCK, (b + 1) * BLOCK)
        out = cot_ref[:, cols].astype(F32) + dot_t(d_lat_ref[...], w_ref[0, cols])
        out_ref[:, cols] = out.astype(BF)


def step1_kernel(u, where_ref, mask_ref, w_ref, latent_ref, factor_ref, normed_ref, cot0_ref, d_lat0_ref, arr_ref,
                 *refs):
    x_hbm, cot_ref, d_lat_ref, mine_ref, other_ref, x_ref, x_sem = refs[-7:]
    z = where_ref[0]
    core = where_ref[1]
    x_copy = pltpu.make_async_copy(x_hbm.at[0, :, u], x_ref, x_sem)
    x_copy.start()

    def emit(grad, b, kind):
        for i in range(2):
            k = lax.rem(2 * b + i - z + NZ, NZ)
            for xl in range(2):
                base = (i * 4 + xl * 2) * ROWS
                low = grad[base : base + ROWS]
                high = grad[base + ROWS : base + 2 * ROWS]
                mine_ref[k, xl, kind] = jnp.where(core == 0, low, high)
                other_ref[k, xl, kind] = jnp.where(core == 0, high, low)

    end = is_end(where_ref, u)

    @pl.when(end)
    def _():
        x_copy.wait()
        for b in range(D // BLOCK):
            cols = slice(b * BLOCK, (b + 1) * BLOCK)
            out = x_ref[1, :, cols].astype(F32) + dot_t(normed_ref[TOK:], w_ref[1, cols])
            cot_ref[:, cols] = (mask_ref[1, u] * out).astype(BF)

    @pl.when(jnp.logical_not(end))
    def _():
        cot_ref[...] = arr_ref[...]
        x_copy.wait()

    d_norm = dot(cot_ref[...], w_ref[1])
    d_lat = backward(latent_ref[TOK:], factor_ref[TOK:, :1], d_norm)
    d_lat_ref[...] = d_lat
    d_lats = jnp.concatenate([d_lat0_ref[...], d_lat], axis=0)
    for b in range(D // BLOCK):
        cols = slice(b * BLOCK, (b + 1) * BLOCK)
        cots = jnp.concatenate([cot0_ref[:, cols], cot_ref[:, cols]], axis=0)
        emit((dot_tn(cots, normed_ref[...]) * SCALES[1]).astype(BF), b, 1)
        xs = x_ref[:, :, cols].reshape(STEPS * TOK, BLOCK)
        emit((dot_tn(xs, d_lats) * SCALES[0]).astype(BF), b, 0)


def carry_kernel(where_ref, *refs):
    out_ref = refs[-1]
    for u in range(2):
        w_ref, d_lat_ref, cot_ref = refs[u * 3 : u * 3 + 3]
        for b in range(D // BLOCK):
            cols = slice(b * BLOCK, (b + 1) * BLOCK)
            out = cot_ref[:, cols].astype(F32) + dot_t(d_lat_ref[...], w_ref[0, cols])
            out_ref[0, u, :, cols] = out.astype(BF)


def far_kernel(where_ref, mine_ref, theirs_ref, low_ref, high_ref):
    for xl, ref in enumerate((low_ref, high_ref)):
        ref[...] = (mine_ref[4, xl].astype(F32) + theirs_ref[4, xl].astype(F32)).astype(BF)


def join_kernel(k, half, where_ref, mine_ref, theirs_ref, arrived_ref, out_ref):
    for xl in range(2):
        total = mine_ref[k, xl].astype(F32) + theirs_ref[k, xl].astype(F32)
        if half is None:
            total = total + arrived_ref[xl].astype(F32)
        elif half == xl:
            total = total + arrived_ref[...].astype(F32)
        out_ref[xl] = total.astype(BF)


def last_kernel(where_ref, mine_ref, theirs_ref, ahead_ref, back_ref, *refs):
    keep_ref, give_ref = refs[-2:]
    xl = where_ref[3]

    def total(i):
        parts = (mine_ref[0, i], theirs_ref[0, i], ahead_ref[i], back_ref[i])
        return sum(part.astype(F32) for part in parts)

    keep_ref[...] = total(xl).astype(keep_ref.dtype)
    give_ref[...] = total(1 - xl).astype(BF)


def token(*arrays):
    return sum(a.reshape(-1, a.shape[-1])[:8, :128].astype(F32) for a in arrays)


def local(section_inputs, carry_in, loss_mask, weights, moment1, moment2):
    where = jnp.stack(
        [lax.axis_index("z"), lax.axis_index("core"), lax.axis_index(PIPE), lax.axis_index("xl")]
    ).astype(jnp.int32)
    multipliers = jnp.array(SCALES, F32).reshape(2, 1, 1)
    own = (weights[0] * multipliers).astype(BF)
    mask = loss_mask.astype(F32)[..., None]
    shard = (2, ROWS, LATENT)
    chunk = sds((2, *shard), BF)
    unit = 2 * TOK * D * LATENT
    small = 1 << 20

    def gather(start):
        ahead, back = [start], [start]
        for _ in range(3):
            ahead.append(shift(ahead[-1], "z", 1, NZ))
            back.append(shift(back[-1], "z", -1, NZ))
        low = shift(ahead[3][0], "z", 1, NZ)
        high = shift(back[3][1], "z", -1, NZ)
        chunks = [start, back[1], ahead[1], back[2], ahead[2]]
        early = call(pack_kernel, [sds((5, *start.shape), BF)], [where, *chunks], small)[0]
        chunks = [early, back[3], ahead[3], low, high]
        return chunks + [swap(c, "core") for c in chunks]

    def step0(u, packs, *after):
        return call(
            lambda *refs: step0_kernel(u, *refs),
            [sds((2, D, LATENT), BF), sds((STEPS * TOK, LATENT), F32), sds((STEPS * TOK, 128), F32),
             sds((STEPS * TOK, LATENT), BF), sds((TOK, D), BF), sds((TOK, LATENT), BF), sds((TOK, D), BF)],
            [where, mask, *packs, *after],
            5 * unit,
            [section_inputs, carry_in],
            [pltpu.VMEM((STEPS, TOK, D), BF), pltpu.SemaphoreType.DMA, pltpu.SemaphoreType.DMA],
        )

    def hop(u, out):
        if u == 0:
            return lax.ppermute(out, PIPE, [(i, i - 1) for i in range(1, NP)])
        return lax.ppermute(out, PIPE, [(i, i + 1) for i in range(NP - 1)])

    def step1(u, state, arrived, *after):
        w, latent, factor, normed, cot0, d_lat0, _ = state
        terms = sds((NZ, *chunk.shape), BF)
        cot1, d_lat1, mine, other = call(
            lambda *refs: step1_kernel(u, *refs),
            [sds((TOK, D), BF), sds((TOK, LATENT), BF), terms, terms],
            [where, mask, w, latent, factor, normed, cot0, d_lat0, arrived, *after],
            6 * unit,
            [section_inputs],
            [pltpu.VMEM((STEPS, TOK, D), BF), pltpu.SemaphoreType.DMA],
        )
        return (w, d_lat1, cot1), mine, swap(other, "core")

    def scatter(mine, theirs, keep_type, *after):
        both = [where, mine, theirs]

        def join(k, half, arrived):
            return call(lambda *refs: join_kernel(k, half, *refs), [chunk], [*both, arrived], small)[0]

        low, high = call(far_kernel, [sds(shard, BF), sds(shard, BF)], both, small)
        ahead = join(3, 0, shift(low, "z", 1, NZ))
        back = join(5, 1, shift(high, "z", -1, NZ))
        ahead = join(2, None, shift(ahead, "z", 1, NZ))
        back = join(6, None, shift(back, "z", -1, NZ))
        ahead = join(1, None, shift(ahead, "z", 1, NZ))
        back = join(7, None, shift(back, "z", -1, NZ))
        ahead = shift(ahead, "z", 1, NZ)
        back = shift(back, "z", -1, NZ)
        parts = [*both, ahead, back, *after]
        keep, give = call(last_kernel, [sds(shard, keep_type), sds(shard, BF)], parts, small)
        return keep, give

    shards = [where, own, mirror(own), swap(own, "xl"), mirror_cross(own)]
    chunks = gather(call(quad_kernel, [sds((2, 2, *shard), BF)], shards, small)[0])
    state_a = step0(0, chunks)
    arrived_a = hop(0, state_a[-1])
    state_b = step0(1, chunks, token(state_a[5]))
    arrived_b = hop(1, state_b[-1])
    end_a, mine_a, theirs_a = step1(0, state_a, arrived_a)
    keep_a, give_a = scatter(mine_a, theirs_a, F32)
    end_b, mine_b, theirs_b = step1(1, state_b, arrived_b, token(end_a[1]))
    (carry_out,) = call(carry_kernel, [sds((1, 2, TOK, D), BF)], [where, *end_a, *end_b], 2 * unit)
    keep_b, give_b = scatter(mine_b, theirs_b, BF, token(carry_out))
    near = swap(give_a, "xl").astype(F32)
    mirrored = mirror(keep_b).astype(F32)
    crossed = mirror_cross(give_b).astype(F32)
    gradient = (keep_a + near + mirrored + crossed)[None]

    squares = jnp.sum((gradient * gradient).reshape(-1, 128), axis=0)
    squares = jnp.broadcast_to(squares, (NP * NZ * 4, 1, 128))
    square_total = jnp.sum(lax.all_to_all(squares, PIPE + DP, 0, 0, tiled=True))
    clip_limit = math.sqrt(2.0 * NP * D * LATENT)
    clip_scale = jnp.minimum(1.0, clip_limit / jnp.sqrt(square_total + CLIP_EPS))
    clipped = gradient * clip_scale
    new_moment1 = BETA_ONE * moment1 + (1.0 - BETA_ONE) * clipped
    new_moment2 = BETA_TWO * moment2 + (1.0 - BETA_TWO) * clipped * clipped
    update = (
        new_moment1
        / (1.0 - BETA_ONE**ADAM_STEP)
        / (jnp.sqrt(new_moment2 / (1.0 - BETA_TWO**ADAM_STEP)) + ADAM_EPS)
    )
    new_weights = weights - LEARN_RATE * (update + DECAY_RATE * weights)
    return (carry_out, new_weights, new_moment1, new_moment2)


def solution(mesh):
    fine = Mesh(mesh.devices.reshape(2, 4, 8, 2, 2), PIPE + DP)
    rows = P(PIPE, None, DP, None)
    return jax.shard_map(
        local,
        mesh=fine,
        in_specs=(P(PIPE, None, None, DP, None), rows, P(None, None, DP), rows, rows, rows),
        out_specs=(rows, rows, rows, rows),
        check_vma=False,
    )
```

```python
import math

import jax
import jax.numpy as jnp
from jax import lax
from jax.experimental import pallas as pl
from jax.experimental.pallas import tpu as pltpu
from jax.sharding import Mesh
from jax.sharding import PartitionSpec as P

D = 3584
LATENT = 256
STEPS = 2
ADAM_STEP = 10
TOK = 128
ROWS = 112
NZ = 8
NP = 8
BLOCK = 896
KERNEL_MB = 12

NORM_EPS = 1e-06
BETA_ONE = 0.9
BETA_TWO = 0.95
ADAM_EPS = 1e-08
LEARN_RATE = 0.02
DECAY_RATE = 0.1
CLIP_EPS = 1e-06

SCALES = (D ** (-0.5), LATENT ** (-0.5))
PIPE = ("xh", "y")
DP = ("z", "xl", "core")
BF = jnp.bfloat16
F32 = jnp.float32


def shift(value, axis, by, size):
    return lax.ppermute(value, axis, [(i, (i + by) % size) for i in range(size)])


def swap(value, axis):
    return lax.ppermute(value, axis, [(0, 1), (1, 0)])


def mirror(value):
    return lax.ppermute(value, PIPE, [(i, NP - 1 - i) for i in range(NP)])


def mirror_cross(value):
    pairs = [(i * 2 + a, (NP - 1 - i) * 2 + 1 - a) for i in range(NP) for a in range(2)]
    return lax.ppermute(value, ("xh", "y", "xl"), pairs)


def sds(shape, dtype):
    return jax.ShapeDtypeStruct(shape, dtype)


def call(kernel, out_shape, ins, flops):
    nbytes = sum(math.prod(a.shape) * a.dtype.itemsize for a in list(ins) + list(out_shape))
    vmem = pl.BlockSpec(memory_space=pltpu.VMEM)
    return pl.pallas_call(
        kernel,
        out_shape=out_shape,
        in_specs=[pl.BlockSpec(memory_space=pltpu.SMEM)] + [vmem] * (len(ins) - 1),
        out_specs=[vmem] * len(out_shape),
        compiler_params=pltpu.CompilerParams(vmem_limit_bytes=KERNEL_MB * 2**20),
        cost_estimate=pl.CostEstimate(flops=flops, bytes_accessed=nbytes, transcendentals=0),
    )(*ins)


def dot(a, b):
    return jnp.dot(a, b, preferred_element_type=F32)


def dot_t(a, b):
    return lax.dot_general(a, b, (((1,), (1,)), ((), ())), preferred_element_type=F32)


def dot_tn(a, b):
    return lax.dot_general(a, b, (((0,), (0,)), ((), ())), preferred_element_type=F32)


def backward(latent, factor, d_norm):
    inner = jnp.mean(d_norm * latent, axis=-1, keepdims=True)
    return (factor * (d_norm - latent * (factor * factor * inner))).astype(BF)


def is_end(where_ref, u):
    return where_ref[2] == (NP - 1 if u == 0 else 0)


def quad_kernel(where_ref, own_ref, mirrored_ref, near_ref, crossed_ref, out_ref):
    xl = where_ref[3]
    out_ref[xl, 0] = own_ref[...]
    out_ref[xl, 1] = mirrored_ref[...]
    out_ref[1 - xl, 0] = near_ref[...]
    out_ref[1 - xl, 1] = crossed_ref[...]


def step0_kernel(where_ref, mask_ref, x_ref, carry_ref, *refs):
    chunks = refs[:18]
    outs = refs[18:]
    z = where_ref[0]
    core = where_ref[1]
    for part, c in enumerate((core, 1 - core)):
        refs = chunks[part * 9 : part * 9 + 9]
        for k in range(NZ):
            zz = lax.rem(z + k, NZ)
            for xl in range(2):
                row = pl.multiple_of(zz * 448 + xl * 224 + c * ROWS, 16)
                for sec in range(2):
                    for kind in range(2):
                        if k == 4:
                            block = refs[7 + xl][sec, kind]
                        else:
                            block = refs[k if k < 4 else k - 1][xl, sec, kind]
                        outs[sec * 7][kind, pl.ds(row, ROWS), :] = block
    for u in range(2):
        w_ref, latent_ref, factor_ref, normed_ref, cot_ref, d_lat_ref, out_ref = outs[u * 7 : u * 7 + 7]
        latent = dot(x_ref[0, :, u].reshape(STEPS * TOK, D), w_ref[0])
        factor = lax.rsqrt(jnp.mean(latent * latent, axis=-1, keepdims=True) + NORM_EPS)
        latent_ref[...] = latent
        factor_ref[...] = jnp.broadcast_to(factor, (STEPS * TOK, 128))
        normed_ref[...] = (latent * factor).astype(BF)
        end = is_end(where_ref, u)

        @pl.when(end)
        def _():
            for b in range(D // BLOCK):
                cols = slice(b * BLOCK, (b + 1) * BLOCK)
                out = x_ref[0, 0, u, :, cols].astype(F32) + dot_t(normed_ref[:TOK], w_ref[1, cols])
                cot_ref[:, cols] = (mask_ref[0, u] * out).astype(BF)

        @pl.when(jnp.logical_not(end))
        def _():
            cot_ref[...] = carry_ref[0, u]

        d_norm = dot(cot_ref[...], w_ref[1])
        d_lat_ref[...] = backward(latent_ref[:TOK], factor_ref[:TOK, :1], d_norm)
        for b in range(D // BLOCK):
            cols = slice(b * BLOCK, (b + 1) * BLOCK)
            out = cot_ref[:, cols].astype(F32) + dot_t(d_lat_ref[...], w_ref[0, cols])
            out_ref[:, cols] = out.astype(BF)


def step1_kernel(u, where_ref, mask_ref, x_ref, w_ref, latent_ref, factor_ref, normed_ref, cot0_ref, d_lat0_ref,
                 arr_ref, *refs):
    cot_ref, d_lat_ref, mine_ref, other_ref = refs[-4:]
    z = where_ref[0]
    core = where_ref[1]

    def emit(grad, b, kind):
        for i in range(2):
            k = lax.rem(2 * b + i - z + NZ, NZ)
            for xl in range(2):
                base = (i * 4 + xl * 2) * ROWS
                low = grad[base : base + ROWS]
                high = grad[base + ROWS : base + 2 * ROWS]
                mine_ref[k, xl, kind] = jnp.where(core == 0, low, high)
                other_ref[k, xl, kind] = jnp.where(core == 0, high, low)

    end = is_end(where_ref, u)

    @pl.when(end)
    def _():
        for b in range(D // BLOCK):
            cols = slice(b * BLOCK, (b + 1) * BLOCK)
            out = x_ref[0, 1, u, :, cols].astype(F32) + dot_t(normed_ref[TOK:], w_ref[1, cols])
            cot_ref[:, cols] = (mask_ref[1, u] * out).astype(BF)

    @pl.when(jnp.logical_not(end))
    def _():
        cot_ref[...] = arr_ref[...]

    d_norm = dot(cot_ref[...], w_ref[1])
    d_lat = backward(latent_ref[TOK:], factor_ref[TOK:, :1], d_norm)
    d_lat_ref[...] = d_lat
    d_lats = jnp.concatenate([d_lat0_ref[...], d_lat], axis=0)
    for b in range(D // BLOCK):
        cols = slice(b * BLOCK, (b + 1) * BLOCK)
        cots = jnp.concatenate([cot0_ref[:, cols], cot_ref[:, cols]], axis=0)
        emit((dot_tn(cots, normed_ref[...]) * SCALES[1]).astype(BF), b, 1)
        xs = x_ref[0, :, u, :, cols].reshape(STEPS * TOK, BLOCK)
        emit((dot_tn(xs, d_lats) * SCALES[0]).astype(BF), b, 0)


def carry_kernel(where_ref, *refs):
    out_ref = refs[-1]
    for u in range(2):
        w_ref, d_lat_ref, cot_ref = refs[u * 3 : u * 3 + 3]
        for b in range(D // BLOCK):
            cols = slice(b * BLOCK, (b + 1) * BLOCK)
            out = cot_ref[:, cols].astype(F32) + dot_t(d_lat_ref[...], w_ref[0, cols])
            out_ref[0, u, :, cols] = out.astype(BF)


def far_kernel(where_ref, mine_ref, theirs_ref, low_ref, high_ref):
    for xl, ref in enumerate((low_ref, high_ref)):
        ref[...] = (mine_ref[4, xl].astype(F32) + theirs_ref[4, xl].astype(F32)).astype(BF)


def join_kernel(k, half, where_ref, mine_ref, theirs_ref, arrived_ref, out_ref):
    for xl in range(2):
        total = mine_ref[k, xl].astype(F32) + theirs_ref[k, xl].astype(F32)
        if half is None:
            total = total + arrived_ref[xl].astype(F32)
        elif half == xl:
            total = total + arrived_ref[...].astype(F32)
        out_ref[xl] = total.astype(BF)


def last_kernel(where_ref, mine_ref, theirs_ref, ahead_ref, back_ref, *refs):
    keep_ref, give_ref = refs[-2:]
    xl = where_ref[3]

    def total(i):
        parts = (mine_ref[0, i], theirs_ref[0, i], ahead_ref[i], back_ref[i])
        return sum(part.astype(F32) for part in parts)

    keep_ref[...] = total(xl).astype(keep_ref.dtype)
    give_ref[...] = total(1 - xl).astype(BF)


def token(*arrays):
    return sum(a.reshape(-1, a.shape[-1])[:8, :128].astype(F32) for a in arrays)


def local(section_inputs, carry_in, loss_mask, weights, moment1, moment2):
    where = jnp.stack(
        [lax.axis_index("z"), lax.axis_index("core"), lax.axis_index(PIPE), lax.axis_index("xl")]
    ).astype(jnp.int32)
    multipliers = jnp.array(SCALES, F32).reshape(2, 1, 1)
    own = (weights[0] * multipliers).astype(BF)
    mask = loss_mask.astype(F32)[..., None]
    shard = (2, ROWS, LATENT)
    chunk = sds((2, *shard), BF)
    unit = 2 * TOK * D * LATENT
    small = 1 << 20

    def gather(start):
        ahead, back = [start], [start]
        for _ in range(3):
            ahead.append(shift(ahead[-1], "z", 1, NZ))
            back.append(shift(back[-1], "z", -1, NZ))
        low = shift(ahead[3][0], "z", 1, NZ)
        high = shift(back[3][1], "z", -1, NZ)
        chunks = back + ahead[:0:-1] + [low, high]
        return chunks + [swap(c, "core") for c in chunks]

    def hop(u, out):
        if u == 0:
            return lax.ppermute(out, PIPE, [(i, i - 1) for i in range(1, NP)])
        return lax.ppermute(out, PIPE, [(i, i + 1) for i in range(NP - 1)])

    def step1(u, state, arrived, *after):
        w, latent, factor, normed, cot0, d_lat0, _ = state
        terms = sds((NZ, *chunk.shape), BF)
        cot1, d_lat1, mine, other = call(
            lambda *refs: step1_kernel(u, *refs),
            [sds((TOK, D), BF), sds((TOK, LATENT), BF), terms, terms],
            [where, mask, section_inputs, w, latent, factor, normed, cot0, d_lat0, arrived, *after],
            6 * unit,
        )
        return (w, d_lat1, cot1), mine, swap(other, "core")

    def scatter(mine, theirs, keep_type, *after):
        both = [where, mine, theirs]

        def join(k, half, arrived):
            return call(lambda *refs: join_kernel(k, half, *refs), [chunk], [*both, arrived], small)[0]

        low, high = call(far_kernel, [sds(shard, BF), sds(shard, BF)], both, small)
        ahead = join(3, 0, shift(low, "z", 1, NZ))
        back = join(5, 1, shift(high, "z", -1, NZ))
        ahead = join(2, None, shift(ahead, "z", 1, NZ))
        back = join(6, None, shift(back, "z", -1, NZ))
        ahead = join(1, None, shift(ahead, "z", 1, NZ))
        back = join(7, None, shift(back, "z", -1, NZ))
        ahead = shift(ahead, "z", 1, NZ)
        back = shift(back, "z", -1, NZ)
        parts = [*both, ahead, back, *after]
        keep, give = call(last_kernel, [sds(shard, keep_type), sds(shard, BF)], parts, small)
        return keep, give

    shards = [where, own, mirror(own), swap(own, "xl"), mirror_cross(own)]
    chunks = gather(call(quad_kernel, [sds((2, 2, *shard), BF)], shards, small)[0])
    state = [
        sds((2, D, LATENT), BF), sds((STEPS * TOK, LATENT), F32), sds((STEPS * TOK, 128), F32),
        sds((STEPS * TOK, LATENT), BF), sds((TOK, D), BF), sds((TOK, LATENT), BF), sds((TOK, D), BF),
    ]
    states = call(step0_kernel, state * 2, [where, mask, section_inputs, carry_in, *chunks], 10 * unit)
    state_a, state_b = states[:7], states[7:]
    arrived_b = hop(1, state_b[-1])
    arrived_a = hop(0, state_a[-1])
    end_b, mine_b, theirs_b = step1(1, state_b, arrived_b)
    end_a, mine_a, theirs_a = step1(0, state_a, arrived_a, token(end_b[1]))
    (carry_out,) = call(carry_kernel, [sds((1, 2, TOK, D), BF)], [where, *end_a, *end_b], 2 * unit)
    keep_b, give_b = scatter(mine_b, theirs_b, BF)
    mirrored = mirror(keep_b).astype(F32)
    crossed = mirror_cross(give_b).astype(F32)
    keep_a, give_a = scatter(mine_a, theirs_a, F32, token(carry_out), token(keep_b))
    near = swap(give_a, "xl").astype(F32)
    gradient = (keep_a + near + mirrored + crossed)[None]

    squares = jnp.sum((gradient * gradient).reshape(-1, 128), axis=0)
    squares = jnp.broadcast_to(squares, (NP * NZ * 4, 1, 128))
    square_total = jnp.sum(lax.all_to_all(squares, PIPE + DP, 0, 0, tiled=True))
    clip_limit = math.sqrt(2.0 * NP * D * LATENT)
    clip_scale = jnp.minimum(1.0, clip_limit / jnp.sqrt(square_total + CLIP_EPS))
    clipped = gradient * clip_scale
    new_moment1 = BETA_ONE * moment1 + (1.0 - BETA_ONE) * clipped
    new_moment2 = BETA_TWO * moment2 + (1.0 - BETA_TWO) * clipped * clipped
    update = (
        new_moment1
        / (1.0 - BETA_ONE**ADAM_STEP)
        / (jnp.sqrt(new_moment2 / (1.0 - BETA_TWO**ADAM_STEP)) + ADAM_EPS)
    )
    new_weights = weights - LEARN_RATE * (update + DECAY_RATE * weights)
    return (carry_out, new_weights, new_moment1, new_moment2)


def solution(mesh):
    fine = Mesh(mesh.devices.reshape(2, 4, 8, 2, 2), PIPE + DP)
    rows = P(PIPE, None, DP, None)
    return jax.shard_map(
        local,
        mesh=fine,
        in_specs=(P(PIPE, None, None, DP, None), rows, P(None, None, DP), rows, rows, rows),
        out_specs=(rows, rows, rows, rows),
        check_vma=False,
    )
```

```python
import math

import jax
import jax.numpy as jnp
from jax import lax
from jax.experimental import pallas as pl
from jax.experimental.pallas import tpu as pltpu
from jax.sharding import Mesh
from jax.sharding import PartitionSpec as P

D = 3584
LATENT = 256
STEPS = 2
ADAM_STEP = 10
TOK = 128
ROWS = 112
NZ = 8
NP = 8
BLOCK = 896
KERNEL_MB = 12

NORM_EPS = 1e-06
BETA_ONE = 0.9
BETA_TWO = 0.95
ADAM_EPS = 1e-08
LEARN_RATE = 0.02
DECAY_RATE = 0.1
CLIP_EPS = 1e-06

SCALES = (D ** (-0.5), LATENT ** (-0.5))
PIPE = ("xh", "y")
DP = ("z", "xl", "core")
BF = jnp.bfloat16
F32 = jnp.float32


def shift(value, axis, by, size):
    return lax.ppermute(value, axis, [(i, (i + by) % size) for i in range(size)])


def swap(value, axis):
    return lax.ppermute(value, axis, [(0, 1), (1, 0)])


def mirror(value):
    return lax.ppermute(value, PIPE, [(i, NP - 1 - i) for i in range(NP)])


def mirror_cross(value):
    pairs = [(i * 2 + a, (NP - 1 - i) * 2 + 1 - a) for i in range(NP) for a in range(2)]
    return lax.ppermute(value, ("xh", "y", "xl"), pairs)


def sds(shape, dtype):
    return jax.ShapeDtypeStruct(shape, dtype)


def call(kernel, out_shape, ins, flops, aliases=None):
    nbytes = sum(math.prod(a.shape) * a.dtype.itemsize for a in list(ins) + list(out_shape))
    vmem = pl.BlockSpec(memory_space=pltpu.VMEM)
    return pl.pallas_call(
        kernel,
        out_shape=out_shape,
        in_specs=[pl.BlockSpec(memory_space=pltpu.SMEM)] + [vmem] * (len(ins) - 1),
        out_specs=[vmem] * len(out_shape),
        input_output_aliases=aliases or {},
        compiler_params=pltpu.CompilerParams(vmem_limit_bytes=KERNEL_MB * 2**20),
        cost_estimate=pl.CostEstimate(flops=flops, bytes_accessed=nbytes, transcendentals=0),
    )(*ins)


def dot(a, b):
    return jnp.dot(a, b, preferred_element_type=F32)


def dot_t(a, b):
    return lax.dot_general(a, b, (((1,), (1,)), ((), ())), preferred_element_type=F32)


def dot_tn(a, b):
    return lax.dot_general(a, b, (((0,), (0,)), ((), ())), preferred_element_type=F32)


def backward(latent, factor, d_norm):
    inner = jnp.mean(d_norm * latent, axis=-1, keepdims=True)
    return (factor * (d_norm - latent * (factor * factor * inner))).astype(BF)


def is_end(where_ref, u):
    return where_ref[2] == (NP - 1 if u == 0 else 0)


def quad_kernel(where_ref, own_ref, mirrored_ref, near_ref, crossed_ref, out_ref):
    xl = where_ref[3]
    out_ref[xl, 0] = own_ref[...]
    out_ref[xl, 1] = mirrored_ref[...]
    out_ref[1 - xl, 0] = near_ref[...]
    out_ref[1 - xl, 1] = crossed_ref[...]


def put(where_ref, w_ref, k, other, block_of):
    core = where_ref[1]
    zz = lax.rem(where_ref[0] + k, NZ)
    for xl in range(2):
        row = zz * 448 + xl * 224 + (1 - core if other else core) * ROWS
        for sec in range(2):
            for kind in range(2):
                w_ref[sec, kind, pl.ds(pl.multiple_of(row, 16), ROWS), :] = block_of(xl, sec, kind)


def place_kernel(ks, where_ref, *refs):
    w_ref = refs[-1]
    for i, ref in enumerate(refs[: 2 * len(ks)]):
        put(where_ref, w_ref, ks[i // 2], i % 2, lambda xl, sec, kind: ref[xl, sec, kind])


def step0_kernel(where_ref, mask_ref, x_ref, carry_ref, low_ref, low2_ref, high_ref, high2_ref, _, *outs):
    w_both_ref = outs[-1]
    for other, halves in enumerate(((low_ref, high_ref), (low2_ref, high2_ref))):
        put(where_ref, w_both_ref, 4, other, lambda xl, sec, kind: halves[xl][sec, kind])
    for u in range(2):
        latent_ref, factor_ref, normed_ref, cot_ref, d_lat_ref, out_ref = outs[u * 6 : u * 6 + 6]
        w_ref = w_both_ref.at[u]
        latent = dot(x_ref[0, :, u].reshape(STEPS * TOK, D), w_ref[0])
        factor = lax.rsqrt(jnp.mean(latent * latent, axis=-1, keepdims=True) + NORM_EPS)
        latent_ref[...] = latent
        factor_ref[...] = jnp.broadcast_to(factor, (STEPS * TOK, 128))
        normed_ref[...] = (latent * factor).astype(BF)
        end = is_end(where_ref, u)

        @pl.when(end)
        def _():
            for b in range(D // BLOCK):
                cols = slice(b * BLOCK, (b + 1) * BLOCK)
                out = x_ref[0, 0, u, :, cols].astype(F32) + dot_t(normed_ref[:TOK], w_ref[1, cols])
                cot_ref[:, cols] = (mask_ref[0, u] * out).astype(BF)

        @pl.when(jnp.logical_not(end))
        def _():
            cot_ref[...] = carry_ref[0, u]

        d_norm = dot(cot_ref[...], w_ref[1])
        d_lat_ref[...] = backward(latent_ref[:TOK], factor_ref[:TOK, :1], d_norm)
        for b in range(D // BLOCK):
            cols = slice(b * BLOCK, (b + 1) * BLOCK)
            out = cot_ref[:, cols].astype(F32) + dot_t(d_lat_ref[...], w_ref[0, cols])
            out_ref[:, cols] = out.astype(BF)


def step1_kernel(u, where_ref, mask_ref, x_ref, w_both_ref, latent_ref, factor_ref, normed_ref, cot0_ref, d_lat0_ref,
                 arr_ref, *refs):
    cot_ref, d_lat_ref, mine_ref, other_ref = refs[-4:]
    w_ref = w_both_ref.at[u]
    z = where_ref[0]
    core = where_ref[1]

    def emit(grad, b, kind):
        for i in range(2):
            k = lax.rem(2 * b + i - z + NZ, NZ)
            for xl in range(2):
                base = (i * 4 + xl * 2) * ROWS
                low = grad[base : base + ROWS]
                high = grad[base + ROWS : base + 2 * ROWS]
                mine_ref[k, xl, kind] = jnp.where(core == 0, low, high)
                other_ref[k, xl, kind] = jnp.where(core == 0, high, low)

    end = is_end(where_ref, u)

    @pl.when(end)
    def _():
        for b in range(D // BLOCK):
            cols = slice(b * BLOCK, (b + 1) * BLOCK)
            out = x_ref[0, 1, u, :, cols].astype(F32) + dot_t(normed_ref[TOK:], w_ref[1, cols])
            cot_ref[:, cols] = (mask_ref[1, u] * out).astype(BF)

    @pl.when(jnp.logical_not(end))
    def _():
        cot_ref[...] = arr_ref[...]

    d_norm = dot(cot_ref[...], w_ref[1])
    d_lat = backward(latent_ref[TOK:], factor_ref[TOK:, :1], d_norm)
    d_lat_ref[...] = d_lat
    d_lats = jnp.concatenate([d_lat0_ref[...], d_lat], axis=0)
    for b in range(D // BLOCK):
        cols = slice(b * BLOCK, (b + 1) * BLOCK)
        cots = jnp.concatenate([cot0_ref[:, cols], cot_ref[:, cols]], axis=0)
        emit((dot_tn(cots, normed_ref[...]) * SCALES[1]).astype(BF), b, 1)
        xs = x_ref[0, :, u, :, cols].reshape(STEPS * TOK, BLOCK)
        emit((dot_tn(xs, d_lats) * SCALES[0]).astype(BF), b, 0)


def carry_kernel(where_ref, w_both_ref, *refs):
    out_ref, done_ref = refs[-2:]
    done_ref[...] = jnp.zeros_like(done_ref)
    for u in range(2):
        w_ref = w_both_ref.at[u]
        d_lat_ref, cot_ref = refs[u * 2 : u * 2 + 2]
        for b in range(D // BLOCK):
            cols = slice(b * BLOCK, (b + 1) * BLOCK)
            out = cot_ref[:, cols].astype(F32) + dot_t(d_lat_ref[...], w_ref[0, cols])
            out_ref[0, u, :, cols] = out.astype(BF)


def far_kernel(where_ref, mine_ref, theirs_ref, low_ref, high_ref):
    for xl, ref in enumerate((low_ref, high_ref)):
        ref[...] = (mine_ref[4, xl].astype(F32) + theirs_ref[4, xl].astype(F32)).astype(BF)


def join_kernel(k, half, where_ref, mine_ref, theirs_ref, arrived_ref, out_ref):
    for xl in range(2):
        total = mine_ref[k, xl].astype(F32) + theirs_ref[k, xl].astype(F32)
        if half is None:
            total = total + arrived_ref[xl].astype(F32)
        elif half == xl:
            total = total + arrived_ref[...].astype(F32)
        out_ref[xl] = total.astype(BF)


def last_kernel(where_ref, mine_ref, theirs_ref, ahead_ref, back_ref, *refs):
    keep_ref, give_ref = refs[-2:]
    xl = where_ref[3]

    def total(i):
        parts = (mine_ref[0, i], theirs_ref[0, i], ahead_ref[i], back_ref[i])
        return sum(part.astype(F32) for part in parts)

    keep_ref[...] = total(xl).astype(keep_ref.dtype)
    give_ref[...] = total(1 - xl).astype(BF)


def gradient_kernel(where_ref, keep_ref, near_ref, mirrored_ref, crossed_ref, _, out_ref, squares_ref):
    total = keep_ref[...] + near_ref[...].astype(F32) + mirrored_ref[...].astype(F32) + crossed_ref[...].astype(F32)
    out_ref[0] = total
    squares = jnp.sum((total * total).reshape(2 * ROWS, LATENT), axis=0, keepdims=True)
    squares_ref[...] = squares[:, :128] + squares[:, 128:]


def local(section_inputs, carry_in, loss_mask, weights, moment1, moment2):
    where = jnp.stack(
        [lax.axis_index("z"), lax.axis_index("core"), lax.axis_index(PIPE), lax.axis_index("xl")]
    ).astype(jnp.int32)
    multipliers = jnp.array(SCALES, F32).reshape(2, 1, 1)
    own = (weights[0] * multipliers).astype(BF)
    mask = loss_mask.astype(F32)[..., None]
    shard = (2, ROWS, LATENT)
    chunk = sds((2, *shard), BF)
    unit = 2 * TOK * D * LATENT
    small = 1 << 20

    def place(ks, chunks, *held):
        ins = [where]
        for c in chunks:
            ins += [c, swap(c, "core")]
        ins += held
        aliases = {len(ins) - 1: 0} if held else None
        kernel = lambda *refs: place_kernel(ks, *refs)
        return call(kernel, [sds((2, 2, D, LATENT), BF)], ins, 40 * unit, aliases)[0]

    def gather(start):
        w = place((0,), [start])
        ahead = back = start
        for k in range(1, 4):
            ahead = shift(ahead, "z", 1, NZ)
            back = shift(back, "z", -1, NZ)
            w = place((k, NZ - k), [back, ahead], w)
        return w, shift(ahead[0], "z", 1, NZ), shift(back[1], "z", -1, NZ)

    def hop(u, out):
        if u == 0:
            return lax.ppermute(out, PIPE, [(i, i - 1) for i in range(1, NP)])
        return lax.ppermute(out, PIPE, [(i, i + 1) for i in range(NP - 1)])

    def step1(u, state, arrived, *after):
        latent, factor, normed, cot0, d_lat0, _ = state
        terms = sds((NZ, *chunk.shape), BF)
        cot1, d_lat1, mine, other = call(
            lambda *refs: step1_kernel(u, *refs),
            [sds((TOK, D), BF), sds((TOK, LATENT), BF), terms, terms],
            [where, mask, section_inputs, w, latent, factor, normed, cot0, d_lat0, arrived, *after],
            6 * unit,
        )
        return (d_lat1, cot1), mine, swap(other, "core")

    def scatter(mine, theirs, keep_type, *after):
        both = [where, mine, theirs]

        def join(k, half, arrived):
            return call(lambda *refs: join_kernel(k, half, *refs), [chunk], [*both, arrived], small)[0]

        low, high = call(far_kernel, [sds(shard, BF), sds(shard, BF)], both, small)
        ahead = join(3, 0, shift(low, "z", 1, NZ))
        back = join(5, 1, shift(high, "z", -1, NZ))
        ahead = join(2, None, shift(ahead, "z", 1, NZ))
        back = join(6, None, shift(back, "z", -1, NZ))
        ahead = join(1, None, shift(ahead, "z", 1, NZ))
        back = join(7, None, shift(back, "z", -1, NZ))
        ahead = shift(ahead, "z", 1, NZ)
        back = shift(back, "z", -1, NZ)
        parts = [*both, ahead, back, *after]
        keep, give = call(last_kernel, [sds(shard, keep_type), sds(shard, BF)], parts, small)
        return keep, give

    shards = [where, own, mirror(own), swap(own, "xl"), mirror_cross(own)]
    w, low, high = gather(call(quad_kernel, [sds((2, 2, *shard), BF)], shards, small)[0])
    state = [
        sds((STEPS * TOK, LATENT), F32), sds((STEPS * TOK, 128), F32), sds((STEPS * TOK, LATENT), BF),
        sds((TOK, D), BF), sds((TOK, LATENT), BF), sds((TOK, D), BF),
    ]
    ins = [where, mask, section_inputs, carry_in, low, swap(low, "core"), high, swap(high, "core"), w]
    *states, w = call(step0_kernel, state * 2 + [sds(w.shape, BF)], ins, 10 * unit, {len(ins) - 1: 12})
    state_a, state_b = states[:6], states[6:]
    arrived_b = hop(1, state_b[-1])
    arrived_a = hop(0, state_a[-1])
    end_b, mine_b, theirs_b = step1(1, state_b, arrived_b)
    end_a, mine_a, theirs_a = step1(0, state_a, arrived_a, end_b[0])
    keep_b, give_b = scatter(mine_b, theirs_b, BF)
    mirrored = mirror(keep_b)
    crossed = mirror_cross(give_b)
    keep_a, give_a = scatter(mine_a, theirs_a, F32, keep_b)
    near = swap(give_a, "xl")
    outs = [sds((1, 2, TOK, D), BF), sds((8, 128), F32)]
    carry_out, done = call(carry_kernel, outs, [where, w, *end_a, *end_b], 2 * unit)
    outs = [sds((1, *shard), F32), sds((1, 128), F32)]
    gradient, squares = call(gradient_kernel, outs, [where, keep_a, near, mirrored, crossed, done], small)
    squares = jnp.broadcast_to(squares, (NP * NZ * 4, 1, 128))
    square_total = jnp.sum(lax.all_to_all(squares, PIPE + DP, 0, 0, tiled=True))
    clip_limit = math.sqrt(2.0 * NP * D * LATENT)
    clip_scale = jnp.minimum(1.0, clip_limit / jnp.sqrt(square_total + CLIP_EPS))
    clipped = gradient * clip_scale
    new_moment1 = BETA_ONE * moment1 + (1.0 - BETA_ONE) * clipped
    new_moment2 = BETA_TWO * moment2 + (1.0 - BETA_TWO) * clipped * clipped
    update = (
        new_moment1
        / (1.0 - BETA_ONE**ADAM_STEP)
        / (jnp.sqrt(new_moment2 / (1.0 - BETA_TWO**ADAM_STEP)) + ADAM_EPS)
    )
    new_weights = weights - LEARN_RATE * (update + DECAY_RATE * weights)
    return (carry_out, new_weights, new_moment1, new_moment2)


def solution(mesh):
    fine = Mesh(mesh.devices.reshape(2, 4, 8, 2, 2), PIPE + DP)
    rows = P(PIPE, None, DP, None)
    return jax.shard_map(
        local,
        mesh=fine,
        in_specs=(P(PIPE, None, None, DP, None), rows, P(None, None, DP), rows, rows, rows),
        out_specs=(rows, rows, rows, rows),
        check_vma=False,
    )
```

```python
import functools
import math

import jax
import jax.numpy as jnp
from jax import lax
from jax.experimental import pallas as pl
from jax.experimental.pallas import tpu as pltpu
from jax.sharding import Mesh
from jax.sharding import PartitionSpec as P

D = 3584
LATENT = 256
STEPS = 2
ADAM_STEP = 10
TOK = 128
ROWS = 112
NZ = 8
NP = 8
BLOCK = 896
KERNEL_MB = 12

NORM_EPS = 1e-06
BETA_ONE = 0.9
BETA_TWO = 0.95
ADAM_EPS = 1e-08
LEARN_RATE = 0.02
DECAY_RATE = 0.1
CLIP_EPS = 1e-06

SCALES = (D ** (-0.5), LATENT ** (-0.5))
PIPE = ("xh", "y")
DP = ("z", "xl", "core")
BF = jnp.bfloat16
F32 = jnp.float32


def shift(value, axis, by, size):
    return lax.ppermute(value, axis, [(i, (i + by) % size) for i in range(size)])


def swap(value, axis):
    return lax.ppermute(value, axis, [(0, 1), (1, 0)])


def mirror(value):
    return lax.ppermute(value, PIPE, [(i, NP - 1 - i) for i in range(NP)])


def mirror_cross(value):
    pairs = [(i * 2 + a, (NP - 1 - i) * 2 + 1 - a) for i in range(NP) for a in range(2)]
    return lax.ppermute(value, ("xh", "y", "xl"), pairs)


def sds(shape, dtype):
    return jax.ShapeDtypeStruct(shape, dtype)


def call(kernel, out_shape, ins, flops, aliases=None):
    nbytes = sum(math.prod(a.shape) * a.dtype.itemsize for a in list(ins) + list(out_shape))
    vmem = pl.BlockSpec(memory_space=pltpu.VMEM)
    return pl.pallas_call(
        kernel,
        out_shape=out_shape,
        in_specs=[pl.BlockSpec(memory_space=pltpu.SMEM)] + [vmem] * (len(ins) - 1),
        out_specs=[vmem] * len(out_shape),
        input_output_aliases=aliases or {},
        compiler_params=pltpu.CompilerParams(vmem_limit_bytes=KERNEL_MB * 2**20),
        cost_estimate=pl.CostEstimate(flops=flops, bytes_accessed=nbytes, transcendentals=0),
    )(*ins)


def dot(a, b):
    return jnp.dot(a, b, preferred_element_type=F32)


def dot_t(a, b):
    return lax.dot_general(a, b, (((1,), (1,)), ((), ())), preferred_element_type=F32)


def dot_tn(a, b):
    return lax.dot_general(a, b, (((0,), (0,)), ((), ())), preferred_element_type=F32)


def backward(latent, factor, d_norm):
    inner = jnp.mean(d_norm * latent, axis=-1, keepdims=True)
    return (factor * (d_norm - latent * (factor * factor * inner))).astype(BF)


def is_end(where_ref, u):
    return where_ref[2] == (NP - 1 if u == 0 else 0)


def quad_kernel(where_ref, own_ref, mirrored_ref, near_ref, crossed_ref, out_ref):
    xl = where_ref[3]
    out_ref[xl, 0] = own_ref[...]
    out_ref[xl, 1] = mirrored_ref[...]
    out_ref[1 - xl, 0] = near_ref[...]
    out_ref[1 - xl, 1] = crossed_ref[...]


def put(where_ref, w_ref, sections, k, other, block_of):
    core = where_ref[1]
    zz = lax.rem(where_ref[0] + k, NZ)
    for xl in range(2):
        row = zz * 448 + xl * 224 + (1 - core if other else core) * ROWS
        for sec in sections:
            for kind in range(2):
                w_ref[sec, kind, pl.ds(pl.multiple_of(row, 16), ROWS), :] = block_of(xl, sec, kind)


def place_kernel(ks, where_ref, *refs):
    w_ref = refs[-1]
    for i, ref in enumerate(refs[: 2 * len(ks)]):
        put(where_ref, w_ref, (0, 1), ks[i // 2], i % 2, lambda xl, sec, kind: ref[xl, sec, kind])


def step0_kernel(u, where_ref, mask_ref, x_ref, carry_ref, low_ref, low2_ref, high_ref, high2_ref, _, *outs):
    latent_ref, factor_ref, normed_ref, cot_ref, d_lat_ref, out_ref, w_both_ref = outs
    w_ref = w_both_ref.at[u]
    for other, halves in enumerate(((low_ref, high_ref), (low2_ref, high2_ref))):
        put(where_ref, w_both_ref, (u,), 4, other, lambda xl, sec, kind: halves[xl][sec, kind])
    latent = dot(x_ref[0, :, u].reshape(STEPS * TOK, D), w_ref[0])
    factor = lax.rsqrt(jnp.mean(latent * latent, axis=-1, keepdims=True) + NORM_EPS)
    latent_ref[...] = latent
    factor_ref[...] = jnp.broadcast_to(factor, (STEPS * TOK, 128))
    normed_ref[...] = (latent * factor).astype(BF)
    end = is_end(where_ref, u)

    @pl.when(end)
    def _():
        for b in range(D // BLOCK):
            cols = slice(b * BLOCK, (b + 1) * BLOCK)
            out = x_ref[0, 0, u, :, cols].astype(F32) + dot_t(normed_ref[:TOK], w_ref[1, cols])
            cot_ref[:, cols] = (mask_ref[0, u] * out).astype(BF)

    @pl.when(jnp.logical_not(end))
    def _():
        cot_ref[...] = carry_ref[0, u]

    d_norm = dot(cot_ref[...], w_ref[1])
    d_lat_ref[...] = backward(latent_ref[:TOK], factor_ref[:TOK, :1], d_norm)
    for b in range(D // BLOCK):
        cols = slice(b * BLOCK, (b + 1) * BLOCK)
        out = cot_ref[:, cols].astype(F32) + dot_t(d_lat_ref[...], w_ref[0, cols])
        out_ref[:, cols] = out.astype(BF)


def step1_kernel(u, where_ref, mask_ref, x_ref, w_both_ref, latent_ref, factor_ref, normed_ref, cot0_ref, d_lat0_ref,
                 arr_ref, *refs):
    cot_ref, d_lat_ref, mine_ref, other_ref = refs[-4:]
    w_ref = w_both_ref.at[u]
    z = where_ref[0]
    core = where_ref[1]

    def emit(grad, b, kind):
        for i in range(2):
            k = lax.rem(2 * b + i - z + NZ, NZ)
            for xl in range(2):
                base = (i * 4 + xl * 2) * ROWS
                low = grad[base : base + ROWS]
                high = grad[base + ROWS : base + 2 * ROWS]
                mine_ref[k, xl, kind] = jnp.where(core == 0, low, high)
                other_ref[k, xl, kind] = jnp.where(core == 0, high, low)

    end = is_end(where_ref, u)

    @pl.when(end)
    def _():
        for b in range(D // BLOCK):
            cols = slice(b * BLOCK, (b + 1) * BLOCK)
            out = x_ref[0, 1, u, :, cols].astype(F32) + dot_t(normed_ref[TOK:], w_ref[1, cols])
            cot_ref[:, cols] = (mask_ref[1, u] * out).astype(BF)

    @pl.when(jnp.logical_not(end))
    def _():
        cot_ref[...] = arr_ref[...]

    d_norm = dot(cot_ref[...], w_ref[1])
    d_lat = backward(latent_ref[TOK:], factor_ref[TOK:, :1], d_norm)
    d_lat_ref[...] = d_lat
    d_lats = jnp.concatenate([d_lat0_ref[...], d_lat], axis=0)
    for b in range(D // BLOCK):
        cols = slice(b * BLOCK, (b + 1) * BLOCK)
        cots = jnp.concatenate([cot0_ref[:, cols], cot_ref[:, cols]], axis=0)
        emit((dot_tn(cots, normed_ref[...]) * SCALES[1]).astype(BF), b, 1)
        xs = x_ref[0, :, u, :, cols].reshape(STEPS * TOK, BLOCK)
        emit((dot_tn(xs, d_lats) * SCALES[0]).astype(BF), b, 0)


def carry_kernel(where_ref, w_both_ref, *refs):
    out_ref, done_ref = refs[-2:]
    done_ref[...] = jnp.zeros_like(done_ref)
    for u in range(2):
        w_ref = w_both_ref.at[u]
        d_lat_ref, cot_ref = refs[u * 2 : u * 2 + 2]
        for b in range(D // BLOCK):
            cols = slice(b * BLOCK, (b + 1) * BLOCK)
            out = cot_ref[:, cols].astype(F32) + dot_t(d_lat_ref[...], w_ref[0, cols])
            out_ref[0, u, :, cols] = out.astype(BF)


def far_kernel(where_ref, mine_ref, theirs_ref, low_ref, high_ref):
    for xl, ref in enumerate((low_ref, high_ref)):
        ref[...] = (mine_ref[4, xl].astype(F32) + theirs_ref[4, xl].astype(F32)).astype(BF)


def join_kernel(k, where_ref, mine_ref, theirs_ref, ahead_ref, back_ref, ahead_out_ref, back_out_ref):
    sides = ((k, ahead_ref, ahead_out_ref, 0), (NZ - k, back_ref, back_out_ref, 1))
    for place, arrived_ref, out_ref, half in sides:
        for xl in range(2):
            total = mine_ref[place, xl].astype(F32) + theirs_ref[place, xl].astype(F32)
            if k < 3:
                total = total + arrived_ref[xl].astype(F32)
            elif xl == half:
                total = total + arrived_ref[...].astype(F32)
            out_ref[xl] = total.astype(BF)


def last_kernel(where_ref, mine_ref, theirs_ref, ahead_ref, back_ref, *refs):
    keep_ref, give_ref = refs[-2:]
    xl = where_ref[3]

    def total(i):
        parts = (mine_ref[0, i], theirs_ref[0, i], ahead_ref[i], back_ref[i])
        return sum(part.astype(F32) for part in parts)

    keep_ref[...] = total(xl).astype(keep_ref.dtype)
    give_ref[...] = total(1 - xl).astype(BF)


def gradient_kernel(where_ref, keep_ref, near_ref, mirrored_ref, crossed_ref, _, out_ref, squares_ref):
    total = keep_ref[...] + near_ref[...].astype(F32) + mirrored_ref[...].astype(F32) + crossed_ref[...].astype(F32)
    out_ref[0] = total
    squares = jnp.sum((total * total).reshape(2 * ROWS, LATENT), axis=0, keepdims=True)
    squares_ref[...] = squares[:, :128] + squares[:, 128:]


def local(section_inputs, carry_in, loss_mask, weights, moment1, moment2):
    where = jnp.stack(
        [lax.axis_index("z"), lax.axis_index("core"), lax.axis_index(PIPE), lax.axis_index("xl")]
    ).astype(jnp.int32)
    multipliers = jnp.array(SCALES, F32).reshape(2, 1, 1)
    own = (weights[0] * multipliers).astype(BF)
    mask = loss_mask.astype(F32)[..., None]
    shard = (2, ROWS, LATENT)
    chunk = sds((2, *shard), BF)
    unit = 2 * TOK * D * LATENT
    small = 1 << 20

    def place(ks, chunks, *held):
        ins = [where]
        for c in chunks:
            ins += [c, swap(c, "core")]
        ins += held
        aliases = {len(ins) - 1: 0} if held else None
        kernel = lambda *refs: place_kernel(ks, *refs)
        return call(kernel, [sds((2, 2, D, LATENT), BF)], ins, 10 * unit, aliases)[0]

    def gather(start):
        w = place((0,), [start])
        ahead = back = start
        for k in range(1, 4):
            ahead = shift(ahead, "z", 1, NZ)
            back = shift(back, "z", -1, NZ)
            w = place((k, NZ - k), [back, ahead], w)
        return w, shift(ahead[0], "z", 1, NZ), shift(back[1], "z", -1, NZ)

    def hop(u, out):
        if u == 0:
            return lax.ppermute(out, PIPE, [(i, i - 1) for i in range(1, NP)])
        return lax.ppermute(out, PIPE, [(i, i + 1) for i in range(NP - 1)])

    def step1(u, state, arrived, *after):
        latent, factor, normed, cot0, d_lat0, _ = state
        terms = sds((NZ, *chunk.shape), BF)
        cot1, d_lat1, mine, other = call(
            lambda *refs: step1_kernel(u, *refs),
            [sds((TOK, D), BF), sds((TOK, LATENT), BF), terms, terms],
            [where, mask, section_inputs, w, latent, factor, normed, cot0, d_lat0, arrived, *after],
            6 * unit,
        )
        return (d_lat1, cot1), mine, swap(other, "core")

    def scatter(mine, theirs, keep_type, *after):
        both = [where, mine, theirs]

        ahead, back = call(far_kernel, [sds(shard, BF), sds(shard, BF)], both, small)
        for k in (3, 2, 1):
            ins = [*both, shift(ahead, "z", 1, NZ), shift(back, "z", -1, NZ)]
            ahead, back = call(functools.partial(join_kernel, k), [chunk, chunk], ins, small)
        ahead = shift(ahead, "z", 1, NZ)
        back = shift(back, "z", -1, NZ)
        parts = [*both, ahead, back, *after]
        keep, give = call(last_kernel, [sds(shard, keep_type), sds(shard, BF)], parts, small)
        return keep, give

    shards = [where, own, mirror(own), swap(own, "xl"), mirror_cross(own)]
    w, low, high = gather(call(quad_kernel, [sds((2, 2, *shard), BF)], shards, small)[0])
    state = [
        sds((STEPS * TOK, LATENT), F32), sds((STEPS * TOK, 128), F32), sds((STEPS * TOK, LATENT), BF),
        sds((TOK, D), BF), sds((TOK, LATENT), BF), sds((TOK, D), BF),
    ]
    last = [low, swap(low, "core"), high, swap(high, "core")]

    def step0(u, w):
        ins = [where, mask, section_inputs, carry_in, *last, w]
        kernel = lambda *refs: step0_kernel(u, *refs)
        *out, w = call(kernel, state + [sds(w.shape, BF)], ins, 5 * unit, {len(ins) - 1: len(state)})
        return out, w

    state_b, w = step0(1, w)
    state_a, w = step0(0, w)
    arrived_b = hop(1, state_b[-1])
    arrived_a = hop(0, state_a[-1])
    end_b, mine_b, theirs_b = step1(1, state_b, arrived_b)
    end_a, mine_a, theirs_a = step1(0, state_a, arrived_a, end_b[0])
    keep_b, give_b = scatter(mine_b, theirs_b, BF)
    mirrored = mirror(keep_b)
    crossed = mirror_cross(give_b)
    keep_a, give_a = scatter(mine_a, theirs_a, F32, keep_b)
    near = swap(give_a, "xl")
    outs = [sds((1, 2, TOK, D), BF), sds((8, 128), F32)]
    carry_out, done = call(carry_kernel, outs, [where, w, *end_a, *end_b], 2 * unit)
    outs = [sds((1, *shard), F32), sds((1, 128), F32)]
    gradient, squares = call(gradient_kernel, outs, [where, keep_a, near, mirrored, crossed, done], small)
    squares = jnp.broadcast_to(squares, (NP * NZ * 4, 1, 128))
    square_total = jnp.sum(lax.all_to_all(squares, PIPE + DP, 0, 0, tiled=True))
    clip_limit = math.sqrt(2.0 * NP * D * LATENT)
    clip_scale = jnp.minimum(1.0, clip_limit / jnp.sqrt(square_total + CLIP_EPS))
    clipped = gradient * clip_scale
    new_moment1 = BETA_ONE * moment1 + (1.0 - BETA_ONE) * clipped
    new_moment2 = BETA_TWO * moment2 + (1.0 - BETA_TWO) * clipped * clipped
    update = (
        new_moment1
        / (1.0 - BETA_ONE**ADAM_STEP)
        / (jnp.sqrt(new_moment2 / (1.0 - BETA_TWO**ADAM_STEP)) + ADAM_EPS)
    )
    new_weights = weights - LEARN_RATE * (update + DECAY_RATE * weights)
    return (carry_out, new_weights, new_moment1, new_moment2)


def solution(mesh):
    fine = Mesh(mesh.devices.reshape(2, 4, 8, 2, 2), PIPE + DP)
    rows = P(PIPE, None, DP, None)
    return jax.shard_map(
        local,
        mesh=fine,
        in_specs=(P(PIPE, None, None, DP, None), rows, P(None, None, DP), rows, rows, rows),
        out_specs=(rows, rows, rows, rows),
        check_vma=False,
    )
```

```python
import functools
import math

import jax
import jax.numpy as jnp
from jax import lax
from jax.experimental import pallas as pl
from jax.experimental.pallas import tpu as pltpu
from jax.sharding import Mesh
from jax.sharding import PartitionSpec as P

D = 3584
LATENT = 256
STEPS = 2
ADAM_STEP = 10
TOK = 128
ROWS = 112
NZ = 8
NP = 8
BLOCK = 896
FIRST = (4, 3, 5)
SECOND = (2, 6, 1, 7, 0)
KERNEL_MB = 12

NORM_EPS = 1e-06
BETA_ONE = 0.9
BETA_TWO = 0.95
ADAM_EPS = 1e-08
LEARN_RATE = 0.02
DECAY_RATE = 0.1
CLIP_EPS = 1e-06

SCALES = (D ** (-0.5), LATENT ** (-0.5))
PIPE = ("xh", "y")
DP = ("z", "xl", "core")
BF = jnp.bfloat16
F32 = jnp.float32


def shift(value, axis, by, size):
    return lax.ppermute(value, axis, [(i, (i + by) % size) for i in range(size)])


def swap(value, axis):
    return lax.ppermute(value, axis, [(0, 1), (1, 0)])


def mirror(value):
    return lax.ppermute(value, PIPE, [(i, NP - 1 - i) for i in range(NP)])


def mirror_cross(value):
    pairs = [(i * 2 + a, (NP - 1 - i) * 2 + 1 - a) for i in range(NP) for a in range(2)]
    return lax.ppermute(value, ("xh", "y", "xl"), pairs)


def sds(shape, dtype):
    return jax.ShapeDtypeStruct(shape, dtype)


def call(kernel, out_shape, ins, flops, aliases=None):
    nbytes = sum(math.prod(a.shape) * a.dtype.itemsize for a in list(ins) + list(out_shape))
    vmem = pl.BlockSpec(memory_space=pltpu.VMEM)
    return pl.pallas_call(
        kernel,
        out_shape=out_shape,
        in_specs=[pl.BlockSpec(memory_space=pltpu.SMEM)] + [vmem] * (len(ins) - 1),
        out_specs=[vmem] * len(out_shape),
        input_output_aliases=aliases or {},
        compiler_params=pltpu.CompilerParams(vmem_limit_bytes=KERNEL_MB * 2**20),
        cost_estimate=pl.CostEstimate(flops=flops, bytes_accessed=nbytes, transcendentals=0),
    )(*ins)


def dot(a, b):
    return jnp.dot(a, b, preferred_element_type=F32)


def dot_t(a, b):
    return lax.dot_general(a, b, (((1,), (1,)), ((), ())), preferred_element_type=F32)


def dot_tn(a, b):
    return lax.dot_general(a, b, (((0,), (0,)), ((), ())), preferred_element_type=F32)


def backward(latent, factor, d_norm):
    inner = jnp.mean(d_norm * latent, axis=-1, keepdims=True)
    return (factor * (d_norm - latent * (factor * factor * inner))).astype(BF)


def is_end(where_ref, u):
    return where_ref[2] == (NP - 1 if u == 0 else 0)


def quad_kernel(where_ref, own_ref, mirrored_ref, near_ref, crossed_ref, out_ref):
    xl = where_ref[3]
    out_ref[xl, 0] = own_ref[...]
    out_ref[xl, 1] = mirrored_ref[...]
    out_ref[1 - xl, 0] = near_ref[...]
    out_ref[1 - xl, 1] = crossed_ref[...]


def put(where_ref, w_ref, sections, k, other, block_of):
    core = where_ref[1]
    zz = lax.rem(where_ref[0] + k, NZ)
    for xl in range(2):
        row = zz * 448 + xl * 224 + (1 - core if other else core) * ROWS
        for sec in sections:
            for kind in range(2):
                w_ref[sec, kind, pl.ds(pl.multiple_of(row, 16), ROWS), :] = block_of(xl, sec, kind)


def place_kernel(ks, where_ref, *refs):
    w_ref = refs[-1]
    for i, ref in enumerate(refs[: 2 * len(ks)]):
        put(where_ref, w_ref, (0, 1), ks[i // 2], i % 2, lambda xl, sec, kind: ref[xl, sec, kind])


def step0_kernel(u, where_ref, mask_ref, x_ref, carry_ref, low_ref, low2_ref, high_ref, high2_ref, _, *outs):
    latent_ref, factor_ref, normed_ref, cot_ref, d_lat_ref, out_ref, w_both_ref = outs
    w_ref = w_both_ref.at[u]
    for other, halves in enumerate(((low_ref, high_ref), (low2_ref, high2_ref))):
        put(where_ref, w_both_ref, (u,), 4, other, lambda xl, sec, kind: halves[xl][sec, kind])
    latent = dot(x_ref[0, :, u].reshape(STEPS * TOK, D), w_ref[0])
    factor = lax.rsqrt(jnp.mean(latent * latent, axis=-1, keepdims=True) + NORM_EPS)
    latent_ref[...] = latent
    factor_ref[...] = jnp.broadcast_to(factor, (STEPS * TOK, 128))
    normed_ref[...] = (latent * factor).astype(BF)
    end = is_end(where_ref, u)

    @pl.when(end)
    def _():
        for b in range(D // BLOCK):
            cols = slice(b * BLOCK, (b + 1) * BLOCK)
            out = x_ref[0, 0, u, :, cols].astype(F32) + dot_t(normed_ref[:TOK], w_ref[1, cols])
            cot_ref[:, cols] = (mask_ref[0, u] * out).astype(BF)

    @pl.when(jnp.logical_not(end))
    def _():
        cot_ref[...] = carry_ref[0, u]

    d_norm = dot(cot_ref[...], w_ref[1])
    d_lat_ref[...] = backward(latent_ref[:TOK], factor_ref[:TOK, :1], d_norm)
    for b in range(D // BLOCK):
        cols = slice(b * BLOCK, (b + 1) * BLOCK)
        out = cot_ref[:, cols].astype(F32) + dot_t(d_lat_ref[...], w_ref[0, cols])
        out_ref[:, cols] = out.astype(BF)


def step1_kernel(u, where_ref, mask_ref, x_ref, w_both_ref, latent_ref, factor_ref, normed_ref, cot0_ref, d_lat0_ref,
                 arr_ref, *refs):
    cot_ref, d_lat_ref, mine_ref, other_ref = refs[-4:]
    w_ref = w_both_ref.at[u]
    z = where_ref[0]
    core = where_ref[1]

    def emit(grad, b, kind):
        for i in range(2):
            k = lax.rem(2 * b + i - z + NZ, NZ)
            for xl in range(2):
                base = (i * 4 + xl * 2) * ROWS
                low = grad[base : base + ROWS]
                high = grad[base + ROWS : base + 2 * ROWS]
                mine_ref[k, xl, kind] = jnp.where(core == 0, low, high)
                other_ref[k, xl, kind] = jnp.where(core == 0, high, low)

    end = is_end(where_ref, u)

    @pl.when(end)
    def _():
        for b in range(D // BLOCK):
            cols = slice(b * BLOCK, (b + 1) * BLOCK)
            out = x_ref[0, 1, u, :, cols].astype(F32) + dot_t(normed_ref[TOK:], w_ref[1, cols])
            cot_ref[:, cols] = (mask_ref[1, u] * out).astype(BF)

    @pl.when(jnp.logical_not(end))
    def _():
        cot_ref[...] = arr_ref[...]

    d_norm = dot(cot_ref[...], w_ref[1])
    d_lat = backward(latent_ref[TOK:], factor_ref[TOK:, :1], d_norm)
    d_lat_ref[...] = d_lat
    d_lats = jnp.concatenate([d_lat0_ref[...], d_lat], axis=0)
    for b in range(D // BLOCK):
        cols = slice(b * BLOCK, (b + 1) * BLOCK)
        cots = jnp.concatenate([cot0_ref[:, cols], cot_ref[:, cols]], axis=0)
        emit((dot_tn(cots, normed_ref[...]) * SCALES[1]).astype(BF), b, 1)
        xs = x_ref[0, :, u, :, cols].reshape(STEPS * TOK, BLOCK)
        emit((dot_tn(xs, d_lats) * SCALES[0]).astype(BF), b, 0)


def carry_kernel(where_ref, w_both_ref, *refs):
    out_ref, done_ref = refs[-2:]
    done_ref[...] = jnp.zeros_like(done_ref)
    for u in range(2):
        w_ref = w_both_ref.at[u]
        d_lat_ref, cot_ref = refs[u * 2 : u * 2 + 2]
        for b in range(D // BLOCK):
            cols = slice(b * BLOCK, (b + 1) * BLOCK)
            out = cot_ref[:, cols].astype(F32) + dot_t(d_lat_ref[...], w_ref[0, cols])
            out_ref[0, u, :, cols] = out.astype(BF)


def far_kernel(where_ref, mine_ref, theirs_ref, low_ref, high_ref):
    for xl, ref in enumerate((low_ref, high_ref)):
        ref[...] = (mine_ref[4, xl].astype(F32) + theirs_ref[4, xl].astype(F32)).astype(BF)


def join_kernel(k, where_ref, mine_ref, theirs_ref, ahead_ref, back_ref, ahead_out_ref, back_out_ref):
    sides = ((k, ahead_ref, ahead_out_ref, 0), (NZ - k, back_ref, back_out_ref, 1))
    for place, arrived_ref, out_ref, half in sides:
        for xl in range(2):
            total = mine_ref[place, xl].astype(F32) + theirs_ref[place, xl].astype(F32)
            if k < 3:
                total = total + arrived_ref[xl].astype(F32)
            elif xl == half:
                total = total + arrived_ref[...].astype(F32)
            out_ref[xl] = total.astype(BF)


def last_kernel(where_ref, mine_ref, theirs_ref, ahead_ref, back_ref, keep_ref, give_ref):
    xl = where_ref[3]

    def total(i):
        parts = (mine_ref[0, i], theirs_ref[0, i], ahead_ref[i], back_ref[i])
        return sum(part.astype(F32) for part in parts).astype(BF)

    keep_ref[...] = total(xl)
    give_ref[...] = total(1 - xl)


def give_kernel(ks, where_ref, mine_ref, theirs_ref, *refs):
    out_ref = refs[-1]
    xl = where_ref[3]
    for i, k in enumerate(ks):
        out_ref[i] = (mine_ref[k, 1 - xl].astype(F32) + theirs_ref[k, 1 - xl].astype(F32)).astype(BF)


def pair_terms(where_ref, mine_ref, theirs_ref, given_ref, ks, k, kind):
    xl = where_ref[3]
    parts = (mine_ref[k, xl, kind], theirs_ref[k, xl, kind], given_ref[ks.index(k), kind])
    return sum(part.astype(F32) for part in parts)


def pair_far_kernel(where_ref, mine_ref, theirs_ref, given_ref, *outs):
    for kind, ref in enumerate(outs):
        ref[...] = pair_terms(where_ref, mine_ref, theirs_ref, given_ref, FIRST, 4, kind).astype(BF)


def pair_join_kernel(k, where_ref, mine_ref, theirs_ref, given_ref, ahead_ref, back_ref, ahead_out_ref, back_out_ref):
    ks = FIRST if k == 3 else SECOND
    sides = ((k, ahead_ref, ahead_out_ref, 0), (NZ - k, back_ref, back_out_ref, 1))
    for place, arrived_ref, out_ref, half in sides:
        for kind in range(2):
            total = pair_terms(where_ref, mine_ref, theirs_ref, given_ref, ks, place, kind)
            if k < 3:
                total = total + arrived_ref[kind].astype(F32)
            elif kind == half:
                total = total + arrived_ref[...].astype(F32)
            out_ref[kind] = total.astype(BF)


def gradient_kernel(where_ref, mine_ref, theirs_ref, given_ref, ahead_ref, back_ref, mirrored_ref, crossed_ref, _,
                    out_ref, squares_ref):
    squares = 0.0
    for kind in range(2):
        total = pair_terms(where_ref, mine_ref, theirs_ref, given_ref, SECOND, 0, kind)
        for ref in (ahead_ref, back_ref, mirrored_ref, crossed_ref):
            total = total + ref[kind].astype(F32)
        out_ref[0, kind] = total
        squares = squares + jnp.sum(total * total, axis=0, keepdims=True)
    squares_ref[...] = squares[:, :128] + squares[:, 128:]


def local(section_inputs, carry_in, loss_mask, weights, moment1, moment2):
    where = jnp.stack(
        [lax.axis_index("z"), lax.axis_index("core"), lax.axis_index(PIPE), lax.axis_index("xl")]
    ).astype(jnp.int32)
    multipliers = jnp.array(SCALES, F32).reshape(2, 1, 1)
    own = (weights[0] * multipliers).astype(BF)
    mask = loss_mask.astype(F32)[..., None]
    shard = (2, ROWS, LATENT)
    chunk = sds((2, *shard), BF)
    unit = 2 * TOK * D * LATENT
    small = 1 << 20

    def place(ks, chunks, *held):
        ins = [where]
        for c in chunks:
            ins += [c, swap(c, "core")]
        ins += held
        aliases = {len(ins) - 1: 0} if held else None
        kernel = lambda *refs: place_kernel(ks, *refs)
        return call(kernel, [sds((2, 2, D, LATENT), BF)], ins, 10 * unit, aliases)[0]

    def gather(start):
        w = place((0,), [start])
        ahead = back = start
        for k in range(1, 4):
            ahead = shift(ahead, "z", 1, NZ)
            back = shift(back, "z", -1, NZ)
            held = [section_inputs, carry_in] if k > 1 else []
            w = place((k, NZ - k), [back, ahead], *held, w)
        return w, shift(ahead[0], "z", 1, NZ), shift(back[1], "z", -1, NZ)

    def hop(u, out):
        if u == 0:
            return lax.ppermute(out, PIPE, [(i, i - 1) for i in range(1, NP)])
        return lax.ppermute(out, PIPE, [(i, i + 1) for i in range(NP - 1)])

    def step1(u, state, arrived, *after):
        latent, factor, normed, cot0, d_lat0, _ = state
        terms = sds((NZ, *chunk.shape), BF)
        cot1, d_lat1, mine, other = call(
            lambda *refs: step1_kernel(u, *refs),
            [sds((TOK, D), BF), sds((TOK, LATENT), BF), terms, terms],
            [where, mask, section_inputs, w, latent, factor, normed, cot0, d_lat0, arrived, *after],
            6 * unit,
        )
        return (d_lat1, cot1), mine, swap(other, "core")

    def around(ahead, back):
        return shift(ahead, "z", 1, NZ), shift(back, "z", -1, NZ)

    shards = [where, own, mirror(own), swap(own, "xl"), mirror_cross(own)]
    w, low, high = gather(call(quad_kernel, [sds((2, 2, *shard), BF)], shards, small)[0])
    state = [
        sds((STEPS * TOK, LATENT), F32), sds((STEPS * TOK, 128), F32), sds((STEPS * TOK, LATENT), BF),
        sds((TOK, D), BF), sds((TOK, LATENT), BF), sds((TOK, D), BF),
    ]
    last = [low, swap(low, "core"), high, swap(high, "core")]

    def step0(u, w):
        ins = [where, mask, section_inputs, carry_in, *last, w]
        kernel = lambda *refs: step0_kernel(u, *refs)
        *out, w = call(kernel, state + [sds(w.shape, BF)], ins, 5 * unit, {len(ins) - 1: len(state)})
        return out, w

    state_b, w = step0(1, w)
    state_a, w = step0(0, w)
    arrived_b = hop(1, state_b[-1])
    arrived_a = hop(0, state_a[-1])
    end_b, *both_b = step1(1, state_b, arrived_b)
    end_a, *both_a = step1(0, state_a, arrived_a, end_b[0])
    both_b = [where, *both_b]
    both_a = [where, *both_a]
    one = sds(shard, BF)

    sides = call(far_kernel, [one, one], both_b, small)
    for k in (3, 2, 1):
        sides = call(functools.partial(join_kernel, k), [chunk, chunk], [*both_b, *around(*sides)], small)
    keep, give = call(last_kernel, [one, one], [*both_b, *around(*sides)], small)
    mirrored = mirror(keep)
    crossed = mirror_cross(give)

    def given(ks, *after):
        ins = [*both_a, *after]
        (out,) = call(functools.partial(give_kernel, ks), [sds((len(ks), *shard), BF)], ins, small)
        return swap(out, "xl")

    first = [*both_a, given(FIRST)]
    half = sds((ROWS, LATENT), BF)
    sides = call(pair_far_kernel, [half, half], first, small)
    second = [*both_a, given(SECOND, sides[0])]
    for k in (3, 2, 1):
        ins = [*(first if k == 3 else second), *around(*sides)]
        sides = call(functools.partial(pair_join_kernel, k), [one, one], ins, small)
    outs = [sds((1, 2, TOK, D), BF), sds((8, 128), F32)]
    carry_out, done = call(carry_kernel, outs, [where, w, *end_a, *end_b], 2 * unit)
    outs = [sds((1, *shard), F32), sds((1, 128), F32)]
    ins = [*second, *around(*sides), mirrored, crossed, done]
    gradient, squares = call(gradient_kernel, outs, ins, small)
    squares = jnp.broadcast_to(squares, (NP * NZ * 4, 1, 128))
    square_total = jnp.sum(lax.all_to_all(squares, PIPE + DP, 0, 0, tiled=True))
    clip_limit = math.sqrt(2.0 * NP * D * LATENT)
    clip_scale = jnp.minimum(1.0, clip_limit / jnp.sqrt(square_total + CLIP_EPS))
    clipped = gradient * clip_scale
    new_moment1 = BETA_ONE * moment1 + (1.0 - BETA_ONE) * clipped
    new_moment2 = BETA_TWO * moment2 + (1.0 - BETA_TWO) * clipped * clipped
    update = (
        new_moment1
        / (1.0 - BETA_ONE**ADAM_STEP)
        / (jnp.sqrt(new_moment2 / (1.0 - BETA_TWO**ADAM_STEP)) + ADAM_EPS)
    )
    new_weights = weights - LEARN_RATE * (update + DECAY_RATE * weights)
    return (carry_out, new_weights, new_moment1, new_moment2)


def solution(mesh):
    fine = Mesh(mesh.devices.reshape(2, 4, 8, 2, 2), PIPE + DP)
    rows = P(PIPE, None, DP, None)
    return jax.shard_map(
        local,
        mesh=fine,
        in_specs=(P(PIPE, None, None, DP, None), rows, P(None, None, DP), rows, rows, rows),
        out_specs=(rows, rows, rows, rows),
        check_vma=False,
    )
```

```python
import functools
import math

import jax
import jax.numpy as jnp
from jax import lax
from jax.experimental import pallas as pl
from jax.experimental.pallas import tpu as pltpu
from jax.sharding import Mesh
from jax.sharding import PartitionSpec as P

D = 3584
LATENT = 256
STEPS = 2
ADAM_STEP = 10
TOK = 128
ROWS = 112
NZ = 8
NP = 8
BLOCK = 896
KERNEL_MB = 12

NORM_EPS = 1e-06
BETA_ONE = 0.9
BETA_TWO = 0.95
ADAM_EPS = 1e-08
LEARN_RATE = 0.02
DECAY_RATE = 0.1
CLIP_EPS = 1e-06

SCALES = (D ** (-0.5), LATENT ** (-0.5))
PIPE = ("xh", "y")
DP = ("z", "xl", "core")
BF = jnp.bfloat16
F32 = jnp.float32


def shift(value, axis, by, size):
    return lax.ppermute(value, axis, [(i, (i + by) % size) for i in range(size)])


def swap(value, axis):
    return lax.ppermute(value, axis, [(0, 1), (1, 0)])


def mirror(value):
    return lax.ppermute(value, PIPE, [(i, NP - 1 - i) for i in range(NP)])


def mirror_cross(value):
    pairs = [(i * 2 + a, (NP - 1 - i) * 2 + 1 - a) for i in range(NP) for a in range(2)]
    return lax.ppermute(value, ("xh", "y", "xl"), pairs)


def sds(shape, dtype):
    return jax.ShapeDtypeStruct(shape, dtype)


def call(kernel, out_shape, ins, flops, aliases=None):
    nbytes = sum(math.prod(a.shape) * a.dtype.itemsize for a in list(ins) + list(out_shape))
    vmem = pl.BlockSpec(memory_space=pltpu.VMEM)
    return pl.pallas_call(
        kernel,
        out_shape=out_shape,
        in_specs=[pl.BlockSpec(memory_space=pltpu.SMEM)] + [vmem] * (len(ins) - 1),
        out_specs=[vmem] * len(out_shape),
        input_output_aliases=aliases or {},
        compiler_params=pltpu.CompilerParams(vmem_limit_bytes=KERNEL_MB * 2**20),
        cost_estimate=pl.CostEstimate(flops=flops, bytes_accessed=nbytes, transcendentals=0),
    )(*ins)


def dot(a, b):
    return jnp.dot(a, b, preferred_element_type=F32)


def dot_t(a, b):
    return lax.dot_general(a, b, (((1,), (1,)), ((), ())), preferred_element_type=F32)


def dot_tn(a, b):
    return lax.dot_general(a, b, (((0,), (0,)), ((), ())), preferred_element_type=F32)


def backward(latent, factor, d_norm):
    inner = jnp.mean(d_norm * latent, axis=-1, keepdims=True)
    return (factor * (d_norm - latent * (factor * factor * inner))).astype(BF)


def is_end(where_ref, u):
    return where_ref[2] == (NP - 1 if u == 0 else 0)


def quad_kernel(where_ref, own_ref, mirrored_ref, near_ref, crossed_ref, out_ref):
    xl = where_ref[3]
    out_ref[xl, 0] = own_ref[...]
    out_ref[xl, 1] = mirrored_ref[...]
    out_ref[1 - xl, 0] = near_ref[...]
    out_ref[1 - xl, 1] = crossed_ref[...]


def put(where_ref, w_ref, sections, k, other, block_of):
    core = where_ref[1]
    zz = lax.rem(where_ref[0] + k, NZ)
    for xl in range(2):
        row = zz * 448 + xl * 224 + (1 - core if other else core) * ROWS
        for sec in sections:
            for kind in range(2):
                w_ref[sec, kind, pl.ds(pl.multiple_of(row, 16), ROWS), :] = block_of(xl, sec, kind)


def place_kernel(ks, where_ref, *refs):
    w_ref = refs[-1]
    for i, ref in enumerate(refs[: 2 * len(ks)]):
        put(where_ref, w_ref, (0, 1), ks[i // 2], i % 2, lambda xl, sec, kind: ref[xl, sec, kind])


def step0_kernel(where_ref, mask_ref, x_ref, carry_ref, low_ref, low2_ref, high_ref, high2_ref, _, *outs):
    w_both_ref = outs[-1]
    for u in (1, 0):
        latent_ref, factor_ref, normed_ref, cot_ref, d_lat_ref, out_ref = outs[u * 6 : u * 6 + 6]
        w_ref = w_both_ref.at[u]
        for other, halves in enumerate(((low_ref, high_ref), (low2_ref, high2_ref))):
            put(where_ref, w_both_ref, (u,), 4, other, lambda xl, sec, kind: halves[xl][sec, kind])
        latent = dot(x_ref[0, :, u].reshape(STEPS * TOK, D), w_ref[0])
        factor = lax.rsqrt(jnp.mean(latent * latent, axis=-1, keepdims=True) + NORM_EPS)
        latent_ref[...] = latent
        factor_ref[...] = jnp.broadcast_to(factor, (STEPS * TOK, 128))
        normed_ref[...] = (latent * factor).astype(BF)
        end = is_end(where_ref, u)

        @pl.when(end)
        def _():
            for b in range(D // BLOCK):
                cols = slice(b * BLOCK, (b + 1) * BLOCK)
                out = x_ref[0, 0, u, :, cols].astype(F32) + dot_t(normed_ref[:TOK], w_ref[1, cols])
                cot_ref[:, cols] = (mask_ref[0, u] * out).astype(BF)

        @pl.when(jnp.logical_not(end))
        def _():
            cot_ref[...] = carry_ref[0, u]

        d_norm = dot(cot_ref[...], w_ref[1])
        d_lat_ref[...] = backward(latent_ref[:TOK], factor_ref[:TOK, :1], d_norm)
        for b in range(D // BLOCK):
            cols = slice(b * BLOCK, (b + 1) * BLOCK)
            out = cot_ref[:, cols].astype(F32) + dot_t(d_lat_ref[...], w_ref[0, cols])
            out_ref[:, cols] = out.astype(BF)


def step1_kernel(u, where_ref, mask_ref, x_ref, w_both_ref, latent_ref, factor_ref, normed_ref, cot0_ref, d_lat0_ref,
                 arr_ref, *refs):
    cot_ref, d_lat_ref, mine_ref, other_ref = refs[-4:]
    w_ref = w_both_ref.at[u]
    z = where_ref[0]
    core = where_ref[1]

    def emit(grad, b, kind):
        for i in range(2):
            k = lax.rem(2 * b + i - z + NZ, NZ)
            for xl in range(2):
                base = (i * 4 + xl * 2) * ROWS
                low = grad[base : base + ROWS]
                high = grad[base + ROWS : base + 2 * ROWS]
                mine_ref[k, xl, kind] = jnp.where(core == 0, low, high)
                other_ref[k, xl, kind] = jnp.where(core == 0, high, low)

    end = is_end(where_ref, u)

    @pl.when(end)
    def _():
        for b in range(D // BLOCK):
            cols = slice(b * BLOCK, (b + 1) * BLOCK)
            out = x_ref[0, 1, u, :, cols].astype(F32) + dot_t(normed_ref[TOK:], w_ref[1, cols])
            cot_ref[:, cols] = (mask_ref[1, u] * out).astype(BF)

    @pl.when(jnp.logical_not(end))
    def _():
        cot_ref[...] = arr_ref[...]

    d_norm = dot(cot_ref[...], w_ref[1])
    d_lat = backward(latent_ref[TOK:], factor_ref[TOK:, :1], d_norm)
    d_lat_ref[...] = d_lat
    d_lats = jnp.concatenate([d_lat0_ref[...], d_lat], axis=0)
    for b in range(D // BLOCK):
        cols = slice(b * BLOCK, (b + 1) * BLOCK)
        cots = jnp.concatenate([cot0_ref[:, cols], cot_ref[:, cols]], axis=0)
        emit((dot_tn(cots, normed_ref[...]) * SCALES[1]).astype(BF), b, 1)
        xs = x_ref[0, :, u, :, cols].reshape(STEPS * TOK, BLOCK)
        emit((dot_tn(xs, d_lats) * SCALES[0]).astype(BF), b, 0)


def carry_kernel(where_ref, w_both_ref, *refs):
    out_ref, done_ref = refs[-2:]
    done_ref[...] = jnp.zeros_like(done_ref)
    for u in range(2):
        w_ref = w_both_ref.at[u]
        d_lat_ref, cot_ref = refs[u * 2 : u * 2 + 2]
        for b in range(D // BLOCK):
            cols = slice(b * BLOCK, (b + 1) * BLOCK)
            out = cot_ref[:, cols].astype(F32) + dot_t(d_lat_ref[...], w_ref[0, cols])
            out_ref[0, u, :, cols] = out.astype(BF)


def far_kernel(where_ref, mine_ref, theirs_ref, low_ref, high_ref):
    for xl, ref in enumerate((low_ref, high_ref)):
        ref[...] = (mine_ref[4, xl].astype(F32) + theirs_ref[4, xl].astype(F32)).astype(BF)


def join_kernel(k, where_ref, mine_ref, theirs_ref, ahead_ref, back_ref, ahead_out_ref, back_out_ref):
    sides = ((k, ahead_ref, ahead_out_ref, 0), (NZ - k, back_ref, back_out_ref, 1))
    for place, arrived_ref, out_ref, half in sides:
        for xl in range(2):
            total = mine_ref[place, xl].astype(F32) + theirs_ref[place, xl].astype(F32)
            if k < 3:
                total = total + arrived_ref[xl].astype(F32)
            elif xl == half:
                total = total + arrived_ref[...].astype(F32)
            out_ref[xl] = total.astype(BF)


def last_kernel(where_ref, mine_ref, theirs_ref, ahead_ref, back_ref, *refs):
    keep_ref, give_ref = refs[-2:]
    xl = where_ref[3]

    def total(i):
        parts = (mine_ref[0, i], theirs_ref[0, i], ahead_ref[i], back_ref[i])
        return sum(part.astype(F32) for part in parts)

    keep_ref[...] = total(xl).astype(keep_ref.dtype)
    give_ref[...] = total(1 - xl).astype(BF)


def gradient_kernel(where_ref, keep_ref, near_ref, mirrored_ref, crossed_ref, _, out_ref, squares_ref):
    total = keep_ref[...] + near_ref[...].astype(F32) + mirrored_ref[...].astype(F32) + crossed_ref[...].astype(F32)
    out_ref[0] = total
    squares = jnp.sum((total * total).reshape(2 * ROWS, LATENT), axis=0, keepdims=True)
    squares_ref[...] = squares[:, :128] + squares[:, 128:]


def update_kernel(where_ref, squares_ref, gradient_ref, weights_ref, moment1_ref, moment2_ref, new_weights_ref,
                  new_moment1_ref, new_moment2_ref):
    square_total = jnp.sum(jnp.sum(squares_ref[...], axis=0), axis=-1, keepdims=True)
    clip_limit = math.sqrt(2.0 * NP * D * LATENT)
    clip_scale = jnp.minimum(1.0, clip_limit / jnp.sqrt(square_total + CLIP_EPS))
    for kind in range(2):
        clipped = gradient_ref[0, kind] * clip_scale
        moment1 = BETA_ONE * moment1_ref[0, kind] + (1.0 - BETA_ONE) * clipped
        moment2 = BETA_TWO * moment2_ref[0, kind] + (1.0 - BETA_TWO) * clipped * clipped
        root = jnp.sqrt(moment2 / (1.0 - BETA_TWO**ADAM_STEP)) + ADAM_EPS
        update = moment1 / (1.0 - BETA_ONE**ADAM_STEP) / root
        new_moment1_ref[0, kind] = moment1
        new_moment2_ref[0, kind] = moment2
        new_weights_ref[0, kind] = weights_ref[0, kind] - LEARN_RATE * (update + DECAY_RATE * weights_ref[0, kind])


def local(section_inputs, carry_in, loss_mask, weights, moment1, moment2):
    where = jnp.stack(
        [lax.axis_index("z"), lax.axis_index("core"), lax.axis_index(PIPE), lax.axis_index("xl")]
    ).astype(jnp.int32)
    multipliers = jnp.array(SCALES, F32).reshape(2, 1, 1)
    own = (weights[0] * multipliers).astype(BF)
    mask = loss_mask.astype(F32)[..., None]
    shard = (2, ROWS, LATENT)
    chunk = sds((2, *shard), BF)
    unit = 2 * TOK * D * LATENT
    small = 1 << 20

    def place(ks, chunks, *held):
        ins = [where]
        for c in chunks:
            ins += [c, swap(c, "core")]
        ins += held
        aliases = {len(ins) - 1: 0} if held else None
        kernel = lambda *refs: place_kernel(ks, *refs)
        return call(kernel, [sds((2, 2, D, LATENT), BF)], ins, 10 * unit, aliases)[0]

    def gather(start):
        w = place((0,), [start])
        ahead = back = start
        for k in range(1, 4):
            ahead = shift(ahead, "z", 1, NZ)
            back = shift(back, "z", -1, NZ)
            held = [section_inputs, carry_in] if k > 1 else []
            w = place((k, NZ - k), [back, ahead], *held, w)
        return w, shift(ahead[0], "z", 1, NZ), shift(back[1], "z", -1, NZ)

    def hop(u, out):
        if u == 0:
            return lax.ppermute(out, PIPE, [(i, i - 1) for i in range(1, NP)])
        return lax.ppermute(out, PIPE, [(i, i + 1) for i in range(NP - 1)])

    def step1(u, state, arrived, *after):
        latent, factor, normed, cot0, d_lat0, _ = state
        terms = sds((NZ, *chunk.shape), BF)
        cot1, d_lat1, mine, other = call(
            lambda *refs: step1_kernel(u, *refs),
            [sds((TOK, D), BF), sds((TOK, LATENT), BF), terms, terms],
            [where, mask, section_inputs, w, latent, factor, normed, cot0, d_lat0, arrived, *after],
            6 * unit,
        )
        return (d_lat1, cot1), mine, swap(other, "core")

    def scatter(mine, theirs, keep_type, *after):
        both = [where, mine, theirs]

        ahead, back = call(far_kernel, [sds(shard, BF), sds(shard, BF)], both, small)
        for k in (3, 2, 1):
            ins = [*both, shift(ahead, "z", 1, NZ), shift(back, "z", -1, NZ)]
            ahead, back = call(functools.partial(join_kernel, k), [chunk, chunk], ins, small)
        ahead = shift(ahead, "z", 1, NZ)
        back = shift(back, "z", -1, NZ)
        parts = [*both, ahead, back, *after]
        keep, give = call(last_kernel, [sds(shard, keep_type), sds(shard, BF)], parts, small)
        return keep, give

    shards = [where, own, mirror(own), swap(own, "xl"), mirror_cross(own)]
    w, low, high = gather(call(quad_kernel, [sds((2, 2, *shard), BF)], shards, small)[0])
    state = [
        sds((STEPS * TOK, LATENT), F32), sds((STEPS * TOK, 128), F32), sds((STEPS * TOK, LATENT), BF),
        sds((TOK, D), BF), sds((TOK, LATENT), BF), sds((TOK, D), BF),
    ]
    ins = [where, mask, section_inputs, carry_in, low, swap(low, "core"), high, swap(high, "core"), w]
    *states, w = call(step0_kernel, state * 2 + [sds(w.shape, BF)], ins, 10 * unit, {len(ins) - 1: 12})
    state_a, state_b = states[:6], states[6:]
    arrived_b = hop(1, state_b[-1])
    arrived_a = hop(0, state_a[-1])
    end_b, mine_b, theirs_b = step1(1, state_b, arrived_b)
    end_a, mine_a, theirs_a = step1(0, state_a, arrived_a, end_b[0])
    keep_b, give_b = scatter(mine_b, theirs_b, BF)
    mirrored = mirror(keep_b)
    crossed = mirror_cross(give_b)
    keep_a, give_a = scatter(mine_a, theirs_a, F32, keep_b)
    near = swap(give_a, "xl")
    outs = [sds((1, 2, TOK, D), BF), sds((8, 128), F32)]
    carry_out, done = call(carry_kernel, outs, [where, w, *end_a, *end_b], 2 * unit)
    outs = [sds((1, *shard), F32), sds((1, 128), F32)]
    gradient, squares = call(gradient_kernel, outs, [where, keep_a, near, mirrored, crossed, done], small)
    squares = jnp.broadcast_to(squares, (NP * NZ * 4, 1, 128))
    squares = lax.all_to_all(squares, PIPE + DP, 0, 0, tiled=True)
    owned = sds(weights.shape, F32)
    ins = [where, squares, gradient, weights, moment1, moment2]
    return (carry_out, *call(update_kernel, [owned, owned, owned], ins, small))


def solution(mesh):
    fine = Mesh(mesh.devices.reshape(2, 4, 8, 2, 2), PIPE + DP)
    rows = P(PIPE, None, DP, None)
    return jax.shard_map(
        local,
        mesh=fine,
        in_specs=(P(PIPE, None, None, DP, None), rows, P(None, None, DP), rows, rows, rows),
        out_specs=(rows, rows, rows, rows),
        check_vma=False,
    )
```

```python
import functools
import math

import jax
import jax.numpy as jnp
from jax import lax
from jax.experimental import pallas as pl
from jax.experimental.pallas import tpu as pltpu
from jax.sharding import Mesh
from jax.sharding import PartitionSpec as P

D = 3584
LATENT = 256
STEPS = 2
ADAM_STEP = 10
TOK = 128
ROWS = 112
NZ = 8
NP = 8
BLOCK = 896
KERNEL_MB = 12

NORM_EPS = 1e-06
BETA_ONE = 0.9
BETA_TWO = 0.95
ADAM_EPS = 1e-08
LEARN_RATE = 0.02
DECAY_RATE = 0.1
CLIP_EPS = 1e-06

SCALES = (D ** (-0.5), LATENT ** (-0.5))
PIPE = ("xh", "y")
DP = ("z", "xl", "core")
BF = jnp.bfloat16
F32 = jnp.float32


def shift(value, axis, by, size):
    return lax.ppermute(value, axis, [(i, (i + by) % size) for i in range(size)])


def swap(value, axis):
    return lax.ppermute(value, axis, [(0, 1), (1, 0)])


def mirror(value):
    return lax.ppermute(value, PIPE, [(i, NP - 1 - i) for i in range(NP)])


def mirror_cross(value):
    pairs = [(i * 2 + a, (NP - 1 - i) * 2 + 1 - a) for i in range(NP) for a in range(2)]
    return lax.ppermute(value, ("xh", "y", "xl"), pairs)


def sds(shape, dtype):
    return jax.ShapeDtypeStruct(shape, dtype)


def call(kernel, out_shape, ins, flops, aliases=None, nbytes=None):
    nbytes = nbytes or sum(math.prod(a.shape) * a.dtype.itemsize for a in list(ins) + list(out_shape))
    vmem = pl.BlockSpec(memory_space=pltpu.VMEM)
    return pl.pallas_call(
        kernel,
        out_shape=out_shape,
        in_specs=[pl.BlockSpec(memory_space=pltpu.SMEM)] + [vmem] * (len(ins) - 1),
        out_specs=[vmem] * len(out_shape),
        input_output_aliases=aliases or {},
        compiler_params=pltpu.CompilerParams(vmem_limit_bytes=KERNEL_MB * 2**20),
        cost_estimate=pl.CostEstimate(flops=flops, bytes_accessed=nbytes, transcendentals=0),
    )(*ins)


def dot(a, b):
    return jnp.dot(a, b, preferred_element_type=F32)


def dot_t(a, b):
    return lax.dot_general(a, b, (((1,), (1,)), ((), ())), preferred_element_type=F32)


def dot_tn(a, b):
    return lax.dot_general(a, b, (((0,), (0,)), ((), ())), preferred_element_type=F32)


def backward(latent, factor, d_norm):
    inner = jnp.mean(d_norm * latent, axis=-1, keepdims=True)
    return (factor * (d_norm - latent * (factor * factor * inner))).astype(BF)


def is_end(where_ref, u):
    return where_ref[2] == (NP - 1 if u == 0 else 0)


def quad_kernel(where_ref, own_ref, mirrored_ref, near_ref, crossed_ref, out_ref):
    xl = where_ref[3]
    out_ref[xl, 0] = own_ref[...]
    out_ref[xl, 1] = mirrored_ref[...]
    out_ref[1 - xl, 0] = near_ref[...]
    out_ref[1 - xl, 1] = crossed_ref[...]


def put(where_ref, w_ref, sections, k, other, block_of):
    core = where_ref[1]
    zz = lax.rem(where_ref[0] + k, NZ)
    for xl in range(2):
        row = zz * 448 + xl * 224 + (1 - core if other else core) * ROWS
        for sec in sections:
            for kind in range(2):
                w_ref[sec, kind, pl.ds(pl.multiple_of(row, 16), ROWS), :] = block_of(xl, sec, kind)


def halves_kernel(where_ref, ahead_ref, back_ref, _, __, low_ref, high_ref):
    low_ref[...] = ahead_ref[0]
    high_ref[...] = back_ref[1]


def place_kernel(ks, where_ref, *refs):
    w_ref = refs[-1]
    for i, ref in enumerate(refs[: 2 * len(ks)]):
        put(where_ref, w_ref, (0, 1), ks[i // 2], i % 2, lambda xl, sec, kind: ref[xl, sec, kind])


def step0_kernel(u, where_ref, mask_ref, x_ref, carry_ref, low_ref, low2_ref, high_ref, high2_ref, _, *outs):
    latent_ref, factor_ref, normed_ref, cot_ref, d_lat_ref, out_ref, w_both_ref = outs
    w_ref = w_both_ref.at[u]
    for other, halves in enumerate(((low_ref, high_ref), (low2_ref, high2_ref))):
        put(where_ref, w_both_ref, (u,), 4, other, lambda xl, sec, kind: halves[xl][sec, kind])
    latent = dot(x_ref[0, :, u].reshape(STEPS * TOK, D), w_ref[0])
    factor = lax.rsqrt(jnp.mean(latent * latent, axis=-1, keepdims=True) + NORM_EPS)
    latent_ref[...] = latent
    factor_ref[...] = jnp.broadcast_to(factor, (STEPS * TOK, 128))
    normed_ref[...] = (latent * factor).astype(BF)
    end = is_end(where_ref, u)

    @pl.when(end)
    def _():
        for b in range(D // BLOCK):
            cols = slice(b * BLOCK, (b + 1) * BLOCK)
            out = x_ref[0, 0, u, :, cols].astype(F32) + dot_t(normed_ref[:TOK], w_ref[1, cols])
            cot_ref[:, cols] = (mask_ref[0, u] * out).astype(BF)

    @pl.when(jnp.logical_not(end))
    def _():
        cot_ref[...] = carry_ref[0, u]

    d_norm = dot(cot_ref[...], w_ref[1])
    d_lat_ref[...] = backward(latent_ref[:TOK], factor_ref[:TOK, :1], d_norm)
    for b in range(D // BLOCK):
        cols = slice(b * BLOCK, (b + 1) * BLOCK)
        out = cot_ref[:, cols].astype(F32) + dot_t(d_lat_ref[...], w_ref[0, cols])
        out_ref[:, cols] = out.astype(BF)


def step1_kernel(u, where_ref, mask_ref, x_ref, w_both_ref, latent_ref, factor_ref, normed_ref, cot0_ref, d_lat0_ref,
                 arr_ref, *refs):
    cot_ref, d_lat_ref, mine_ref, other_ref = refs[-4:]
    w_ref = w_both_ref.at[u]
    z = where_ref[0]
    core = where_ref[1]

    def emit(grad, b, kind):
        for i in range(2):
            k = lax.rem(2 * b + i - z + NZ, NZ)
            for xl in range(2):
                base = (i * 4 + xl * 2) * ROWS
                low = grad[base : base + ROWS]
                high = grad[base + ROWS : base + 2 * ROWS]
                mine_ref[k, xl, kind] = jnp.where(core == 0, low, high)
                other_ref[k, xl, kind] = jnp.where(core == 0, high, low)

    end = is_end(where_ref, u)

    @pl.when(end)
    def _():
        for b in range(D // BLOCK):
            cols = slice(b * BLOCK, (b + 1) * BLOCK)
            out = x_ref[0, 1, u, :, cols].astype(F32) + dot_t(normed_ref[TOK:], w_ref[1, cols])
            cot_ref[:, cols] = (mask_ref[1, u] * out).astype(BF)

    @pl.when(jnp.logical_not(end))
    def _():
        cot_ref[...] = arr_ref[...]

    d_norm = dot(cot_ref[...], w_ref[1])
    d_lat = backward(latent_ref[TOK:], factor_ref[TOK:, :1], d_norm)
    d_lat_ref[...] = d_lat
    d_lats = jnp.concatenate([d_lat0_ref[...], d_lat], axis=0)
    for b in range(D // BLOCK):
        cols = slice(b * BLOCK, (b + 1) * BLOCK)
        cots = jnp.concatenate([cot0_ref[:, cols], cot_ref[:, cols]], axis=0)
        emit((dot_tn(cots, normed_ref[...]) * SCALES[1]).astype(BF), b, 1)
        xs = x_ref[0, :, u, :, cols].reshape(STEPS * TOK, BLOCK)
        emit((dot_tn(xs, d_lats) * SCALES[0]).astype(BF), b, 0)


def carry_kernel(where_ref, w_both_ref, *refs):
    out_ref, done_ref = refs[-2:]
    done_ref[...] = jnp.zeros_like(done_ref)
    for u in range(2):
        w_ref = w_both_ref.at[u]
        d_lat_ref, cot_ref = refs[u * 2 : u * 2 + 2]
        for b in range(D // BLOCK):
            cols = slice(b * BLOCK, (b + 1) * BLOCK)
            out = cot_ref[:, cols].astype(F32) + dot_t(d_lat_ref[...], w_ref[0, cols])
            out_ref[0, u, :, cols] = out.astype(BF)


def far_kernel(where_ref, mine_ref, theirs_ref, low_ref, high_ref):
    for xl, ref in enumerate((low_ref, high_ref)):
        ref[...] = (mine_ref[4, xl].astype(F32) + theirs_ref[4, xl].astype(F32)).astype(BF)


def join_kernel(k, where_ref, mine_ref, theirs_ref, ahead_ref, back_ref, ahead_out_ref, back_out_ref):
    sides = ((k, ahead_ref, ahead_out_ref, 0), (NZ - k, back_ref, back_out_ref, 1))
    for place, arrived_ref, out_ref, half in sides:
        for xl in range(2):
            total = mine_ref[place, xl].astype(F32) + theirs_ref[place, xl].astype(F32)
            if k < 3:
                total = total + arrived_ref[xl].astype(F32)
            elif xl == half:
                total = total + arrived_ref[...].astype(F32)
            out_ref[xl] = total.astype(BF)


def last_kernel(where_ref, mine_ref, theirs_ref, ahead_ref, back_ref, *refs):
    keep_ref, give_ref = refs[-2:]
    xl = where_ref[3]

    def total(i):
        parts = (mine_ref[0, i], theirs_ref[0, i], ahead_ref[i], back_ref[i])
        return sum(part.astype(F32) for part in parts)

    keep_ref[...] = total(xl).astype(keep_ref.dtype)
    give_ref[...] = total(1 - xl).astype(BF)


def meet_kernel(where_ref, keep_ref, near_ref, out_ref):
    out_ref[...] = (keep_ref[...].astype(F32) + near_ref[...].astype(F32)).astype(BF)


def gradient_kernel(where_ref, keep_ref, near_ref, mirrored_ref, _, out_ref, squares_ref):
    total = keep_ref[...] + near_ref[...].astype(F32) + mirrored_ref[...].astype(F32)
    out_ref[0] = total
    squares = jnp.sum((total * total).reshape(2 * ROWS, LATENT), axis=0, keepdims=True)
    squares_ref[...] = squares[:, :128] + squares[:, 128:]


def update_kernel(where_ref, squares_ref, gradient_ref, weights_ref, moment1_ref, moment2_ref, new_weights_ref,
                  new_moment1_ref, new_moment2_ref):
    square_total = jnp.sum(jnp.sum(squares_ref[...], axis=0), axis=-1, keepdims=True)
    clip_limit = math.sqrt(2.0 * NP * D * LATENT)
    clip_scale = jnp.minimum(1.0, clip_limit / jnp.sqrt(square_total + CLIP_EPS))
    for kind in range(2):
        clipped = gradient_ref[0, kind] * clip_scale
        moment1 = BETA_ONE * moment1_ref[0, kind] + (1.0 - BETA_ONE) * clipped
        moment2 = BETA_TWO * moment2_ref[0, kind] + (1.0 - BETA_TWO) * clipped * clipped
        root = jnp.sqrt(moment2 / (1.0 - BETA_TWO**ADAM_STEP)) + ADAM_EPS
        update = moment1 / (1.0 - BETA_ONE**ADAM_STEP) / root
        new_moment1_ref[0, kind] = moment1
        new_moment2_ref[0, kind] = moment2
        new_weights_ref[0, kind] = weights_ref[0, kind] - LEARN_RATE * (update + DECAY_RATE * weights_ref[0, kind])


def local(section_inputs, carry_in, loss_mask, weights, moment1, moment2):
    where = jnp.stack(
        [lax.axis_index("z"), lax.axis_index("core"), lax.axis_index(PIPE), lax.axis_index("xl")]
    ).astype(jnp.int32)
    multipliers = jnp.array(SCALES, F32).reshape(2, 1, 1)
    own = (weights[0] * multipliers).astype(BF)
    mask = loss_mask.astype(F32)[..., None]
    shard = (2, ROWS, LATENT)
    chunk = sds((2, *shard), BF)
    unit = 2 * TOK * D * LATENT
    small = 1 << 20

    def place(ks, chunks, *held):
        ins = [where]
        for pair in chunks:
            ins += pair
        ins += held
        aliases = {len(ins) - 1: 0} if held else None
        kernel = lambda *refs: place_kernel(ks, *refs)
        return call(kernel, [sds((2, 2, D, LATENT), BF)], ins, 10 * unit, aliases)[0]

    def gather(start):
        ahead, back = [start], [start]
        for _ in range(3):
            ahead.append(shift(ahead[-1], "z", 1, NZ))
            back.append(shift(back[-1], "z", -1, NZ))
        swapped = [[swap(back[k], "core"), swap(ahead[k], "core")] for k in range(4)]
        ins = [where, ahead[3], back[3], *swapped[2]]
        low, high = call(halves_kernel, [sds(start.shape[1:], BF)] * 2, ins, small)
        w = place((0,), [(start, swapped[0][0])])
        w = place((1, 7), list(zip((back[1], ahead[1]), swapped[1])), w)
        held = [section_inputs, carry_in]
        w = place((2, 6), list(zip((back[2], ahead[2]), swapped[2])), *held, w)
        w = place((3, 5), list(zip((back[3], ahead[3]), swapped[3])), *held, w)
        return w, shift(low, "z", 1, NZ), shift(high, "z", -1, NZ)

    def hop(u, out):
        if u == 0:
            return lax.ppermute(out, PIPE, [(i, i - 1) for i in range(1, NP)])
        return lax.ppermute(out, PIPE, [(i, i + 1) for i in range(NP - 1)])

    def step1(u, state, arrived, *after):
        latent, factor, normed, cot0, d_lat0, _ = state
        terms = sds((NZ, *chunk.shape), BF)
        cot1, d_lat1, mine, other = call(
            lambda *refs: step1_kernel(u, *refs),
            [sds((TOK, D), BF), sds((TOK, LATENT), BF), terms, terms],
            [where, mask, section_inputs, w, latent, factor, normed, cot0, d_lat0, arrived, *after],
            6 * unit,
        )
        return (d_lat1, cot1), mine, swap(other, "core")

    def scatter(mine, theirs, keep_type, *after):
        both = [where, mine, theirs]

        ahead, back = call(far_kernel, [sds(shard, BF), sds(shard, BF)], both, small)
        for k in (3, 2, 1):
            ins = [*both, shift(ahead, "z", 1, NZ), shift(back, "z", -1, NZ)]
            ahead, back = call(functools.partial(join_kernel, k), [chunk, chunk], ins, small)
        ahead = shift(ahead, "z", 1, NZ)
        back = shift(back, "z", -1, NZ)
        parts = [*both, ahead, back, *after]
        keep, give = call(last_kernel, [sds(shard, keep_type), sds(shard, BF)], parts, small)
        return keep, give

    shards = [where, own, mirror(own), swap(own, "xl"), mirror_cross(own)]
    w, low, high = gather(call(quad_kernel, [sds((2, 2, *shard), BF)], shards, small)[0])
    state = [
        sds((STEPS * TOK, LATENT), F32), sds((STEPS * TOK, 128), F32), sds((STEPS * TOK, LATENT), BF),
        sds((TOK, D), BF), sds((TOK, LATENT), BF), sds((TOK, D), BF),
    ]
    last = [low, swap(low, "core"), high, swap(high, "core")]

    def step0(u, w):
        ins = [where, mask, section_inputs, carry_in, *last, w]
        kernel = lambda *refs: step0_kernel(u, *refs)
        *out, w = call(kernel, state + [sds(w.shape, BF)], ins, 5 * unit, {len(ins) - 1: len(state)})
        return out, w

    state_b, w = step0(1, w)
    state_a, w = step0(0, w)
    arrived_b = hop(1, state_b[-1])
    arrived_a = hop(0, state_a[-1])
    end_b, mine_b, theirs_b = step1(1, state_b, arrived_b)
    end_a, mine_a, theirs_a = step1(0, state_a, arrived_a, end_b[0])
    keep_b, give_b = scatter(mine_b, theirs_b, BF)
    (whole_b,) = call(meet_kernel, [sds(shard, BF)], [where, keep_b, swap(give_b, "xl")], small)
    mirrored = mirror(whole_b)
    keep_a, give_a = scatter(mine_a, theirs_a, F32, whole_b)
    near = swap(give_a, "xl")
    outs = [sds((1, 2, TOK, D), BF), sds((8, 128), F32)]
    carry_out, done = call(carry_kernel, outs, [where, w, *end_a, *end_b], small, nbytes=small)
    outs = [sds((1, *shard), F32), sds((1, 128), F32)]
    gradient, squares = call(gradient_kernel, outs, [where, keep_a, near, mirrored, done], small)
    squares = jnp.broadcast_to(squares, (NP * NZ * 4, 1, 128))
    squares = lax.all_to_all(squares, PIPE + DP, 0, 0, tiled=True)
    owned = sds(weights.shape, F32)
    ins = [where, squares, gradient, weights, moment1, moment2]
    return (carry_out, *call(update_kernel, [owned, owned, owned], ins, small))


def solution(mesh):
    fine = Mesh(mesh.devices.reshape(2, 4, 8, 2, 2), PIPE + DP)
    rows = P(PIPE, None, DP, None)
    return jax.shard_map(
        local,
        mesh=fine,
        in_specs=(P(PIPE, None, None, DP, None), rows, P(None, None, DP), rows, rows, rows),
        out_specs=(rows, rows, rows, rows),
        check_vma=False,
    )
```

```python
import functools
import math

import jax
import jax.numpy as jnp
from jax import lax
from jax.experimental import pallas as pl
from jax.experimental.pallas import tpu as pltpu
from jax.sharding import Mesh
from jax.sharding import PartitionSpec as P

D = 3584
LATENT = 256
STEPS = 2
ADAM_STEP = 10
TOK = 128
ROWS = 112
NZ = 8
NP = 8
BLOCK = 896
KERNEL_MB = 12

NORM_EPS = 1e-06
BETA_ONE = 0.9
BETA_TWO = 0.95
ADAM_EPS = 1e-08
LEARN_RATE = 0.02
DECAY_RATE = 0.1
CLIP_EPS = 1e-06

SCALES = (D ** (-0.5), LATENT ** (-0.5))
PIPE = ("xh", "y")
DP = ("z", "xl", "core")
BF = jnp.bfloat16
F32 = jnp.float32


def shift(value, axis, by, size):
    return lax.ppermute(value, axis, [(i, (i + by) % size) for i in range(size)])


def swap(value, axis):
    return lax.ppermute(value, axis, [(0, 1), (1, 0)])


def mirror(value):
    return lax.ppermute(value, PIPE, [(i, NP - 1 - i) for i in range(NP)])


def mirror_cross(value):
    pairs = [(i * 2 + a, (NP - 1 - i) * 2 + 1 - a) for i in range(NP) for a in range(2)]
    return lax.ppermute(value, ("xh", "y", "xl"), pairs)


def sds(shape, dtype):
    return jax.ShapeDtypeStruct(shape, dtype)


def call(kernel, out_shape, ins, flops, aliases=None):
    nbytes = sum(math.prod(a.shape) * a.dtype.itemsize for a in list(ins) + list(out_shape))
    vmem = pl.BlockSpec(memory_space=pltpu.VMEM)
    return pl.pallas_call(
        kernel,
        out_shape=out_shape,
        in_specs=[pl.BlockSpec(memory_space=pltpu.SMEM)] + [vmem] * (len(ins) - 1),
        out_specs=[vmem] * len(out_shape),
        input_output_aliases=aliases or {},
        compiler_params=pltpu.CompilerParams(vmem_limit_bytes=KERNEL_MB * 2**20),
        cost_estimate=pl.CostEstimate(flops=flops, bytes_accessed=nbytes, transcendentals=0),
    )(*ins)


def dot(a, b):
    return jnp.dot(a, b, preferred_element_type=F32)


def dot_t(a, b):
    return lax.dot_general(a, b, (((1,), (1,)), ((), ())), preferred_element_type=F32)


def dot_tn(a, b):
    return lax.dot_general(a, b, (((0,), (0,)), ((), ())), preferred_element_type=F32)


def backward(latent, factor, d_norm):
    inner = jnp.mean(d_norm * latent, axis=-1, keepdims=True)
    return (factor * (d_norm - latent * (factor * factor * inner))).astype(BF)


def is_end(where_ref, u):
    return where_ref[2] == (NP - 1 if u == 0 else 0)


def quad_kernel(where_ref, own_ref, mirrored_ref, near_ref, crossed_ref, out_ref):
    xl = where_ref[3]
    out_ref[xl, 0] = own_ref[...]
    out_ref[xl, 1] = mirrored_ref[...]
    out_ref[1 - xl, 0] = near_ref[...]
    out_ref[1 - xl, 1] = crossed_ref[...]


def put(where_ref, w_ref, sections, k, other, block_of):
    core = where_ref[1]
    zz = lax.rem(where_ref[0] + k, NZ)
    for xl in range(2):
        row = zz * 448 + xl * 224 + (1 - core if other else core) * ROWS
        for sec in sections:
            for kind in range(2):
                w_ref[sec, kind, pl.ds(pl.multiple_of(row, 16), ROWS), :] = block_of(xl, sec, kind)


def place_kernel(ks, where_ref, *refs):
    w_ref = refs[-1]
    for i, ref in enumerate(refs[: 2 * len(ks)]):
        put(where_ref, w_ref, (0, 1), ks[i // 2], i % 2, lambda xl, sec, kind: ref[xl, sec, kind])


def step0_kernel(u, where_ref, mask_ref, x_ref, carry_ref, low_ref, low2_ref, high_ref, high2_ref, _, *outs):
    latent_ref, factor_ref, normed_ref, cot_ref, d_lat_ref, out_ref, w_both_ref = outs
    w_ref = w_both_ref.at[u]
    for other, halves in enumerate(((low_ref, high_ref), (low2_ref, high2_ref))):
        put(where_ref, w_both_ref, (u,), 4, other, lambda xl, sec, kind: halves[xl][sec, kind])
    latent = dot(x_ref[0, :, u].reshape(STEPS * TOK, D), w_ref[0])
    factor = lax.rsqrt(jnp.mean(latent * latent, axis=-1, keepdims=True) + NORM_EPS)
    latent_ref[...] = latent
    factor_ref[...] = jnp.broadcast_to(factor, (STEPS * TOK, 128))
    normed_ref[...] = (latent * factor).astype(BF)
    end = is_end(where_ref, u)

    @pl.when(end)
    def _():
        for b in range(D // BLOCK):
            cols = slice(b * BLOCK, (b + 1) * BLOCK)
            out = x_ref[0, 0, u, :, cols].astype(F32) + dot_t(normed_ref[:TOK], w_ref[1, cols])
            cot_ref[:, cols] = (mask_ref[0, u] * out).astype(BF)

    @pl.when(jnp.logical_not(end))
    def _():
        cot_ref[...] = carry_ref[0, u]

    d_norm = dot(cot_ref[...], w_ref[1])
    d_lat_ref[...] = backward(latent_ref[:TOK], factor_ref[:TOK, :1], d_norm)
    for b in range(D // BLOCK):
        cols = slice(b * BLOCK, (b + 1) * BLOCK)
        out = cot_ref[:, cols].astype(F32) + dot_t(d_lat_ref[...], w_ref[0, cols])
        out_ref[:, cols] = out.astype(BF)


def step1_kernel(u, where_ref, mask_ref, x_ref, w_both_ref, latent_ref, factor_ref, normed_ref, cot0_ref, d_lat0_ref,
                 arr_ref, *refs):
    cot_ref, d_lat_ref, mine_ref, other_ref = refs[-4:]
    w_ref = w_both_ref.at[u]
    z = where_ref[0]
    core = where_ref[1]

    def emit(grad, b, kind):
        for i in range(2):
            k = lax.rem(2 * b + i - z + NZ, NZ)
            for xl in range(2):
                base = (i * 4 + xl * 2) * ROWS
                low = grad[base : base + ROWS]
                high = grad[base + ROWS : base + 2 * ROWS]
                mine_ref[k, xl, kind] = jnp.where(core == 0, low, high)
                other_ref[k, xl, kind] = jnp.where(core == 0, high, low)

    end = is_end(where_ref, u)

    @pl.when(end)
    def _():
        for b in range(D // BLOCK):
            cols = slice(b * BLOCK, (b + 1) * BLOCK)
            out = x_ref[0, 1, u, :, cols].astype(F32) + dot_t(normed_ref[TOK:], w_ref[1, cols])
            cot_ref[:, cols] = (mask_ref[1, u] * out).astype(BF)

    @pl.when(jnp.logical_not(end))
    def _():
        cot_ref[...] = arr_ref[...]

    d_norm = dot(cot_ref[...], w_ref[1])
    d_lat = backward(latent_ref[TOK:], factor_ref[TOK:, :1], d_norm)
    d_lat_ref[...] = d_lat
    d_lats = jnp.concatenate([d_lat0_ref[...], d_lat], axis=0)
    for b in range(D // BLOCK):
        cols = slice(b * BLOCK, (b + 1) * BLOCK)
        cots = jnp.concatenate([cot0_ref[:, cols], cot_ref[:, cols]], axis=0)
        emit((dot_tn(cots, normed_ref[...]) * SCALES[1]).astype(BF), b, 1)
        xs = x_ref[0, :, u, :, cols].reshape(STEPS * TOK, BLOCK)
        emit((dot_tn(xs, d_lats) * SCALES[0]).astype(BF), b, 0)


def carry_kernel(where_ref, w_both_ref, *refs):
    out_ref, done_ref = refs[-2:]
    done_ref[...] = jnp.zeros_like(done_ref)
    for u in range(2):
        w_ref = w_both_ref.at[u]
        d_lat_ref, cot_ref = refs[u * 2 : u * 2 + 2]
        for b in range(D // BLOCK):
            cols = slice(b * BLOCK, (b + 1) * BLOCK)
            out = cot_ref[:, cols].astype(F32) + dot_t(d_lat_ref[...], w_ref[0, cols])
            out_ref[0, u, :, cols] = out.astype(BF)


def far_kernel(where_ref, mine_ref, theirs_ref, low_ref, high_ref):
    for xl, ref in enumerate((low_ref, high_ref)):
        ref[...] = (mine_ref[4, xl].astype(F32) + theirs_ref[4, xl].astype(F32)).astype(BF)


def join_kernel(k, where_ref, mine_ref, theirs_ref, ahead_ref, back_ref, ahead_out_ref, back_out_ref):
    sides = ((k, ahead_ref, ahead_out_ref, 0), (NZ - k, back_ref, back_out_ref, 1))
    for place, arrived_ref, out_ref, half in sides:
        for xl in range(2):
            total = mine_ref[place, xl].astype(F32) + theirs_ref[place, xl].astype(F32)
            if k < 3:
                total = total + arrived_ref[xl].astype(F32)
            elif xl == half:
                total = total + arrived_ref[...].astype(F32)
            out_ref[xl] = total.astype(BF)


def whole_kernel(where_ref, mine_ref, theirs_ref, ahead_ref, back_ref, out_ref):
    for xl in range(2):
        parts = (mine_ref[0, xl], theirs_ref[0, xl], ahead_ref[xl], back_ref[xl])
        out_ref[xl] = sum(part.astype(F32) for part in parts).astype(BF)


def last_kernel(where_ref, mine_ref, theirs_ref, ahead_ref, back_ref, mirrored_ref, keep_ref, give_ref):
    xl = where_ref[3]

    def total(i):
        parts = (mine_ref[0, i], theirs_ref[0, i], ahead_ref[i], back_ref[i], mirrored_ref[i])
        return sum(part.astype(F32) for part in parts)

    keep_ref[...] = total(xl)
    give_ref[...] = total(1 - xl).astype(BF)


def gradient_kernel(where_ref, keep_ref, near_ref, _, out_ref, squares_ref):
    total = keep_ref[...] + near_ref[...].astype(F32)
    out_ref[0] = total
    squares = jnp.sum((total * total).reshape(2 * ROWS, LATENT), axis=0, keepdims=True)
    squares_ref[...] = squares[:, :128] + squares[:, 128:]


def update_kernel(where_ref, squares_ref, gradient_ref, weights_ref, moment1_ref, moment2_ref, new_weights_ref,
                  new_moment1_ref, new_moment2_ref):
    square_total = jnp.sum(jnp.sum(squares_ref[...], axis=0), axis=-1, keepdims=True)
    clip_limit = math.sqrt(2.0 * NP * D * LATENT)
    clip_scale = jnp.minimum(1.0, clip_limit / jnp.sqrt(square_total + CLIP_EPS))
    for kind in range(2):
        clipped = gradient_ref[0, kind] * clip_scale
        moment1 = BETA_ONE * moment1_ref[0, kind] + (1.0 - BETA_ONE) * clipped
        moment2 = BETA_TWO * moment2_ref[0, kind] + (1.0 - BETA_TWO) * clipped * clipped
        root = jnp.sqrt(moment2 / (1.0 - BETA_TWO**ADAM_STEP)) + ADAM_EPS
        update = moment1 / (1.0 - BETA_ONE**ADAM_STEP) / root
        new_moment1_ref[0, kind] = moment1
        new_moment2_ref[0, kind] = moment2
        new_weights_ref[0, kind] = weights_ref[0, kind] - LEARN_RATE * (update + DECAY_RATE * weights_ref[0, kind])


def local(section_inputs, carry_in, loss_mask, weights, moment1, moment2):
    where = jnp.stack(
        [lax.axis_index("z"), lax.axis_index("core"), lax.axis_index(PIPE), lax.axis_index("xl")]
    ).astype(jnp.int32)
    multipliers = jnp.array(SCALES, F32).reshape(2, 1, 1)
    own = (weights[0] * multipliers).astype(BF)
    mask = loss_mask.astype(F32)[..., None]
    shard = (2, ROWS, LATENT)
    chunk = sds((2, *shard), BF)
    unit = 2 * TOK * D * LATENT
    small = 1 << 20

    def place(ks, chunks, *held):
        ins = [where]
        for c in chunks:
            ins += [c, swap(c, "core")]
        ins += held
        aliases = {len(ins) - 1: 0} if held else None
        kernel = lambda *refs: place_kernel(ks, *refs)
        return call(kernel, [sds((2, 2, D, LATENT), BF)], ins, 10 * unit, aliases)[0]

    def gather(start):
        w = place((0,), [start])
        ahead = back = start
        for k in range(1, 4):
            ahead = shift(ahead, "z", 1, NZ)
            back = shift(back, "z", -1, NZ)
            held = [section_inputs, carry_in] if k > 1 else []
            w = place((k, NZ - k), [back, ahead], *held, w)
        return w, shift(ahead[0], "z", 1, NZ), shift(back[1], "z", -1, NZ)

    def hop(u, out):
        if u == 0:
            return lax.ppermute(out, PIPE, [(i, i - 1) for i in range(1, NP)])
        return lax.ppermute(out, PIPE, [(i, i + 1) for i in range(NP - 1)])

    def step1(u, state, arrived, *after):
        latent, factor, normed, cot0, d_lat0, _ = state
        terms = sds((NZ, *chunk.shape), BF)
        cot1, d_lat1, mine, other = call(
            lambda *refs: step1_kernel(u, *refs),
            [sds((TOK, D), BF), sds((TOK, LATENT), BF), terms, terms],
            [where, mask, section_inputs, w, latent, factor, normed, cot0, d_lat0, arrived, *after],
            6 * unit,
        )
        return (d_lat1, cot1), mine, swap(other, "core")

    def scatter(mine, theirs):
        both = [where, mine, theirs]

        ahead, back = call(far_kernel, [sds(shard, BF), sds(shard, BF)], both, small)
        for k in (3, 2, 1):
            ins = [*both, shift(ahead, "z", 1, NZ), shift(back, "z", -1, NZ)]
            ahead, back = call(functools.partial(join_kernel, k), [chunk, chunk], ins, small)
        ahead = shift(ahead, "z", 1, NZ)
        back = shift(back, "z", -1, NZ)
        return [*both, ahead, back]

    shards = [where, own, mirror(own), swap(own, "xl"), mirror_cross(own)]
    w, low, high = gather(call(quad_kernel, [sds((2, 2, *shard), BF)], shards, small)[0])
    state = [
        sds((STEPS * TOK, LATENT), F32), sds((STEPS * TOK, 128), F32), sds((STEPS * TOK, LATENT), BF),
        sds((TOK, D), BF), sds((TOK, LATENT), BF), sds((TOK, D), BF),
    ]
    last = [low, swap(low, "core"), high, swap(high, "core")]

    def step0(u, w):
        ins = [where, mask, section_inputs, carry_in, *last, w]
        kernel = lambda *refs: step0_kernel(u, *refs)
        *out, w = call(kernel, state + [sds(w.shape, BF)], ins, 5 * unit, {len(ins) - 1: len(state)})
        return out, w

    state_b, w = step0(1, w)
    state_a, w = step0(0, w)
    arrived_b = hop(1, state_b[-1])
    arrived_a = hop(0, state_a[-1])
    end_b, mine_b, theirs_b = step1(1, state_b, arrived_b)
    end_a, mine_a, theirs_a = step1(0, state_a, arrived_a, end_b[0])
    (whole_b,) = call(whole_kernel, [chunk], scatter(mine_b, theirs_b), small)
    parts = [*scatter(mine_a, theirs_a), mirror(whole_b)]
    keep_a, give_a = call(last_kernel, [sds(shard, F32), sds(shard, BF)], parts, small)
    near = swap(give_a, "xl")
    outs = [sds((1, 2, TOK, D), BF), sds((8, 128), F32)]
    carry_out, done = call(carry_kernel, outs, [where, w, *end_a, *end_b], 2 * unit)
    outs = [sds((1, *shard), F32), sds((1, 128), F32)]
    gradient, squares = call(gradient_kernel, outs, [where, keep_a, near, done], small)
    squares = jnp.broadcast_to(squares, (NP * NZ * 4, 1, 128))
    squares = lax.all_to_all(squares, PIPE + DP, 0, 0, tiled=True)
    owned = sds(weights.shape, F32)
    ins = [where, squares, gradient, weights, moment1, moment2]
    return (carry_out, *call(update_kernel, [owned, owned, owned], ins, small))


def solution(mesh):
    fine = Mesh(mesh.devices.reshape(2, 4, 8, 2, 2), PIPE + DP)
    rows = P(PIPE, None, DP, None)
    return jax.shard_map(
        local,
        mesh=fine,
        in_specs=(P(PIPE, None, None, DP, None), rows, P(None, None, DP), rows, rows, rows),
        out_specs=(rows, rows, rows, rows),
        check_vma=False,
    )
```

```python
import functools
import math

import jax
import jax.numpy as jnp
from jax import lax
from jax.experimental import pallas as pl
from jax.experimental.pallas import tpu as pltpu
from jax.sharding import Mesh
from jax.sharding import PartitionSpec as P

D = 3584
LATENT = 256
STEPS = 2
ADAM_STEP = 10
TOK = 128
ROWS = 112
NZ = 8
NP = 8
BLOCK = 896
KERNEL_MB = 12

NORM_EPS = 1e-06
BETA_ONE = 0.9
BETA_TWO = 0.95
ADAM_EPS = 1e-08
LEARN_RATE = 0.02
DECAY_RATE = 0.1
CLIP_EPS = 1e-06

SCALES = (D ** (-0.5), LATENT ** (-0.5))
PIPE = ("xh", "y")
DP = ("z", "xl", "core")
BF = jnp.bfloat16
F32 = jnp.float32


def shift(value, axis, by, size):
    return lax.ppermute(value, axis, [(i, (i + by) % size) for i in range(size)])


def swap(value, axis):
    return lax.ppermute(value, axis, [(0, 1), (1, 0)])


def mirror(value):
    return lax.ppermute(value, PIPE, [(i, NP - 1 - i) for i in range(NP)])


def mirror_cross(value):
    pairs = [(i * 2 + a, (NP - 1 - i) * 2 + 1 - a) for i in range(NP) for a in range(2)]
    return lax.ppermute(value, ("xh", "y", "xl"), pairs)


def sds(shape, dtype):
    return jax.ShapeDtypeStruct(shape, dtype)


def call(kernel, out_shape, ins, flops, aliases=None):
    nbytes = sum(math.prod(a.shape) * a.dtype.itemsize for a in list(ins) + list(out_shape))
    vmem = pl.BlockSpec(memory_space=pltpu.VMEM)
    return pl.pallas_call(
        kernel,
        out_shape=out_shape,
        in_specs=[pl.BlockSpec(memory_space=pltpu.SMEM)] + [vmem] * (len(ins) - 1),
        out_specs=[vmem] * len(out_shape),
        input_output_aliases=aliases or {},
        compiler_params=pltpu.CompilerParams(vmem_limit_bytes=KERNEL_MB * 2**20),
        cost_estimate=pl.CostEstimate(flops=flops, bytes_accessed=nbytes, transcendentals=0),
    )(*ins)


def dot(a, b):
    return jnp.dot(a, b, preferred_element_type=F32)


def dot_t(a, b):
    return lax.dot_general(a, b, (((1,), (1,)), ((), ())), preferred_element_type=F32)


def dot_tn(a, b):
    return lax.dot_general(a, b, (((0,), (0,)), ((), ())), preferred_element_type=F32)


def backward(latent, factor, d_norm):
    inner = jnp.mean(d_norm * latent, axis=-1, keepdims=True)
    return (factor * (d_norm - latent * (factor * factor * inner))).astype(BF)


def is_end(where_ref, u):
    return where_ref[2] == (NP - 1 if u == 0 else 0)


def quad_kernel(where_ref, own_ref, mirrored_ref, near_ref, crossed_ref, out_ref):
    xl = where_ref[3]
    out_ref[xl, 0] = own_ref[...]
    out_ref[xl, 1] = mirrored_ref[...]
    out_ref[1 - xl, 0] = near_ref[...]
    out_ref[1 - xl, 1] = crossed_ref[...]


def put(where_ref, w_ref, sections, k, other, block_of):
    core = where_ref[1]
    zz = lax.rem(where_ref[0] + k, NZ)
    for xl in range(2):
        row = zz * 448 + xl * 224 + (1 - core if other else core) * ROWS
        for sec in sections:
            for kind in range(2):
                w_ref[sec, kind, pl.ds(pl.multiple_of(row, 16), ROWS), :] = block_of(xl, sec, kind)


def place_kernel(ks, where_ref, *refs):
    w_ref = refs[-1]
    for i, ref in enumerate(refs[: 2 * len(ks)]):
        put(where_ref, w_ref, (0, 1), ks[i // 2], i % 2, lambda xl, sec, kind: ref[xl, sec, kind])


def step0_kernel(u, where_ref, mask_ref, x_ref, carry_ref, low_ref, low2_ref, high_ref, high2_ref, _, *outs):
    latent_ref, factor_ref, normed_ref, cot_ref, d_lat_ref, out_ref, w_both_ref = outs
    w_ref = w_both_ref.at[u]
    for other, halves in enumerate(((low_ref, high_ref), (low2_ref, high2_ref))):
        put(where_ref, w_both_ref, (u,), 4, other, lambda xl, sec, kind: halves[xl][sec, kind])
    latent = dot(x_ref[0, :, u].reshape(STEPS * TOK, D), w_ref[0])
    factor = lax.rsqrt(jnp.mean(latent * latent, axis=-1, keepdims=True) + NORM_EPS)
    latent_ref[...] = latent
    factor_ref[...] = jnp.broadcast_to(factor, (STEPS * TOK, 128))
    normed_ref[...] = (latent * factor).astype(BF)
    end = is_end(where_ref, u)

    @pl.when(end)
    def _():
        for b in range(D // BLOCK):
            cols = slice(b * BLOCK, (b + 1) * BLOCK)
            out = x_ref[0, 0, u, :, cols].astype(F32) + dot_t(normed_ref[:TOK], w_ref[1, cols])
            cot_ref[:, cols] = (mask_ref[0, u] * out).astype(BF)

    @pl.when(jnp.logical_not(end))
    def _():
        cot_ref[...] = carry_ref[0, u]

    d_norm = dot(cot_ref[...], w_ref[1])
    d_lat_ref[...] = backward(latent_ref[:TOK], factor_ref[:TOK, :1], d_norm)
    for b in range(D // BLOCK):
        cols = slice(b * BLOCK, (b + 1) * BLOCK)
        out = cot_ref[:, cols].astype(F32) + dot_t(d_lat_ref[...], w_ref[0, cols])
        out_ref[:, cols] = out.astype(BF)


def step1_kernel(u, where_ref, mask_ref, x_ref, w_both_ref, latent_ref, factor_ref, normed_ref, cot0_ref, d_lat0_ref,
                 arr_ref, *refs):
    cot_ref, d_lat_ref, mine_ref, other_ref = refs[-4:]
    w_ref = w_both_ref.at[u]
    z = where_ref[0]
    core = where_ref[1]

    def emit(grad, b, kind):
        for i in range(2):
            k = lax.rem(2 * b + i - z + NZ, NZ)
            for xl in range(2):
                base = (i * 4 + xl * 2) * ROWS
                low = grad[base : base + ROWS]
                high = grad[base + ROWS : base + 2 * ROWS]
                mine_ref[k, xl, kind] = jnp.where(core == 0, low, high)
                other_ref[k, xl, kind] = jnp.where(core == 0, high, low)

    end = is_end(where_ref, u)

    @pl.when(end)
    def _():
        for b in range(D // BLOCK):
            cols = slice(b * BLOCK, (b + 1) * BLOCK)
            out = x_ref[0, 1, u, :, cols].astype(F32) + dot_t(normed_ref[TOK:], w_ref[1, cols])
            cot_ref[:, cols] = (mask_ref[1, u] * out).astype(BF)

    @pl.when(jnp.logical_not(end))
    def _():
        cot_ref[...] = arr_ref[...]

    d_norm = dot(cot_ref[...], w_ref[1])
    d_lat = backward(latent_ref[TOK:], factor_ref[TOK:, :1], d_norm)
    d_lat_ref[...] = d_lat
    d_lats = jnp.concatenate([d_lat0_ref[...], d_lat], axis=0)
    for b in range(D // BLOCK):
        cols = slice(b * BLOCK, (b + 1) * BLOCK)
        cots = jnp.concatenate([cot0_ref[:, cols], cot_ref[:, cols]], axis=0)
        emit((dot_tn(cots, normed_ref[...]) * SCALES[1]).astype(BF), b, 1)
        xs = x_ref[0, :, u, :, cols].reshape(STEPS * TOK, BLOCK)
        emit((dot_tn(xs, d_lats) * SCALES[0]).astype(BF), b, 0)


def carry_kernel(where_ref, w_both_ref, *refs):
    out_ref, done_ref = refs[-2:]
    done_ref[...] = jnp.zeros_like(done_ref)
    for u in range(2):
        w_ref = w_both_ref.at[u]
        d_lat_ref, cot_ref = refs[u * 2 : u * 2 + 2]
        for b in range(D // BLOCK):
            cols = slice(b * BLOCK, (b + 1) * BLOCK)
            out = cot_ref[:, cols].astype(F32) + dot_t(d_lat_ref[...], w_ref[0, cols])
            out_ref[0, u, :, cols] = out.astype(BF)


def far_kernel(where_ref, mine_ref, theirs_ref, low_ref, high_ref):
    for xl, ref in enumerate((low_ref, high_ref)):
        ref[...] = (mine_ref[4, xl].astype(F32) + theirs_ref[4, xl].astype(F32)).astype(BF)


def join_kernel(k, where_ref, mine_ref, theirs_ref, ahead_ref, back_ref, ahead_out_ref, back_out_ref):
    sides = ((k, ahead_ref, ahead_out_ref, 0), (NZ - k, back_ref, back_out_ref, 1))
    for place, arrived_ref, out_ref, half in sides:
        for xl in range(2):
            total = mine_ref[place, xl].astype(F32) + theirs_ref[place, xl].astype(F32)
            if k < 3:
                total = total + arrived_ref[xl].astype(F32)
            elif xl == half:
                total = total + arrived_ref[...].astype(F32)
            out_ref[xl] = total.astype(BF)


def last_kernel(where_ref, mine_ref, theirs_ref, ahead_ref, back_ref, *refs):
    keep_ref, give_ref = refs[-2:]
    xl = where_ref[3]

    def total(i):
        parts = (mine_ref[0, i], theirs_ref[0, i], ahead_ref[i], back_ref[i])
        return sum(part.astype(F32) for part in parts)

    keep_ref[...] = total(xl).astype(keep_ref.dtype)
    give_ref[...] = total(1 - xl).astype(BF)


def gradient_kernel(where_ref, keep_ref, near_ref, mirrored_ref, crossed_ref, _, out_ref, squares_ref):
    total = keep_ref[...] + near_ref[...].astype(F32) + mirrored_ref[...].astype(F32) + crossed_ref[...].astype(F32)
    out_ref[0] = total
    squares = jnp.sum((total * total).reshape(2 * ROWS, LATENT), axis=0, keepdims=True)
    squares_ref[...] = squares[:, :128] + squares[:, 128:]


def update_kernel(where_ref, squares_ref, gradient_ref, weights_ref, moment1_ref, moment2_ref, new_weights_ref,
                  new_moment1_ref, new_moment2_ref):
    square_total = jnp.sum(jnp.sum(squares_ref[...], axis=0), axis=-1, keepdims=True)
    clip_limit = math.sqrt(2.0 * NP * D * LATENT)
    clip_scale = jnp.minimum(1.0, clip_limit / jnp.sqrt(square_total + CLIP_EPS))
    for kind in range(2):
        clipped = gradient_ref[0, kind] * clip_scale
        moment1 = BETA_ONE * moment1_ref[0, kind] + (1.0 - BETA_ONE) * clipped
        moment2 = BETA_TWO * moment2_ref[0, kind] + (1.0 - BETA_TWO) * clipped * clipped
        root = jnp.sqrt(moment2 / (1.0 - BETA_TWO**ADAM_STEP)) + ADAM_EPS
        update = moment1 / (1.0 - BETA_ONE**ADAM_STEP) / root
        new_moment1_ref[0, kind] = moment1
        new_moment2_ref[0, kind] = moment2
        new_weights_ref[0, kind] = weights_ref[0, kind] - LEARN_RATE * (update + DECAY_RATE * weights_ref[0, kind])


def local(section_inputs, carry_in, loss_mask, weights, moment1, moment2):
    where = jnp.stack(
        [lax.axis_index("z"), lax.axis_index("core"), lax.axis_index(PIPE), lax.axis_index("xl")]
    ).astype(jnp.int32)
    multipliers = jnp.array(SCALES, F32).reshape(2, 1, 1)
    own = (weights[0] * multipliers).astype(BF)
    mask = loss_mask.astype(F32)[..., None]
    shard = (2, ROWS, LATENT)
    chunk = sds((2, *shard), BF)
    unit = 2 * TOK * D * LATENT
    small = 1 << 20

    def place(ks, chunks, *held):
        ins = [where]
        for c in chunks:
            ins += [c, swap(c, "core")]
        ins += held
        aliases = {len(ins) - 1: 0} if held else None
        kernel = lambda *refs: place_kernel(ks, *refs)
        return call(kernel, [sds((2, 2, D, LATENT), BF)], ins, 10 * unit, aliases)[0]

    def gather(start):
        w = place((0,), [start])
        ahead = back = start
        for k in range(1, 4):
            ahead = shift(ahead, "z", 1, NZ)
            back = shift(back, "z", -1, NZ)
            held = [section_inputs, carry_in] if k > 1 else []
            w = place((k, NZ - k), [back, ahead], *held, w)
        return w, shift(ahead[0], "z", 1, NZ), shift(back[1], "z", -1, NZ)

    def hop(u, out):
        if u == 0:
            return lax.ppermute(out, PIPE, [(i, i - 1) for i in range(1, NP)])
        return lax.ppermute(out, PIPE, [(i, i + 1) for i in range(NP - 1)])

    def step1(u, state, arrived, *after):
        latent, factor, normed, cot0, d_lat0, _ = state
        terms = sds((NZ, *chunk.shape), BF)
        cot1, d_lat1, mine, other = call(
            lambda *refs: step1_kernel(u, *refs),
            [sds((TOK, D), BF), sds((TOK, LATENT), BF), terms, terms],
            [where, mask, section_inputs, w, latent, factor, normed, cot0, d_lat0, arrived, *after],
            6 * unit,
        )
        return (d_lat1, cot1), mine, swap(other, "core")

    def scatter(mine, theirs, keep_type, *after):
        both = [where, mine, theirs]

        ahead, back = call(far_kernel, [sds(shard, BF), sds(shard, BF)], both, small)
        for k in (3, 2, 1):
            ins = [*both, shift(ahead, "z", 1, NZ), shift(back, "z", -1, NZ)]
            ahead, back = call(functools.partial(join_kernel, k), [chunk, chunk], ins, small)
        ahead = shift(ahead, "z", 1, NZ)
        back = shift(back, "z", -1, NZ)
        parts = [*both, ahead, back, *after]
        keep, give = call(last_kernel, [sds(shard, keep_type), sds(shard, BF)], parts, small)
        return keep, give

    shards = [where, own, mirror(own), swap(own, "xl"), mirror_cross(own)]
    w, low, high = gather(call(quad_kernel, [sds((2, 2, *shard), BF)], shards, small)[0])
    state = [
        sds((STEPS * TOK, LATENT), F32), sds((STEPS * TOK, 128), F32), sds((STEPS * TOK, LATENT), BF),
        sds((TOK, D), BF), sds((TOK, LATENT), BF), sds((TOK, D), BF),
    ]
    last = [low, swap(low, "core"), high, swap(high, "core")]

    def step0(u, w):
        ins = [where, mask, section_inputs, carry_in, *last, w]
        kernel = lambda *refs: step0_kernel(u, *refs)
        *out, w = call(kernel, state + [sds(w.shape, BF)], ins, 5 * unit, {len(ins) - 1: len(state)})
        return out, w

    state_b, w = step0(1, w)
    state_a, w = step0(0, w)
    arrived_b = hop(1, state_b[-1])
    arrived_a = hop(0, state_a[-1])
    end_b, mine_b, theirs_b = step1(1, state_b, arrived_b)
    end_a, mine_a, theirs_a = step1(0, state_a, arrived_a, end_b[0])
    keep_b, give_b = scatter(mine_b, theirs_b, BF)
    mirrored = mirror(keep_b)
    crossed = mirror_cross(give_b)
    keep_a, give_a = scatter(mine_a, theirs_a, F32, keep_b)
    near = swap(give_a, "xl")
    outs = [sds((1, 2, TOK, D), BF), sds((8, 128), F32)]
    carry_out, done = call(carry_kernel, outs, [where, w, *end_a, *end_b], 2 * unit)
    outs = [sds((1, *shard), F32), sds((1, 128), F32)]
    gradient, squares = call(gradient_kernel, outs, [where, keep_a, near, mirrored, crossed, done], small)
    squares = squares + swap(squares, "core")
    squares = jnp.broadcast_to(squares, (NP * NZ * 2, 1, 128))
    squares = lax.all_to_all(squares, PIPE + ("z", "xl"), 0, 0, tiled=True)
    owned = sds(weights.shape, F32)
    ins = [where, squares, gradient, weights, moment1, moment2]
    return (carry_out, *call(update_kernel, [owned, owned, owned], ins, small))


def solution(mesh):
    fine = Mesh(mesh.devices.reshape(2, 4, 8, 2, 2), PIPE + DP)
    rows = P(PIPE, None, DP, None)
    return jax.shard_map(
        local,
        mesh=fine,
        in_specs=(P(PIPE, None, None, DP, None), rows, P(None, None, DP), rows, rows, rows),
        out_specs=(rows, rows, rows, rows),
        check_vma=False,
    )
```

```python
import functools
import math

import jax
import jax.numpy as jnp
from jax import lax
from jax.experimental import pallas as pl
from jax.experimental.pallas import tpu as pltpu
from jax.sharding import Mesh
from jax.sharding import PartitionSpec as P

D = 3584
LATENT = 256
STEPS = 2
ADAM_STEP = 10
TOK = 128
ROWS = 112
NZ = 8
NP = 8
BLOCK = 896
KERNEL_MB = 12

NORM_EPS = 1e-06
BETA_ONE = 0.9
BETA_TWO = 0.95
ADAM_EPS = 1e-08
LEARN_RATE = 0.02
DECAY_RATE = 0.1
CLIP_EPS = 1e-06

SCALES = (D ** (-0.5), LATENT ** (-0.5))
PIPE = ("xh", "y")
DP = ("z", "xl", "core")
BF = jnp.bfloat16
F32 = jnp.float32


def shift(value, axis, by, size):
    return lax.ppermute(value, axis, [(i, (i + by) % size) for i in range(size)])


def swap(value, axis):
    return lax.ppermute(value, axis, [(0, 1), (1, 0)])


def mirror(value):
    return lax.ppermute(value, PIPE, [(i, NP - 1 - i) for i in range(NP)])


def mirror_cross(value):
    pairs = [(i * 2 + a, (NP - 1 - i) * 2 + 1 - a) for i in range(NP) for a in range(2)]
    return lax.ppermute(value, ("xh", "y", "xl"), pairs)


def sds(shape, dtype):
    return jax.ShapeDtypeStruct(shape, dtype)


def call(kernel, out_shape, ins, flops, aliases=None):
    nbytes = sum(math.prod(a.shape) * a.dtype.itemsize for a in list(ins) + list(out_shape))
    vmem = pl.BlockSpec(memory_space=pltpu.VMEM)
    return pl.pallas_call(
        kernel,
        out_shape=out_shape,
        in_specs=[pl.BlockSpec(memory_space=pltpu.SMEM)] + [vmem] * (len(ins) - 1),
        out_specs=[vmem] * len(out_shape),
        input_output_aliases=aliases or {},
        compiler_params=pltpu.CompilerParams(vmem_limit_bytes=KERNEL_MB * 2**20),
        cost_estimate=pl.CostEstimate(flops=flops, bytes_accessed=nbytes, transcendentals=0),
    )(*ins)


def dot(a, b):
    return jnp.dot(a, b, preferred_element_type=F32)


def dot_t(a, b):
    return lax.dot_general(a, b, (((1,), (1,)), ((), ())), preferred_element_type=F32)


def dot_tn(a, b):
    return lax.dot_general(a, b, (((0,), (0,)), ((), ())), preferred_element_type=F32)


def backward(latent, factor, d_norm):
    inner = jnp.mean(d_norm * latent, axis=-1, keepdims=True)
    return (factor * (d_norm - latent * (factor * factor * inner))).astype(BF)


def is_end(where_ref, u):
    return where_ref[2] == (NP - 1 if u == 0 else 0)


def quad_kernel(where_ref, own_ref, mirrored_ref, near_ref, crossed_ref, out_ref):
    xl = where_ref[3]
    out_ref[xl, 0] = own_ref[...]
    out_ref[xl, 1] = mirrored_ref[...]
    out_ref[1 - xl, 0] = near_ref[...]
    out_ref[1 - xl, 1] = crossed_ref[...]


def put(where_ref, w_ref, sections, k, other, block_of):
    core = where_ref[1]
    zz = lax.rem(where_ref[0] + k, NZ)
    for xl in range(2):
        row = zz * 448 + xl * 224 + (1 - core if other else core) * ROWS
        for sec in sections:
            for kind in range(2):
                w_ref[sec, kind, pl.ds(pl.multiple_of(row, 16), ROWS), :] = block_of(xl, sec, kind)


def place_kernel(ks, where_ref, *refs):
    w_ref = refs[-1]
    for i, ref in enumerate(refs[: 2 * len(ks)]):
        put(where_ref, w_ref, (0, 1), ks[i // 2], i % 2, lambda xl, sec, kind: ref[xl, sec, kind])


def step0_kernel(u, where_ref, mask_ref, x_ref, carry_ref, low_ref, low2_ref, high_ref, high2_ref, _, *outs):
    latent_ref, factor_ref, normed_ref, cot_ref, d_lat_ref, out_ref, w_both_ref = outs
    w_ref = w_both_ref.at[u]
    for other, halves in enumerate(((low_ref, high_ref), (low2_ref, high2_ref))):
        put(where_ref, w_both_ref, (u,), 4, other, lambda xl, sec, kind: halves[xl][sec, kind])
    latent = dot(x_ref[0, :, u].reshape(STEPS * TOK, D), w_ref[0])
    factor = lax.rsqrt(jnp.mean(latent * latent, axis=-1, keepdims=True) + NORM_EPS)
    latent_ref[...] = latent
    factor_ref[...] = jnp.broadcast_to(factor, (STEPS * TOK, 128))
    normed_ref[...] = (latent * factor).astype(BF)
    end = is_end(where_ref, u)

    @pl.when(end)
    def _():
        for b in range(D // BLOCK):
            cols = slice(b * BLOCK, (b + 1) * BLOCK)
            out = x_ref[0, 0, u, :, cols].astype(F32) + dot_t(normed_ref[:TOK], w_ref[1, cols])
            cot_ref[:, cols] = (mask_ref[0, u] * out).astype(BF)

    @pl.when(jnp.logical_not(end))
    def _():
        cot_ref[...] = carry_ref[0, u]

    d_norm = dot(cot_ref[...], w_ref[1])
    d_lat_ref[...] = backward(latent_ref[:TOK], factor_ref[:TOK, :1], d_norm)
    for b in range(D // BLOCK):
        cols = slice(b * BLOCK, (b + 1) * BLOCK)
        out = cot_ref[:, cols].astype(F32) + dot_t(d_lat_ref[...], w_ref[0, cols])
        out_ref[:, cols] = out.astype(BF)


def step1_kernel(u, where_ref, mask_ref, x_ref, w_both_ref, latent_ref, factor_ref, normed_ref, cot0_ref, d_lat0_ref,
                 arr_ref, *refs):
    cot_ref, d_lat_ref, mine_ref, other_ref = refs[-4:]
    w_ref = w_both_ref.at[u]
    z = where_ref[0]
    core = where_ref[1]

    def emit(grad, b, kind):
        for i in range(2):
            k = lax.rem(2 * b + i - z + NZ, NZ)
            for xl in range(2):
                base = (i * 4 + xl * 2) * ROWS
                low = grad[base : base + ROWS]
                high = grad[base + ROWS : base + 2 * ROWS]
                mine_ref[k, xl, kind] = jnp.where(core == 0, low, high)
                other_ref[k, xl, kind] = jnp.where(core == 0, high, low)

    end = is_end(where_ref, u)

    @pl.when(end)
    def _():
        for b in range(D // BLOCK):
            cols = slice(b * BLOCK, (b + 1) * BLOCK)
            out = x_ref[0, 1, u, :, cols].astype(F32) + dot_t(normed_ref[TOK:], w_ref[1, cols])
            cot_ref[:, cols] = (mask_ref[1, u] * out).astype(BF)

    @pl.when(jnp.logical_not(end))
    def _():
        cot_ref[...] = arr_ref[...]

    d_norm = dot(cot_ref[...], w_ref[1])
    d_lat = backward(latent_ref[TOK:], factor_ref[TOK:, :1], d_norm)
    d_lat_ref[...] = d_lat
    d_lats = jnp.concatenate([d_lat0_ref[...], d_lat], axis=0)
    for b in range(D // BLOCK):
        cols = slice(b * BLOCK, (b + 1) * BLOCK)
        cots = jnp.concatenate([cot0_ref[:, cols], cot_ref[:, cols]], axis=0)
        emit((dot_tn(cots, normed_ref[...]) * SCALES[1]).astype(BF), b, 1)
        xs = x_ref[0, :, u, :, cols].reshape(STEPS * TOK, BLOCK)
        emit((dot_tn(xs, d_lats) * SCALES[0]).astype(BF), b, 0)


def carry_kernel(where_ref, w_both_ref, *refs):
    out_ref, done_ref = refs[-2:]
    done_ref[...] = jnp.zeros_like(done_ref)
    for u in range(2):
        w_ref = w_both_ref.at[u]
        d_lat_ref, cot_ref = refs[u * 2 : u * 2 + 2]
        for b in range(D // BLOCK):
            cols = slice(b * BLOCK, (b + 1) * BLOCK)
            out = cot_ref[:, cols].astype(F32) + dot_t(d_lat_ref[...], w_ref[0, cols])
            out_ref[0, u, :, cols] = out.astype(BF)


def far_kernel(where_ref, mine_ref, theirs_ref, low_ref, high_ref):
    for xl, ref in enumerate((low_ref, high_ref)):
        ref[...] = (mine_ref[4, xl].astype(F32) + theirs_ref[4, xl].astype(F32)).astype(BF)


def join_kernel(k, where_ref, mine_ref, theirs_ref, ahead_ref, back_ref, ahead_out_ref, back_out_ref):
    sides = ((k, ahead_ref, ahead_out_ref, 0), (NZ - k, back_ref, back_out_ref, 1))
    for place, arrived_ref, out_ref, half in sides:
        for xl in range(2):
            total = mine_ref[place, xl].astype(F32) + theirs_ref[place, xl].astype(F32)
            if k < 3:
                total = total + arrived_ref[xl].astype(F32)
            elif xl == half:
                total = total + arrived_ref[...].astype(F32)
            out_ref[xl] = total.astype(BF)


def last_kernel(where_ref, mine_ref, theirs_ref, ahead_ref, back_ref, *refs):
    keep_ref, give_ref = refs[-2:]
    xl = where_ref[3]

    def total(i):
        parts = (mine_ref[0, i], theirs_ref[0, i], ahead_ref[i], back_ref[i])
        return sum(part.astype(F32) for part in parts)

    keep_ref[...] = total(xl).astype(keep_ref.dtype)
    give_ref[...] = total(1 - xl).astype(BF)


def gradient_kernel(where_ref, keep_ref, near_ref, mirrored_ref, crossed_ref, _, out_ref, squares_ref):
    total = keep_ref[...] + near_ref[...].astype(F32) + mirrored_ref[...].astype(F32) + crossed_ref[...].astype(F32)
    out_ref[0] = total
    squares = jnp.sum((total * total).reshape(2 * ROWS, LATENT), axis=0, keepdims=True)
    squares_ref[...] = squares[:, :128] + squares[:, 128:]


def update_kernel(where_ref, squares_ref, gradient_ref, weights_ref, moment1_ref, moment2_ref, new_weights_ref,
                  new_moment1_ref, new_moment2_ref):
    square_total = jnp.sum(jnp.sum(squares_ref[...], axis=0), axis=-1, keepdims=True)
    clip_limit = math.sqrt(2.0 * NP * D * LATENT)
    clip_scale = jnp.minimum(1.0, clip_limit / jnp.sqrt(square_total + CLIP_EPS))
    for kind in range(2):
        clipped = gradient_ref[0, kind] * clip_scale
        moment1 = BETA_ONE * moment1_ref[0, kind] + (1.0 - BETA_ONE) * clipped
        moment2 = BETA_TWO * moment2_ref[0, kind] + (1.0 - BETA_TWO) * clipped * clipped
        root = jnp.sqrt(moment2 / (1.0 - BETA_TWO**ADAM_STEP)) + ADAM_EPS
        update = moment1 / (1.0 - BETA_ONE**ADAM_STEP) / root
        new_moment1_ref[0, kind] = moment1
        new_moment2_ref[0, kind] = moment2
        new_weights_ref[0, kind] = weights_ref[0, kind] - LEARN_RATE * (update + DECAY_RATE * weights_ref[0, kind])


def local(section_inputs, carry_in, loss_mask, weights, moment1, moment2):
    where = jnp.stack(
        [lax.axis_index("z"), lax.axis_index("core"), lax.axis_index(PIPE), lax.axis_index("xl")]
    ).astype(jnp.int32)
    multipliers = jnp.array(SCALES, F32).reshape(2, 1, 1)
    own = (weights[0] * multipliers).astype(BF)
    mask = loss_mask.astype(F32)[..., None]
    shard = (2, ROWS, LATENT)
    chunk = sds((2, *shard), BF)
    unit = 2 * TOK * D * LATENT
    small = 1 << 20

    def place(ks, chunks, *held):
        ins = [where]
        for c in chunks:
            ins += [c, swap(c, "core")]
        ins += held
        aliases = {len(ins) - 1: 0} if held else None
        kernel = lambda *refs: place_kernel(ks, *refs)
        return call(kernel, [sds((2, 2, D, LATENT), BF)], ins, 10 * unit, aliases)[0]

    def gather(start):
        w = place((0,), [start])
        ahead = back = start
        for k in range(1, 4):
            ahead = shift(ahead, "z", 1, NZ)
            back = shift(back, "z", -1, NZ)
            held = [section_inputs, carry_in] if k > 1 else []
            w = place((k, NZ - k), [back, ahead], *held, w)
        return w, shift(ahead[0], "z", 1, NZ), shift(back[1], "z", -1, NZ)

    def hop(u, out):
        if u == 0:
            return lax.ppermute(out, PIPE, [(i, i - 1) for i in range(1, NP)])
        return lax.ppermute(out, PIPE, [(i, i + 1) for i in range(NP - 1)])

    def step1(u, state, arrived, *after):
        latent, factor, normed, cot0, d_lat0, _ = state
        terms = sds((NZ, *chunk.shape), BF)
        cot1, d_lat1, mine, other = call(
            lambda *refs: step1_kernel(u, *refs),
            [sds((TOK, D), BF), sds((TOK, LATENT), BF), terms, terms],
            [where, mask, section_inputs, w, latent, factor, normed, cot0, d_lat0, arrived, *after],
            6 * unit,
        )
        return (d_lat1, cot1), mine, swap(other, "core")

    def scatter(mine, theirs, keep_type, *after):
        both = [where, mine, theirs]

        ahead, back = call(far_kernel, [sds(shard, BF), sds(shard, BF)], both, small)
        for k in (3, 2, 1):
            ins = [*both, shift(ahead, "z", 1, NZ), shift(back, "z", -1, NZ)]
            ahead, back = call(functools.partial(join_kernel, k), [chunk, chunk], ins, small)
        ahead = shift(ahead, "z", 1, NZ)
        back = shift(back, "z", -1, NZ)
        parts = [*both, ahead, back, *after]
        keep, give = call(last_kernel, [sds(shard, keep_type), sds(shard, BF)], parts, small)
        return keep, give

    shards = [where, own, mirror(own), swap(own, "xl"), mirror_cross(own)]
    w, low, high = gather(call(quad_kernel, [sds((2, 2, *shard), BF)], shards, small)[0])
    state = [
        sds((STEPS * TOK, LATENT), F32), sds((STEPS * TOK, 128), F32), sds((STEPS * TOK, LATENT), BF),
        sds((TOK, D), BF), sds((TOK, LATENT), BF), sds((TOK, D), BF),
    ]
    last = [low, swap(low, "core"), high, swap(high, "core")]

    def step0(u, w):
        ins = [where, mask, section_inputs, carry_in, *last, w]
        kernel = lambda *refs: step0_kernel(u, *refs)
        *out, w = call(kernel, state + [sds(w.shape, BF)], ins, 5 * unit, {len(ins) - 1: len(state)})
        return out, w

    state_b, w = step0(1, w)
    state_a, w = step0(0, w)
    arrived_b = hop(1, state_b[-1])
    arrived_a = hop(0, state_a[-1])
    end_b, mine_b, theirs_b = step1(1, state_b, arrived_b)
    end_a, mine_a, theirs_a = step1(0, state_a, arrived_a, end_b[0])
    keep_b, give_b = scatter(mine_b, theirs_b, BF)
    mirrored = mirror(keep_b)
    crossed = mirror_cross(give_b)
    keep_a, give_a = scatter(mine_a, theirs_a, F32, keep_b)
    near = swap(give_a, "xl")
    outs = [sds((1, 2, TOK, D), BF), sds((8, 128), F32)]
    carry_out, done = call(carry_kernel, outs, [where, w, *end_a, *end_b], 2 * unit)
    outs = [sds((1, *shard), F32), sds((1, 128), F32)]
    gradient, squares = call(gradient_kernel, outs, [where, keep_a, near, mirrored, crossed, done], small)
    squares = jnp.broadcast_to(squares, (NP * NZ * 4, 1, 128))
    squares = lax.all_to_all(squares, PIPE + DP, 0, 0, tiled=True)
    owned = sds(weights.shape, F32)
    ins = [where, squares, gradient, weights, moment1, moment2]
    return (carry_out, *call(update_kernel, [owned, owned, owned], ins, small))


def solution(mesh):
    fine = Mesh(mesh.devices.reshape(2, 4, 8, 2, 2), PIPE + DP)
    rows = P(PIPE, None, DP, None)
    return jax.shard_map(
        local,
        mesh=fine,
        in_specs=(P(PIPE, None, None, DP, None), rows, P(None, None, DP), rows, rows, rows),
        out_specs=(rows, rows, rows, rows),
        check_vma=False,
    )
```
